32 devices in a mesh: fsdp: 8 (over z, x), tp: 4 (over y, core).
Axes of the slice: x: 2, y: 2, z: 4, core: 2. Of those that a mesh axis runs over, the one named last changes fastest.
Arguments:
- layer_input: bfloat16 [8192, 2048], P(('fsdp', 'tp')), may hold values from -6 to 6
- out_cotangent: bfloat16 [8192, 2048], P(('fsdp', 'tp')), may hold values from -6 to 6
- segments: int32 [8, 1024], P('fsdp'), may hold values from 0 to 2, as said below
- qkv_weight: float32 [1, 3, 2048, 2048], P(None, None, 'fsdp', 'tp'), may hold values from -0.125 to 0.125
- qkv_first: float32 [1, 3, 2048, 2048], P(None, None, 'fsdp', 'tp'), may hold values from -16 to 16
- qkv_second: float32 [1, 3, 2048, 2048], P(None, None, 'fsdp', 'tp'), may hold values from 19.6608 to 311.296
- out_weight: float32 [1, 2048, 2048], P(None, ('tp', 'fsdp')), may hold values from -0.5 to 0.5
- out_first: float32 [1, 2048, 2048], P(None, ('tp', 'fsdp')), may hold values from -6 to 6
- out_second: float32 [1, 2048, 2048], P(None, ('tp', 'fsdp')), may hold values from 2.12992 to 34.4064
- up_weight: float32 [1, 2048, 8192], P(None, 'fsdp', 'tp'), may hold values from -0.125 to 0.125
- up_first: float32 [1, 2048, 8192], P(None, 'fsdp', 'tp'), may hold values from -16 to 16
- up_second: float32 [1, 2048, 8192], P(None, 'fsdp', 'tp'), may hold values from 19.6608 to 311.296
- down_weight: float32 [1, 8192, 2048], P(None, ('tp', 'fsdp')), may hold values from -0.0625 to 0.0625
- down_first: float32 [1, 8192, 2048], P(None, ('tp', 'fsdp')), may hold values from -32 to 32
- down_second: float32 [1, 8192, 2048], P(None, ('tp', 'fsdp')), may hold values from 77.824 to 1228.8
- small_params: float32 [1, 26624], replicated
- small_first: float32 [1, 26624], replicated, may hold values from -32 to 32
- small_second: float32 [1, 26624], replicated, may hold values from 54.0672 to 860.16
Outputs:
- layer_output: float32 [8192, 2048], P(('fsdp', 'tp'))
- input_grad: float32 [8192, 2048], P(('fsdp', 'tp'))
- qkv_first_new: float32 [1, 3, 2048, 2048], P(None, None, 'fsdp', 'tp')
- qkv_second_new: float32 [1, 3, 2048, 2048], P(None, None, 'fsdp', 'tp')
- qkv_new: float32 [1, 3, 2048, 2048], P(None, None, 'fsdp', 'tp')
- out_first_new: float32 [1, 2048, 2048], P(None, ('tp', 'fsdp'))
- out_second_new: float32 [1, 2048, 2048], P(None, ('tp', 'fsdp'))
- out_new: float32 [1, 2048, 2048], P(None, ('tp', 'fsdp'))
- up_first_new: float32 [1, 2048, 8192], P(None, 'fsdp', 'tp')
- up_second_new: float32 [1, 2048, 8192], P(None, 'fsdp', 'tp')
- up_new: float32 [1, 2048, 8192], P(None, 'fsdp', 'tp')
- down_first_new: float32 [1, 8192, 2048], P(None, ('tp', 'fsdp'))
- down_second_new: float32 [1, 8192, 2048], P(None, ('tp', 'fsdp'))
- down_new: float32 [1, 8192, 2048], P(None, ('tp', 'fsdp'))
- small_first_new: float32 [1, 26624], replicated
- small_second_new: float32 [1, 26624], replicated
- small_new: float32 [1, 26624], replicated
The draws below stay inside these ranges and needn't reach their ends.
Inputs may be any that keep to these rules, and one draw needn't show every extreme that they name: `segments`: each sequence holds two or three documents numbered from 0 in order, none empty. One of them, the middle one, begins within the first 256 positions and ends within the last 256 positions. Before it there may be one document that starts the sequence; after it there is always one document that ends the sequence, of fewer than 256 tokens.
All inputs are finite; a program needn't handle non-finite values.
Results may differ from the reference program's by a relative error of at most 0.019.
Values may be sent and summed in bfloat16 or wider, within the bound.
A program may use at most 192 MiB of HBM per device.

```python
import math
import jax
import jax.numpy as jnp
from jax import lax

D = 2048
HEADS = 8
HD = 256
ROT = 64
FF = 8192
LAYERS = 1
STEP = 10
TOK_DEV = 256
LENGTH = 1024
SEQS = 8
TOKENS = 8192
SMALL = 26624


def draw_segments(key, part):
    key = jax.random.fold_in(key, 11)
    begin_key, tail_key = jax.random.split(key)
    begin = jax.random.randint(begin_key, (SEQS, 1), 0, TOK_DEV)
    tail = jax.random.randint(tail_key, (SEQS, 1), 1, TOK_DEV)
    finish = LENGTH - tail
    indices = jnp.arange(LENGTH, dtype=jnp.int32)[None, :]
    leading = ((indices >= begin) & (begin > 0)).astype(jnp.int32)
    return leading + (indices >= finish).astype(jnp.int32)


def draw_small_params(key, part):
    key = jax.random.fold_in(key, 5)
    gain_key, shift_key = jax.random.split(key)
    gains = jax.random.uniform(gain_key, (LAYERS, SMALL), jnp.float32, 0.6, 1.4)
    shifts = 0.2 * jax.random.normal(shift_key, (LAYERS, SMALL), jnp.float32)
    column = jnp.arange(SMALL, dtype=jnp.int32)[None, :]
    is_gain = (column < D) | (column >= 2 * D) & (column < 3 * D)
    return jnp.where(is_gain, gains, shifts)


def level_of(own_key, dims, cuts, low, largest):
    factor_of = 1.0
    for dim, blocks in cuts:
        draws = jax.random.uniform(jax.random.fold_in(jax.random.fold_in(own_key, 6), dim), (blocks,), jnp.float32, low / len(cuts), largest / len(cuts))
        factor_of = factor_of * jnp.repeat(jnp.exp(draws), dims[dim] // blocks).reshape((-1,) + (1,) * (len(dims) - 1 - dim))
    return factor_of


def bell_draw(key, dims, width, most, pieces=(), held_as=jnp.bfloat16):
    level = level_of(key, dims, pieces, -0.22, 0.18) if pieces else 1.0
    values = jax.random.normal(key, dims, jnp.float32) * width * level
    return jnp.minimum(jnp.maximum(values, -most), most).astype(held_as)


def setup_inputs(seed: int = 0) -> dict:
    key_of = jax.random.split(jax.random.key(seed), 19)
    layer_input = bell_draw(key_of[0], (TOKENS, D), 1.0, 6.0, ((0, 32),))
    out_cotangent = bell_draw(key_of[1], (TOKENS, D), 1.0, 6.0, ((0, 32),))
    segments = draw_segments(jax.random.fold_in(key_of[18], 71), 0)
    qkv_weight = bell_draw(key_of[3], (LAYERS, 3, D, D), D ** -0.5, 0.125, ((2, 8), (3, 4)), jnp.float32)
    qkv_first = bell_draw(key_of[4], (LAYERS, 3, D, D), (0.033 * TOKENS ** 0.5), 16.0, ((2, 8), (3, 4)), jnp.float32)
    qkv_second = jnp.clip(jnp.exp(math.log(311.296) - 2.7621173 * jax.random.uniform(key_of[5], (LAYERS, 3, D, D), jnp.float32) ** level_of(key_of[5], (LAYERS, 3, D, D), ((2, 8), (3, 4)), -0.2, 0.2)), 19.6608, 311.296)
    out_weight = bell_draw(key_of[6], (LAYERS, D, D), (D // 16) ** -0.5, 0.5, ((1, 32),), jnp.float32)
    out_first = bell_draw(key_of[7], (LAYERS, D, D), (0.011 * TOKENS ** 0.5), 6.0, ((1, 32),), jnp.float32)
    out_second = jnp.clip(jnp.exp(math.log(34.4064) - 2.7821581 * jax.random.uniform(key_of[8], (LAYERS, D, D), jnp.float32) ** level_of(key_of[8], (LAYERS, D, D), ((1, 32),), -0.2, 0.2)), 2.12992, 34.4064)
    up_weight = bell_draw(key_of[9], (LAYERS, D, FF), D ** -0.5, 0.125, ((1, 8), (2, 4)), jnp.float32)
    up_first = bell_draw(key_of[10], (LAYERS, D, FF), (0.033 * TOKENS ** 0.5), 16.0, ((1, 8), (2, 4)), jnp.float32)
    up_second = jnp.clip(jnp.exp(math.log(311.296) - 2.7621173 * jax.random.uniform(key_of[11], (LAYERS, D, FF), jnp.float32) ** level_of(key_of[11], (LAYERS, D, FF), ((1, 8), (2, 4)), -0.2, 0.2)), 19.6608, 311.296)
    down_weight = bell_draw(key_of[12], (LAYERS, FF, D), FF ** -0.5, 0.0625, ((1, 32),), jnp.float32)
    down_first = bell_draw(key_of[13], (LAYERS, FF, D), (0.067 * TOKENS ** 0.5), 32.0, ((1, 32),), jnp.float32)
    down_second = jnp.clip(jnp.exp(math.log(1228.8) - 2.7593436 * jax.random.uniform(key_of[14], (LAYERS, FF, D), jnp.float32) ** level_of(key_of[14], (LAYERS, FF, D), ((1, 32),), -0.2, 0.2)), 77.824, 1228.8)
    small_params = draw_small_params(jax.random.fold_in(key_of[18], 71), 0)
    small_first = bell_draw(key_of[16], (LAYERS, SMALL), (0.055 * TOKENS ** 0.5), 32.0, (), jnp.float32)
    small_second = jnp.clip(jnp.exp(jax.random.uniform(key_of[17], (LAYERS, SMALL), jnp.float32, math.log(54.0672), math.log(860.16))), 54.0672, 860.16)
    return {"layer_input": layer_input, "out_cotangent": out_cotangent, "segments": segments, "qkv_weight": qkv_weight, "qkv_first": qkv_first, "qkv_second": qkv_second, "out_weight": out_weight, "out_first": out_first, "out_second": out_second, "up_weight": up_weight, "up_first": up_first, "up_second": up_second, "down_weight": down_weight, "down_first": down_first, "down_second": down_second, "small_params": small_params, "small_first": small_first, "small_second": small_second}


norm_eps = 1e-05
beta_one = 0.9
beta_two = 0.95
adam_eps = 1e-08
decay_rate = 0.01
rate_vector = 0.2
masked_score = -1e+30
highest = lax.Precision.HIGHEST

@jax.custom_vjp
def low(v):
    return lax.optimization_barrier(v.astype(jnp.bfloat16)).astype(jnp.float32)

@jax.custom_vjp
def low_back(v):
    return v

def low_keep(v):
    return (low(v), None)

def low_pass(kept, grad):
    return (grad,)

def back_keep(v):
    return (v, None)

def back_low(kept, grad):
    return (low(grad),)
low.defvjp(low_keep, low_pass)
low_back.defvjp(back_keep, back_low)

def norm_rows(stream, gain, shift):
    mean_row = lax.optimization_barrier(jnp.mean(stream, axis=-1, keepdims=True))
    centred = stream - mean_row
    spread = lax.optimization_barrier(jnp.mean(centred * centred, axis=-1, keepdims=True))
    return centred * lax.rsqrt(spread + norm_eps) * gain + shift

def rotary_tables(seg_ids):
    length = seg_ids.shape[0]
    indices = jnp.arange(length, dtype=jnp.int32)
    earlier = lax.optimization_barrier(jnp.sum((seg_ids[None, :] < seg_ids[:, None]).astype(jnp.int32), axis=1))
    position = (indices - earlier).astype(jnp.float32)
    inverse_freq = 10000.0 ** (-jnp.arange(0, ROT, 2).astype(jnp.float32) / ROT)
    angle = position[:, None] * inverse_freq[None, :]
    return (jnp.cos(angle), jnp.sin(angle))

def rotate(values, cosine, sine):
    half_dims = cosine.shape[-1]
    first_half = values[..., :half_dims]
    second_half = values[..., half_dims:2 * half_dims]
    remainder = values[..., 2 * half_dims:]
    cosine = cosine[:, None, :]
    sine = sine[:, None, :]
    return jnp.concatenate([first_half * cosine - second_half * sine, second_half * cosine + first_half * sine, remainder], axis=-1)

def run_sequence(stream, seg_ids, qkv_low, out_low, up_low, down_low, small):
    length = stream.shape[0]
    cosine, sine = rotary_tables(seg_ids)
    indices = jnp.arange(length, dtype=jnp.int32)
    allowed = (indices[None, :] <= indices[:, None]) & (seg_ids[None, :] == seg_ids[:, None])
    for layer_idx in range(LAYERS):
        vector = small[layer_idx]
        gain_one = vector[0:D]
        shift_one = vector[D:2 * D]
        gain_two = vector[2 * D:3 * D]
        shift_two = vector[3 * D:4 * D]
        bias_out = vector[4 * D:5 * D]
        bias_down = vector[5 * D:6 * D]
        qkv_bias = vector[6 * D:9 * D].reshape(3, D)
        up_bias = vector[9 * D:9 * D + FF]
        normed_one = low(norm_rows(stream, gain_one, shift_one))
        normed_two = low(norm_rows(stream, gain_two, shift_two))
        projected = jnp.einsum('sd,cde->cse', normed_one, qkv_low[layer_idx], precision=highest) + qkv_bias[:, None, :]
        projected = low_back(projected)
        query_rows = low(rotate(projected[0].reshape(length, HEADS, HD), cosine, sine))
        key_rows = low(rotate(projected[1].reshape(length, HEADS, HD), cosine, sine))
        value_rows = low(projected[2].reshape(length, HEADS, HD))
        scores = low_back(jnp.einsum('qhd,khd->hqk', query_rows, key_rows, precision=highest) * HD ** (-0.5))
        scores = jnp.where(allowed[None], scores, masked_score)
        totals = jax.nn.logsumexp(scores, axis=-1, keepdims=True)
        probs = jnp.exp(scores - totals)
        attended = jnp.einsum('hqk,khd->qhd', low(probs), value_rows, precision=highest)
        mixed_rows = low(low_back(attended)).reshape(length, D)
        pre_act = low_back(jnp.dot(normed_two, up_low[layer_idx], precision=highest) + up_bias)
        active = low(jax.nn.gelu(pre_act, approximate=False))
        branch = low_back(jnp.dot(mixed_rows, out_low[layer_idx], precision=highest) + jnp.dot(active, down_low[layer_idx], precision=highest))
        stream = stream + branch + bias_out + bias_down
    return stream

def adam_step(weight, first, second, grad, rate, decay):
    first_new = beta_one * first + (1.0 - beta_one) * grad
    second_new = beta_two * second + (1.0 - beta_two) * grad * grad
    first_hat = first_new / (1.0 - beta_one ** STEP)
    second_hat = second_new / (1.0 - beta_two ** STEP)
    weight_new = weight - rate * (first_hat / (jnp.sqrt(second_hat) + adam_eps) + decay * weight)
    return (first_new, second_new, weight_new)

def reference(layer_input, out_cotangent, segments, qkv_weight, qkv_first, qkv_second, out_weight, out_first, out_second, up_weight, up_first, up_second, down_weight, down_first, down_second, small_params, small_first, small_second):
    rate_matrix = D ** (-0.5)
    rate_output = 4.0 * D ** (-0.5)

    def forward(stream_all, qkv_full, out_full, up_full, down_full, small):
        qkv_low = low(qkv_full)
        out_low = low(out_full)
        up_low = low(up_full)
        down_low = low(down_full)
        sequences = stream_all.reshape(SEQS, LENGTH, D)

        def one_sequence(carry, item):
            stream, seg_ids = item
            return (carry, run_sequence(stream, seg_ids, qkv_low, out_low, up_low, down_low, small))
        _, results = lax.scan(jax.checkpoint(one_sequence), None, (sequences, segments))
        return results.reshape(TOKENS, D)
    layer_output, pullback = jax.vjp(forward, layer_input.astype(jnp.float32), qkv_weight, out_weight, up_weight, down_weight, small_params)
    input_grad, qkv_grad, out_grad, up_grad, down_grad, small_grad = pullback(out_cotangent.astype(jnp.float32))
    qkv_m, qkv_v, qkv_w = adam_step(qkv_weight, qkv_first, qkv_second, qkv_grad, rate_matrix, decay_rate)
    out_m, out_v, out_w = adam_step(out_weight, out_first, out_second, out_grad, rate_output, decay_rate)
    up_m, up_v, up_w = adam_step(up_weight, up_first, up_second, up_grad, rate_matrix, decay_rate)
    down_m, down_v, down_w = adam_step(down_weight, down_first, down_second, down_grad, rate_matrix, decay_rate)
    small_m, small_v, small_w = adam_step(small_params, small_first, small_second, small_grad, rate_vector, 0.0)
    return (layer_output, input_grad, qkv_m, qkv_v, qkv_w, out_m, out_v, out_w, up_m, up_v, up_w, down_m, down_v, down_w, small_m, small_v, small_w)
```

```python
import jax
import jax.numpy as jnp
from jax import lax
from jax.sharding import PartitionSpec as P

HD = 256
ROT = 64
STEP = 10

norm_eps = 1e-05
beta_one = 0.9
beta_two = 0.95
adam_eps = 1e-08
decay_rate = 0.01
rate_vector = 0.2
masked_score = -1e30
f32 = jnp.float32
bf16 = jnp.bfloat16


def rotary_tables(seg_ids):
    length = seg_ids.shape[0]
    indices = jnp.arange(length, dtype=jnp.int32)
    earlier = jnp.sum((seg_ids[None, :] < seg_ids[:, None]).astype(jnp.int32), axis=1)
    position = (indices - earlier).astype(f32)
    inverse_freq = 10000.0 ** (-jnp.arange(0, ROT, 2).astype(f32) / ROT)
    angle = position[:, None] * inverse_freq[None, :]
    return (jnp.cos(angle), jnp.sin(angle))


def rotate(values, cosine, sine):
    half_dims = cosine.shape[-1]
    first_half = values[..., :half_dims]
    second_half = values[..., half_dims : 2 * half_dims]
    remainder = values[..., 2 * half_dims :]
    return jnp.concatenate(
        [
            first_half * cosine - second_half * sine,
            second_half * cosine + first_half * sine,
            remainder,
        ],
        axis=-1,
    )


def adam_step(weight, first, second, grad, rate, decay):
    first_new = beta_one * first + (1.0 - beta_one) * grad
    second_new = beta_two * second + (1.0 - beta_two) * grad * grad
    first_hat = first_new / (1.0 - beta_one**STEP)
    second_hat = second_new / (1.0 - beta_two**STEP)
    weight_new = weight - rate * (first_hat / (jnp.sqrt(second_hat) + adam_eps) + decay * weight)
    return (first_new, second_new, weight_new)


def dot(a, b, dims, out=f32):
    return lax.dot_general(a, b, (dims, ((), ())), preferred_element_type=out)


def make_local(fsdp, tp):
    lo_n = 2
    mid_n = 2
    hi_n = fsdp // (lo_n * mid_n)
    hi_bits = [1 << b for b in range(2, fsdp.bit_length() - 1)]
    top = hi_bits[-1]

    def swap_top(i):
        a, b = (i & 2) // 2, (i & top) // top
        return (i & ~(2 | top)) | (2 * b) | (top * a)

    def px(v, mask):
        return lax.ppermute(v, "fsdp", [(i, i ^ mask) for i in range(fsdp)])

    def pt(v, mask):
        return lax.ppermute(v, "tp", [(i, i ^ mask) for i in range(tp)])

    def local(
        layer_input,
        out_cotangent,
        segments,
        qkv_weight,
        qkv_first,
        qkv_second,
        out_weight,
        out_first,
        out_second,
        up_weight,
        up_first,
        up_second,
        down_weight,
        down_first,
        down_second,
        small_params,
        small_first,
        small_second,
    ):
        f = lax.axis_index("fsdp")
        t = lax.axis_index("tp")
        mid = (f // 2) % 2
        hi = f // 4
        lo = f % 2
        core = t % 2
        half_t = t // 2
        rows, d = layer_input.shape
        length = segments.shape[1]
        width = qkv_weight.shape[3]
        hidden = up_weight.shape[2]
        hidden_all = small_params.shape[1] - 9 * d
        sub = hidden // fsdp
        feat = d // fsdp
        mine = hidden // 2
        orow = width // fsdp
        vector = small_params[0]

        up16 = up_weight[0].astype(bf16).reshape(feat, hi_n, 2, lo_n * sub)
        down16 = down_weight[0].astype(bf16)
        qkv16 = qkv_weight[0].astype(bf16).reshape(3, feat, 2, HD)
        out16 = out_weight[0].astype(bf16)

        def pick(v, index, axis):
            return lax.dynamic_index_in_dim(v, index, axis, keepdims=False)

        def gather_tokens(own):
            mid_block = px(own, 2)
            y_own = pt(own, 2)
            y_mid = pt(mid_block, 2)
            blocks = {(0, 0): own, (2, 0): mid_block, (0, 2): y_own, (2, 2): y_mid}
            for key in list(blocks):
                blocks[(key[0], 1 ^ key[1])] = pt(blocks[key], 1)
            whole = jnp.zeros((2, tp, rows, d), own.dtype)
            for (a, b), block in blocks.items():
                whole = lax.dynamic_update_slice(
                    whole, block[None, None], ((mid ^ (a // 2)), t ^ b, 0, 0)
                )
            return whole.reshape(2 * tp * rows, d)

        def scatter_tokens(part):
            part = part.reshape(2, tp // 2, 2, rows, d)
            keep = pick(part, core, 2)
            give = pick(part, 1 - core, 2)
            part = (keep.astype(f32) + pt(give, 1).astype(f32)).astype(bf16)
            keep = pick(part, half_t, 1)
            give = pick(part, 1 - half_t, 1)
            part = (keep.astype(f32) + pt(give, 2).astype(f32)).astype(bf16)
            keep = pick(part, mid, 0)
            give = pick(part, 1 - mid, 0)
            return keep.astype(f32) + px(give, 2).astype(f32)

        def gather_group(block):
            blocks = {0: block}
            for mask in hi_bits + [1]:
                for key in list(blocks):
                    blocks[key | mask] = px(blocks[key], mask)
            return blocks

        def scatter_group(part):
            keep = pick(part, lo, 1)
            give = pick(part, 1 - lo, 1)
            got = px(give, 1)
            index = hi
            total = keep.astype(f32) + got.astype(f32)
            for mask in reversed(hi_bits):
                total = total.astype(bf16)
                bit = mask // 4
                n = total.shape[0] // 2
                upper = (index & bit) // bit
                shaped = total.reshape((2, n) + total.shape[1:])
                keep = pick(shaped, upper, 0)
                give = pick(shaped, 1 - upper, 0)
                total = keep.astype(f32) + px(give, mask).astype(f32)
            return total[0]

        def halves(v, axis):
            return pick(v, mid, axis), pick(v, 1 - mid, axis)

        own, other = halves(up16, 2)
        from_mid = px(other, 2)
        up_whole = jnp.zeros((hi_n, 2, lo_n, feat, hi_n, lo_n * sub), bf16)
        for a, block in ((0, own), (2, from_mid)):
            for mask, piece in gather_group(block).items():
                g = f ^ a ^ mask
                up_whole = lax.dynamic_update_slice(
                    up_whole, piece[None, None, None], (g // 4, (g // 2) % 2, g % 2, 0, 0, 0)
                )
        up_full = up_whole.reshape(d, mine)
        x_all = gather_tokens(layer_input)
        own, other = halves(qkv16, 2)
        from_mid = px(other, 2)
        qkv_whole = jnp.zeros((3, hi_n, 2, lo_n, feat, HD), bf16)
        for a, block in ((0, own), (2, from_mid)):
            for mask, piece in gather_group(block).items():
                g = f ^ a ^ mask
                qkv_whole = lax.dynamic_update_slice(
                    qkv_whole,
                    piece[:, None, None, None],
                    (0, g // 4, (g // 2) % 2, g % 2, 0, 0),
                )
        qkv_full = qkv_whole.reshape(3, d, HD)
        e_all = gather_tokens(out_cotangent)
        down_whole = jnp.zeros((hi_n, lo_n, sub, d), bf16)
        for mask, piece in gather_group(down16).items():
            g = f ^ mask
            down_whole = lax.dynamic_update_slice(down_whole, piece[None, None], (g // 4, g % 2, 0, 0))
        down_full = down_whole.reshape(mine, d)

        swap_perm = [(i, swap_top(i)) for i in range(fsdp)]
        out_block = lax.ppermute(out16, "fsdp", swap_perm)
        out_whole = jnp.zeros((hi_n, lo_n, orow, d), bf16)
        n_top = top // 4
        hi_rest = hi % n_top if n_top > 1 else 0
        for mask, piece in gather_group(out_block).items():
            g = f ^ mask
            g_top = g // top
            g_rest = (g // 4) % n_top if n_top > 1 else 0
            place = g_rest * 2 + g_top
            out_whole = lax.dynamic_update_slice(out_whole, piece[None, None], (place, g % 2, 0, 0))
        out_full = out_whole.reshape(HD, d)

        seg_other = px(segments.astype(f32), 2).astype(jnp.int32)
        seg = jnp.where(mid == 0, jnp.concatenate([segments, seg_other]), jnp.concatenate([seg_other, segments]))
        cosine, sine = jax.vmap(rotary_tables)(seg)
        idx = jnp.arange(length, dtype=jnp.int32)
        allowed = (idx[None, :] <= idx[:, None])[None] & (seg[:, :, None] == seg[:, None, :])

        stream = layer_input.astype(f32)
        x32 = x_all.astype(f32)
        mean_row = jnp.mean(x32, axis=-1, keepdims=True)
        centred = x32 - mean_row
        inverse = lax.rsqrt(jnp.mean(centred * centred, axis=-1, keepdims=True) + norm_eps)
        normal = centred * inverse
        gain_one, shift_one = vector[0:d], vector[d : 2 * d]
        gain_two, shift_two = vector[2 * d : 3 * d], vector[3 * d : 4 * d]
        bias_out, bias_down = vector[4 * d : 5 * d], vector[5 * d : 6 * d]
        qkv_bias = lax.dynamic_slice_in_dim(
            vector[6 * d : 9 * d].reshape(3, d), t * width + mid * HD, HD, 1
        )
        up_bias = pick(
            pick(vector[9 * d :].reshape(tp, hi_n, 2, lo_n * sub), t, 0), mid, 1
        ).reshape(mine)
        rows_one = (normal * gain_one + shift_one).astype(bf16)
        rows_two = (normal * gain_two + shift_two).astype(bf16)

        pre_act = dot(rows_two, up_full, ((1,), (0,))) + up_bias
        cdf = 0.5 * (1.0 + lax.erf(pre_act * 0.7071067811865476))
        active = (pre_act * cdf).astype(bf16)
        slope = (cdf + pre_act * (jnp.exp(-0.5 * pre_act * pre_act) * 0.3989422804014327)).astype(bf16)
        down_grad = dot(active, e_all, ((0,), (0,)), bf16)
        down_sum = scatter_group(down_grad.reshape(hi_n, lo_n, sub, d))
        active_grad = dot(e_all, down_full, ((1,), (1,)))
        pre_grad = (active_grad * slope.astype(f32)).astype(bf16)
        up_grad = dot(rows_two, pre_grad, ((0,), (0,)), bf16)
        up_bias_grad = jnp.sum(pre_grad, axis=0, dtype=f32)

        def scatter_cols(grad, tail):
            pass

        up_sum = scatter_group(
            up_grad.reshape(hi_n, 2, lo_n, feat, mine).transpose(0, 2, 1, 3, 4)
        ).astype(bf16)
        keep, give = halves(up_sum, 0)
        got = px(give, 2)
        up_total = jnp.where(
            mid == 0,
            jnp.stack([keep.reshape(feat, hi_n, lo_n * sub), got.reshape(feat, hi_n, lo_n * sub)], 2),
            jnp.stack([got.reshape(feat, hi_n, lo_n * sub), keep.reshape(feat, hi_n, lo_n * sub)], 2),
        ).reshape(1, feat, hidden)

        proj = dot(rows_one, qkv_full, ((1,), (1,))) + qkv_bias[None]
        proj = proj.reshape(2, length, 3, HD)
        query = rotate(proj[:, :, 0], cosine, sine).astype(bf16)
        key = rotate(proj[:, :, 1], cosine, sine).astype(bf16)
        value = proj[:, :, 2].astype(bf16)
        scale = HD ** (-0.5)
        scores = jnp.einsum("bqd,bkd->bqk", query, key, preferred_element_type=f32) * scale
        scores = jnp.where(allowed, scores, masked_score)
        peak = jnp.max(scores, axis=-1, keepdims=True)
        total = jnp.log(jnp.sum(jnp.exp(scores - peak), axis=-1, keepdims=True)) + peak
        probs = jnp.exp(scores - total)
        weights = probs.astype(bf16)
        mixed = jnp.einsum("bqk,bkd->bqd", weights, value, preferred_element_type=f32)
        mixed = mixed.astype(bf16).reshape(2 * length, HD)
        out_grad = dot(mixed, e_all, ((0,), (0,)), bf16)
        out_sum = scatter_group(
            jnp.moveaxis(
                out_grad.reshape(hi_n // 2, 2, lo_n, orow, d), 1, 0
            ).reshape(hi_n, lo_n, orow, d)
        ).astype(bf16)
        out_total = lax.ppermute(out_sum, "fsdp", swap_perm)[None].astype(f32)
        mixed_grad = dot(e_all, out_full, ((1,), (1,)), bf16).reshape(2, length, HD)
        prob_grad = jnp.einsum("bqd,bkd->bqk", mixed_grad, value, preferred_element_type=f32)
        inner = jnp.sum(probs * prob_grad, axis=-1, keepdims=True)
        score_grad = (probs * (prob_grad - inner)).astype(bf16)
        query_grad = jnp.einsum("bqk,bkd->bqd", score_grad, key, preferred_element_type=f32) * scale
        key_grad = jnp.einsum("bqk,bqd->bkd", score_grad, query, preferred_element_type=f32) * scale
        value_grad = jnp.einsum("bqk,bqd->bkd", weights, mixed_grad, preferred_element_type=f32)
        proj_grad = jnp.stack(
            [rotate(query_grad, cosine, -sine), rotate(key_grad, cosine, -sine), value_grad], 0
        ).astype(bf16).reshape(3, 2 * length, HD)
        qkv_grad = dot(rows_one, proj_grad, ((0,), (1,)), bf16)
        qkv_bias_grad = jnp.sum(proj_grad, axis=1, dtype=f32)
        qkv_sum = scatter_group(
            qkv_grad.reshape(hi_n, 2, lo_n, feat, 3, HD).transpose(0, 2, 1, 4, 3, 5)
        ).astype(bf16)
        keep, give = halves(qkv_sum, 0)
        got = px(give, 2)
        qkv_total = jnp.where(
            mid == 0, jnp.concatenate([keep, got], -1), jnp.concatenate([got, keep], -1)
        )[None].astype(f32)

        branch = dot(mixed, out_full, ((1,), (0,))) + dot(active, down_full, ((1,), (0,)))
        layer_output = stream + scatter_tokens(branch.astype(bf16)) + bias_out + bias_down

        first_norm = lax.dot_general(
            proj_grad, qkv_full, (((0, 2), (0, 2)), ((), ())), preferred_element_type=f32
        )
        second_norm = dot(pre_grad, up_full, ((1,), (1,)))
        gain_one_grad = jnp.sum(first_norm * normal, axis=0)
        shift_one_grad = jnp.sum(first_norm, axis=0)
        gain_two_grad = jnp.sum(second_norm * normal, axis=0)
        shift_two_grad = jnp.sum(second_norm, axis=0)
        scaled = scatter_tokens((first_norm * gain_one + second_norm * gain_two).astype(bf16))
        own_mean = jnp.mean(stream, axis=-1, keepdims=True)
        own_centred = stream - own_mean
        own_inverse = lax.rsqrt(jnp.mean(own_centred * own_centred, axis=-1, keepdims=True) + norm_eps)
        own_normal = own_centred * own_inverse
        gradient = out_cotangent.astype(f32)
        input_grad = gradient + own_inverse * (
            scaled
            - jnp.mean(scaled, axis=-1, keepdims=True)
            - own_normal * jnp.mean(scaled * own_normal, axis=-1, keepdims=True)
        )

        bias_grad = jnp.sum(gradient, axis=0)
        qkv_spread = lax.dynamic_update_slice(
            jnp.zeros((3, d), f32), qkv_bias_grad, (0, t * width + mid * HD)
        )
        up_spread = lax.dynamic_update_slice(
            jnp.zeros((tp, hi_n, 2, lo_n * sub), f32),
            up_bias_grad.reshape(1, hi_n, 1, lo_n * sub),
            (t, 0, mid, 0),
        )
        small_grad = jnp.concatenate(
            [
                gain_one_grad,
                shift_one_grad,
                gain_two_grad,
                shift_two_grad,
                bias_grad,
                bias_grad,
                qkv_spread.reshape(-1),
                up_spread.reshape(-1),
            ]
        )
        small_total = lax.psum(small_grad[None], ("fsdp", "tp"))
        rate_matrix = d ** (-0.5)
        rate_output = 4.0 * d ** (-0.5)
        down_total = down_sum[None]
        up_total = up_total.astype(f32)
        results = [layer_output, input_grad]
        for weight, first, second, grad, rate, decay in (
            (qkv_weight, qkv_first, qkv_second, qkv_total, rate_matrix, decay_rate),
            (out_weight, out_first, out_second, out_total, rate_output, decay_rate),
            (up_weight, up_first, up_second, up_total, rate_matrix, decay_rate),
            (down_weight, down_first, down_second, down_total, rate_matrix, decay_rate),
            (small_params, small_first, small_second, small_total, rate_vector, 0.0),
        ):
            results.extend(adam_step(weight, first, second, grad, rate, decay))
        return tuple(results)

    return local


def solution(mesh):
    tokens = P(("fsdp", "tp"), None)
    inner = P(None, ("tp", "fsdp"), None)
    qkv = P(None, None, "fsdp", "tp")
    up = P(None, "fsdp", "tp")
    weights = (qkv,) * 3 + (inner,) * 3 + (up,) * 3 + (inner,) * 3 + (P(),) * 3
    return jax.shard_map(
        make_local(mesh.shape["fsdp"], mesh.shape["tp"]),
        mesh=mesh,
        in_specs=(tokens, tokens, P("fsdp", None)) + weights,
        out_specs=(tokens, tokens) + weights,
        check_vma=False,
    )
```

```python
import functools

import jax
import jax.numpy as jnp
from jax import lax
from jax.experimental import pallas as pl
from jax.experimental.pallas import tpu as pltpu
from jax.sharding import PartitionSpec as P

HD = 256
ROT = 64
STEP = 10

norm_eps = 1e-05
beta_one = 0.9
beta_two = 0.95
adam_eps = 1e-08
decay_rate = 0.01
rate_vector = 0.2
masked_score = -1e30
f32 = jnp.float32
bf16 = jnp.bfloat16


def rotary_tables(seg_ids):
    length = seg_ids.shape[0]
    indices = jnp.arange(length, dtype=jnp.int32)
    earlier = jnp.sum((seg_ids[None, :] < seg_ids[:, None]).astype(jnp.int32), axis=1)
    position = (indices - earlier).astype(f32)
    inverse_freq = 10000.0 ** (-jnp.arange(0, ROT, 2).astype(f32) / ROT)
    angle = position[:, None] * inverse_freq[None, :]
    return (jnp.cos(angle), jnp.sin(angle))


def rotate(values, cosine, sine):
    half_dims = cosine.shape[-1]
    first_half = values[..., :half_dims]
    second_half = values[..., half_dims : 2 * half_dims]
    remainder = values[..., 2 * half_dims :]
    return jnp.concatenate(
        [
            first_half * cosine - second_half * sine,
            second_half * cosine + first_half * sine,
            remainder,
        ],
        axis=-1,
    )


def adam_step(weight, first, second, grad, rate, decay):
    first_new = beta_one * first + (1.0 - beta_one) * grad
    second_new = beta_two * second + (1.0 - beta_two) * grad * grad
    first_hat = first_new / (1.0 - beta_one**STEP)
    second_hat = second_new / (1.0 - beta_two**STEP)
    weight_new = weight - rate * (first_hat / (jnp.sqrt(second_hat) + adam_eps) + decay * weight)
    return (first_new, second_new, weight_new)


def dot(a, b, dims, out=f32):
    return lax.dot_general(a, b, (dims, ((), ())), preferred_element_type=out)


MESH = pl.DeviceIdType.MESH


def bit_of(i, mask):
    return (i // mask) % 2


def flip(i, mask):
    return i + mask - 2 * mask * bit_of(i, mask)


class Links:
    def __init__(self, send_sem, recv_sem):
        self.send_sem, self.recv_sem, self.count, self.started = send_sem, recv_sem, 0, []

    def copy(self, src, dst, device):
        k = self.count
        self.count += 1
        c = pltpu.make_async_remote_copy(
            src_ref=src,
            dst_ref=dst,
            send_sem=self.send_sem.at[k],
            recv_sem=self.recv_sem.at[k],
            device_id=device,
            device_id_type=MESH,
        )
        self.started.append(c)
        return c


class Group:
    def __init__(self, links, buf, slot, f, t, masks, root):
        self.links, self.buf, self.slot, self.f, self.t, self.masks = links, buf, slot, f, t, masks
        self.root, self.copies = root, {}

    def _source(self, key):
        g = self.root
        for mask in self.masks:
            if key & mask:
                g = flip(g, mask)
        return g

    def have(self, key):
        after = max([i + 1 for i, m in enumerate(self.masks) if key & m], default=0)
        for mask in self.masks[after:]:
            ref = self.buf.at[self.slot(self._source(key))]
            c = self.links.copy(ref, ref, (flip(self.f, mask), self.t))
            c.start()
            self.copies[key | mask] = c

    def arrive(self, key):
        self.copies[key].wait_recv()
        self.have(key)


def gather_kernel(fsdp, masks, top, x, e, up, qkv, down, out, xa, ea, upa, qkva, downa, outa, send_sem, recv_sem, local_sem):
    f = lax.axis_index("fsdp")
    t = lax.axis_index("tp")
    mid = bit_of(f, 2)
    swapped = f + (top - 2) * (mid - bit_of(f, top))
    barrier = pltpu.get_barrier_semaphore()
    peers = [(flip(f, m), t) for m in masks + [2]] + [(f, flip(t, 1)), (f, flip(t, 2))]
    for peer in peers:
        pl.semaphore_signal(barrier, inc=1, device_id=peer, device_id_type=MESH)

    @pl.when(swapped != f)
    def _():
        pl.semaphore_signal(barrier, inc=1, device_id=(swapped, t), device_id_type=MESH)

    pl.semaphore_wait(barrier, len(peers) + (mid + bit_of(f, top)) % 2)
    links = Links(send_sem, recv_sem)
    locals_ = []

    def local_copy(src, dst):
        c = pltpu.make_async_copy(src, dst, local_sem.at[len(locals_)])
        locals_.append(c)
        c.start()
        return c

    mid_peer, y_peer, core_peer = (flip(f, 2), t), (f, flip(t, 2)), (f, flip(t, 1))
    n_top = top // 4

    def out_slot(g):
        return (((g // 4) % n_top) * 2 + g // top) * 2 + g % 2

    def down_slot(g):
        return (g // 4) * 2 + g % 2

    def same(g):
        return g

    qkv_own = Group(links, qkva, same, f, t, masks, f)
    qkv_mid = Group(links, qkva, same, f, t, masks, flip(f, 2))
    up_own = Group(links, upa, same, f, t, masks, f)
    up_mid = Group(links, upa, same, f, t, masks, flip(f, 2))
    down_own = Group(links, downa, down_slot, f, t, masks, f)
    out_own = Group(links, outa, out_slot, f, t, masks, f)

    def spread(group, source):
        for mask in group.masks:
            c = links.copy(source, group.buf.at[group.slot(f)], (flip(f, mask), t))
            c.start()
            group.copies[mask] = c

    first_qkv = links.copy(qkv.at[1 - mid], qkva.at[f], mid_peer)
    first_qkv.start()
    spread(qkv_own, qkv.at[mid])

    def tokens(source, buf):
        parts = {}
        for name, peer in (("m", mid_peer), ("y", y_peer), ("c", core_peer)):
            c = links.copy(source, buf.at[mid, t], peer)
            c.start()
            parts[name] = c
        return parts

    def tokens_mid(buf, parts):
        parts["m"].wait_recv()
        ref = buf.at[1 - mid, t]
        for name, peer in (("my", y_peer), ("mc", core_peer)):
            parts[name] = links.copy(ref, ref, peer)
            parts[name].start()

    def tokens_y(buf, parts):
        parts["y"].wait_recv()
        ref = buf.at[mid, flip(t, 2)]
        parts["yc"] = links.copy(ref, ref, core_peer)
        parts["yc"].start()

    def tokens_last(buf, parts):
        parts["my"].wait_recv()
        ref = buf.at[1 - mid, flip(t, 2)]
        parts["myc"] = links.copy(ref, ref, core_peer)
        parts["myc"].start()

    def tokens_done(parts):
        for name in ("c", "mc", "yc", "myc"):
            parts[name].wait_recv()

    x_parts = tokens(x, xa)
    swap_copy = links.copy(out, outa.at[out_slot(swapped)], (swapped, t))
    own_out = pltpu.make_async_copy(out, outa.at[out_slot(f)], local_sem.at[5])

    @pl.when(swapped != f)
    def _():
        swap_copy.start()

    @pl.when(swapped == f)
    def _():
        own_out.start()

    first_up = links.copy(up.at[1 - mid], upa.at[f], mid_peer)
    first_up.start()
    own = [
        local_copy(qkv.at[mid], qkva.at[f]),
        local_copy(x, xa.at[mid, t]),
        local_copy(up.at[mid], upa.at[f]),
        local_copy(e, ea.at[mid, t]),
        local_copy(down, downa.at[down_slot(f)]),
    ]
    first_qkv.wait_recv()
    qkv_mid.have(0)
    spread(up_own, up.at[mid])
    e_parts = tokens(e, ea)
    tokens_mid(xa, x_parts)
    tokens_y(xa, x_parts)

    @pl.when(swapped != f)
    def _():
        swap_copy.wait_recv()

    @pl.when(swapped == f)
    def _():
        own_out.wait()

    out_own.have(0)
    for group in (qkv_own,):
        for key in all_keys(masks)[1:]:
            group.arrive(key)
    first_up.wait_recv()
    up_mid.have(0)
    for key in all_keys(masks)[1:]:
        qkv_mid.arrive(key)
    tokens_last(xa, x_parts)
    for key in all_keys(masks)[1:]:
        out_own.arrive(key)
    spread(down_own, down)
    tokens_mid(ea, e_parts)
    tokens_y(ea, e_parts)
    tokens_done(x_parts)
    for key in all_keys(masks)[1:]:
        up_own.arrive(key)
    for key in all_keys(masks)[1:]:
        up_mid.arrive(key)
    tokens_last(ea, e_parts)
    tokens_done(e_parts)
    for key in all_keys(masks)[1:]:
        down_own.arrive(key)
    for c in own:
        c.wait()
    for c in links.started:
        if c is swap_copy:

            @pl.when(swapped != f)
            def _():
                swap_copy.wait_send()

        else:
            c.wait_send()


def all_keys(masks):
    keys = [0]
    for mask in masks:
        keys = keys + [k | mask for k in keys]
    return keys


def gather_all(fsdp, masks, top, x, e, up, qkv, down, out, tp):
    rows, d = x.shape
    n_keys = 1 << len(masks)
    copies = 2 * 7 + 2 * (1 + 2 * (n_keys - 1)) + n_keys - 1 + n_keys
    shape = jax.ShapeDtypeStruct
    return pl.pallas_call(
        functools.partial(gather_kernel, fsdp, masks, top),
        out_shape=(
            shape((2, tp, rows, d), bf16),
            shape((2, tp, rows, d), bf16),
            shape((fsdp,) + up.shape[1:], bf16),
            shape((fsdp,) + qkv.shape[1:], bf16),
            shape((fsdp // 2,) + down.shape, bf16),
            shape((fsdp // 2,) + out.shape, bf16),
        ),
        in_specs=[pl.BlockSpec(memory_space=pl.ANY)] * 6,
        out_specs=(pl.BlockSpec(memory_space=pl.ANY),) * 6,
        scratch_shapes=[
            pltpu.SemaphoreType.DMA((copies,)),
            pltpu.SemaphoreType.DMA((copies,)),
            pltpu.SemaphoreType.DMA((6,)),
        ],
        compiler_params=pltpu.CompilerParams(collective_id=0, has_side_effects=True),
        name="gather_all",
    )(x, e, up, qkv, down, out)


def make_local(fsdp, tp):
    lo_n = 2
    mid_n = 2
    hi_n = fsdp // (lo_n * mid_n)
    hi_bits = [1 << b for b in range(2, fsdp.bit_length() - 1)]
    top = hi_bits[-1]

    def swap_top(i):
        a, b = (i & 2) // 2, (i & top) // top
        return (i & ~(2 | top)) | (2 * b) | (top * a)

    def px(v, mask):
        return lax.ppermute(v, "fsdp", [(i, i ^ mask) for i in range(fsdp)])

    def pt(v, mask):
        return lax.ppermute(v, "tp", [(i, i ^ mask) for i in range(tp)])

    def local(
        layer_input,
        out_cotangent,
        segments,
        qkv_weight,
        qkv_first,
        qkv_second,
        out_weight,
        out_first,
        out_second,
        up_weight,
        up_first,
        up_second,
        down_weight,
        down_first,
        down_second,
        small_params,
        small_first,
        small_second,
    ):
        f = lax.axis_index("fsdp")
        t = lax.axis_index("tp")
        mid = (f // 2) % 2
        hi = f // 4
        lo = f % 2
        core = t % 2
        half_t = t // 2
        rows, d = layer_input.shape
        length = segments.shape[1]
        width = qkv_weight.shape[3]
        hidden = up_weight.shape[2]
        hidden_all = small_params.shape[1] - 9 * d
        sub = hidden // fsdp
        feat = d // fsdp
        mine = hidden // 2
        orow = width // fsdp
        vector = small_params[0]

        up16 = up_weight[0].astype(bf16).reshape(feat, hi_n, 2, lo_n * sub)
        up16 = up16.transpose(2, 0, 1, 3).reshape(2, feat, mine)
        qkv16 = qkv_weight[0].astype(bf16).reshape(3, feat, 2, HD)
        qkv16 = qkv16.transpose(2, 1, 0, 3).reshape(2, feat, 3 * HD)
        down16 = down_weight[0].astype(bf16)
        out16 = out_weight[0].astype(bf16)

        def pick(v, index, axis):
            return lax.dynamic_index_in_dim(v, index, axis, keepdims=False)

        def scatter_tokens(part):
            part = part.reshape(2, tp // 2, 2, rows, d)
            keep = pick(part, core, 2)
            give = pick(part, 1 - core, 2)
            part = (keep.astype(f32) + pt(give, 1).astype(f32)).astype(bf16)
            keep = pick(part, half_t, 1)
            give = pick(part, 1 - half_t, 1)
            part = (keep.astype(f32) + pt(give, 2).astype(f32)).astype(bf16)
            keep = pick(part, mid, 0)
            give = pick(part, 1 - mid, 0)
            return keep.astype(f32) + px(give, 2).astype(f32)

        def scatter_group(part):
            keep = pick(part, lo, 1)
            give = pick(part, 1 - lo, 1)
            got = px(give, 1)
            index = hi
            total = keep.astype(f32) + got.astype(f32)
            for mask in reversed(hi_bits):
                total = total.astype(bf16)
                bit = mask // 4
                n = total.shape[0] // 2
                upper = (index & bit) // bit
                shaped = total.reshape((2, n) + total.shape[1:])
                keep = pick(shaped, upper, 0)
                give = pick(shaped, 1 - upper, 0)
                total = keep.astype(f32) + px(give, mask).astype(f32)
            return total[0]

        def halves(v, axis):
            return pick(v, mid, axis), pick(v, 1 - mid, axis)

        x_all, e_all, up_full, qkv_full, down_full, out_full = gather_all(
            fsdp, hi_bits + [1], top, layer_input, out_cotangent, up16, qkv16, down16, out16, tp
        )
        x_all = x_all.reshape(2 * tp * rows, d)
        e_all = e_all.reshape(2 * tp * rows, d)
        up_full = up_full.reshape(d, mine)
        qkv_full = qkv_full.reshape(d, 3 * HD)
        down_full = down_full.reshape(mine, d)
        out_full = out_full.reshape(HD, d)
        swap_perm = [(i, swap_top(i)) for i in range(fsdp)]

        seg_other = px(segments.astype(f32), 2).astype(jnp.int32)
        seg = jnp.where(mid == 0, jnp.concatenate([segments, seg_other]), jnp.concatenate([seg_other, segments]))
        cosine, sine = jax.vmap(rotary_tables)(seg)
        idx = jnp.arange(length, dtype=jnp.int32)
        allowed = (idx[None, :] <= idx[:, None])[None] & (seg[:, :, None] == seg[:, None, :])

        stream = layer_input.astype(f32)
        x32 = x_all.astype(f32)
        mean_row = jnp.mean(x32, axis=-1, keepdims=True)
        centred = x32 - mean_row
        inverse = lax.rsqrt(jnp.mean(centred * centred, axis=-1, keepdims=True) + norm_eps)
        normal = centred * inverse
        gain_one, shift_one = vector[0:d], vector[d : 2 * d]
        gain_two, shift_two = vector[2 * d : 3 * d], vector[3 * d : 4 * d]
        bias_out, bias_down = vector[4 * d : 5 * d], vector[5 * d : 6 * d]
        qkv_bias = lax.dynamic_slice_in_dim(
            vector[6 * d : 9 * d].reshape(3, d), t * width + mid * HD, HD, 1
        )
        up_bias = pick(
            pick(vector[9 * d :].reshape(tp, hi_n, 2, lo_n * sub), t, 0), mid, 1
        ).reshape(mine)
        rows_one = (normal * gain_one + shift_one).astype(bf16)
        rows_two = (normal * gain_two + shift_two).astype(bf16)

        pre_act = dot(rows_two, up_full, ((1,), (0,))) + up_bias
        cdf = 0.5 * (1.0 + lax.erf(pre_act * 0.7071067811865476))
        active = (pre_act * cdf).astype(bf16)
        slope = (cdf + pre_act * (jnp.exp(-0.5 * pre_act * pre_act) * 0.3989422804014327)).astype(bf16)
        down_grad = dot(active, e_all, ((0,), (0,)), bf16)
        down_sum = scatter_group(down_grad.reshape(hi_n, lo_n, sub, d))
        active_grad = dot(e_all, down_full, ((1,), (1,)))
        pre_grad = (active_grad * slope.astype(f32)).astype(bf16)
        up_grad = dot(rows_two, pre_grad, ((0,), (0,)), bf16)
        up_bias_grad = jnp.sum(pre_grad, axis=0, dtype=f32)

        up_sum = scatter_group(
            up_grad.reshape(hi_n, 2, lo_n, feat, mine).transpose(0, 2, 1, 3, 4)
        ).astype(bf16)
        keep, give = halves(up_sum, 0)
        got = px(give, 2)
        up_total = jnp.where(
            mid == 0,
            jnp.stack([keep.reshape(feat, hi_n, lo_n * sub), got.reshape(feat, hi_n, lo_n * sub)], 2),
            jnp.stack([got.reshape(feat, hi_n, lo_n * sub), keep.reshape(feat, hi_n, lo_n * sub)], 2),
        ).reshape(1, feat, hidden)

        proj = dot(rows_one, qkv_full, ((1,), (0,))) + qkv_bias.reshape(3 * HD)
        proj = proj.reshape(2, length, 3, HD)
        query = rotate(proj[:, :, 0], cosine, sine).astype(bf16)
        key = rotate(proj[:, :, 1], cosine, sine).astype(bf16)
        value = proj[:, :, 2].astype(bf16)
        scale = HD ** (-0.5)
        scores = jnp.einsum("bqd,bkd->bqk", query, key, preferred_element_type=f32) * scale
        scores = jnp.where(allowed, scores, masked_score)
        peak = jnp.max(scores, axis=-1, keepdims=True)
        total = jnp.log(jnp.sum(jnp.exp(scores - peak), axis=-1, keepdims=True)) + peak
        probs = jnp.exp(scores - total)
        weights = probs.astype(bf16)
        mixed = jnp.einsum("bqk,bkd->bqd", weights, value, preferred_element_type=f32)
        mixed = mixed.astype(bf16).reshape(2 * length, HD)
        out_grad = dot(mixed, e_all, ((0,), (0,)), bf16)
        out_sum = scatter_group(
            jnp.moveaxis(
                out_grad.reshape(hi_n // 2, 2, lo_n, orow, d), 1, 0
            ).reshape(hi_n, lo_n, orow, d)
        ).astype(bf16)
        out_total = lax.ppermute(out_sum, "fsdp", swap_perm)[None].astype(f32)
        mixed_grad = dot(e_all, out_full, ((1,), (1,)), bf16).reshape(2, length, HD)
        prob_grad = jnp.einsum("bqd,bkd->bqk", mixed_grad, value, preferred_element_type=f32)
        inner = jnp.sum(probs * prob_grad, axis=-1, keepdims=True)
        score_grad = (probs * (prob_grad - inner)).astype(bf16)
        query_grad = jnp.einsum("bqk,bkd->bqd", score_grad, key, preferred_element_type=f32) * scale
        key_grad = jnp.einsum("bqk,bqd->bkd", score_grad, query, preferred_element_type=f32) * scale
        value_grad = jnp.einsum("bqk,bqd->bkd", weights, mixed_grad, preferred_element_type=f32)
        proj_grad = jnp.concatenate(
            [rotate(query_grad, cosine, -sine), rotate(key_grad, cosine, -sine), value_grad], -1
        ).astype(bf16).reshape(2 * length, 3 * HD)
        qkv_grad = dot(rows_one, proj_grad, ((0,), (0,)), bf16)
        qkv_bias_grad = jnp.sum(proj_grad, axis=0, dtype=f32).reshape(3, HD)
        qkv_sum = scatter_group(
            qkv_grad.reshape(hi_n, 2, lo_n, feat, 3 * HD).transpose(0, 2, 1, 3, 4)
        ).astype(bf16)
        keep, give = halves(qkv_sum, 0)
        got = px(give, 2)
        qkv_total = jnp.where(
            mid == 0, jnp.stack([keep, got]), jnp.stack([got, keep])
        ).reshape(2, feat, 3, HD).transpose(2, 1, 0, 3).reshape(1, 3, feat, width).astype(f32)

        branch = dot(mixed, out_full, ((1,), (0,))) + dot(active, down_full, ((1,), (0,)))
        layer_output = stream + scatter_tokens(branch.astype(bf16)) + bias_out + bias_down

        first_norm = dot(proj_grad, qkv_full, ((1,), (1,)))
        second_norm = dot(pre_grad, up_full, ((1,), (1,)))
        gain_one_grad = jnp.sum(first_norm * normal, axis=0)
        shift_one_grad = jnp.sum(first_norm, axis=0)
        gain_two_grad = jnp.sum(second_norm * normal, axis=0)
        shift_two_grad = jnp.sum(second_norm, axis=0)
        scaled = scatter_tokens((first_norm * gain_one + second_norm * gain_two).astype(bf16))
        own_mean = jnp.mean(stream, axis=-1, keepdims=True)
        own_centred = stream - own_mean
        own_inverse = lax.rsqrt(jnp.mean(own_centred * own_centred, axis=-1, keepdims=True) + norm_eps)
        own_normal = own_centred * own_inverse
        gradient = out_cotangent.astype(f32)
        input_grad = gradient + own_inverse * (
            scaled
            - jnp.mean(scaled, axis=-1, keepdims=True)
            - own_normal * jnp.mean(scaled * own_normal, axis=-1, keepdims=True)
        )

        bias_grad = jnp.sum(gradient, axis=0)
        qkv_spread = lax.dynamic_update_slice(
            jnp.zeros((3, d), f32), qkv_bias_grad, (0, t * width + mid * HD)
        )
        up_spread = lax.dynamic_update_slice(
            jnp.zeros((tp, hi_n, 2, lo_n * sub), f32),
            up_bias_grad.reshape(1, hi_n, 1, lo_n * sub),
            (t, 0, mid, 0),
        )
        small_grad = jnp.concatenate(
            [
                gain_one_grad,
                shift_one_grad,
                gain_two_grad,
                shift_two_grad,
                bias_grad,
                bias_grad,
                qkv_spread.reshape(-1),
                up_spread.reshape(-1),
            ]
        )
        small_total = small_grad[None]
        for mask in (1, 2):
            small_total = small_total + pt(small_total, mask)
        for mask in [1, 2] + hi_bits:
            small_total = small_total + px(small_total, mask)
        rate_matrix = d ** (-0.5)
        rate_output = 4.0 * d ** (-0.5)
        down_total = down_sum[None]
        up_total = up_total.astype(f32)
        results = [layer_output, input_grad]
        for weight, first, second, grad, rate, decay in (
            (qkv_weight, qkv_first, qkv_second, qkv_total, rate_matrix, decay_rate),
            (out_weight, out_first, out_second, out_total, rate_output, decay_rate),
            (up_weight, up_first, up_second, up_total, rate_matrix, decay_rate),
            (down_weight, down_first, down_second, down_total, rate_matrix, decay_rate),
            (small_params, small_first, small_second, small_total, rate_vector, 0.0),
        ):
            results.extend(adam_step(weight, first, second, grad, rate, decay))
        return tuple(results)

    return local


def solution(mesh):
    tokens = P(("fsdp", "tp"), None)
    inner = P(None, ("tp", "fsdp"), None)
    qkv = P(None, None, "fsdp", "tp")
    up = P(None, "fsdp", "tp")
    weights = (qkv,) * 3 + (inner,) * 3 + (up,) * 3 + (inner,) * 3 + (P(),) * 3
    return jax.shard_map(
        make_local(mesh.shape["fsdp"], mesh.shape["tp"]),
        mesh=mesh,
        in_specs=(tokens, tokens, P("fsdp", None)) + weights,
        out_specs=(tokens, tokens) + weights,
        check_vma=False,
    )
```

```python
import functools

import jax
import jax.numpy as jnp
from jax import lax
from jax.experimental import pallas as pl
from jax.experimental.pallas import tpu as pltpu
from jax.sharding import PartitionSpec as P

HD = 256
ROT = 64
STEP = 10

norm_eps = 1e-05
beta_one = 0.9
beta_two = 0.95
adam_eps = 1e-08
decay_rate = 0.01
rate_vector = 0.2
masked_score = -1e30
f32 = jnp.float32
bf16 = jnp.bfloat16


def adam_step(weight, first, second, grad, rate, decay):
    first_new = beta_one * first + (1.0 - beta_one) * grad
    second_new = beta_two * second + (1.0 - beta_two) * grad * grad
    first_hat = first_new / (1.0 - beta_one**STEP)
    second_hat = second_new / (1.0 - beta_two**STEP)
    weight_new = weight - rate * (first_hat / (jnp.sqrt(second_hat) + adam_eps) + decay * weight)
    return (first_new, second_new, weight_new)


MESH = pl.DeviceIdType.MESH


def bit_of(i, mask):
    return (i // mask) % 2


def flip(i, mask):
    return i + mask - 2 * mask * bit_of(i, mask)


class Links:
    def __init__(self, send_sem, recv_sem):
        self.send_sem, self.recv_sem, self.count, self.started = send_sem, recv_sem, 0, []

    def copy(self, src, dst, device):
        k = self.count
        self.count += 1
        c = pltpu.make_async_remote_copy(
            src_ref=src,
            dst_ref=dst,
            send_sem=self.send_sem.at[k],
            recv_sem=self.recv_sem.at[k],
            device_id=device,
            device_id_type=MESH,
        )
        self.started.append(c)
        return c


class Group:
    def __init__(self, links, at, f, t, masks, root):
        self.links, self.at, self.f, self.t, self.masks = links, at, f, t, masks
        self.root, self.copies = root, {}

    def _source(self, key):
        g = self.root
        for mask in self.masks:
            if key & mask:
                g = flip(g, mask)
        return g

    def have(self, key):
        after = max([i + 1 for i, m in enumerate(self.masks) if key & m], default=0)
        for mask in self.masks[after:]:
            ref = self.at(self._source(key))
            c = self.links.copy(ref, ref, (flip(self.f, mask), self.t))
            c.start()
            self.copies[key | mask] = c

    def arrive(self, key):
        self.copies[key].wait_recv()
        self.have(key)


def all_keys(masks):
    keys = [0]
    for mask in masks:
        keys = keys + [k | mask for k in keys]
    return keys


def normalise(x):
    mean = jnp.mean(x, axis=-1, keepdims=True)
    centred = x - mean
    inverse = lax.rsqrt(jnp.mean(centred * centred, axis=-1, keepdims=True) + norm_eps)
    return centred * inverse


def rope(u, c, s):
    lane = lax.broadcasted_iota(jnp.int32, u.shape, 1)
    partner = jnp.where(lane < ROT // 2, pltpu.roll(u, 128 - ROT // 2, 1), pltpu.roll(u, ROT // 2, 1))
    return u * c + partner * s


def dot(a, b, dims):
    return lax.dot_general(a, b, (dims, ((), ())), preferred_element_type=f32)


NN = ((1,), (0,))
NT = ((1,), (1,))
TN = ((0,), (0,))
TILE = 256


def tiles(width):
    return pl.BlockSpec((TILE, width), lambda i: (i, 0))


def columns(height, width):
    return pl.BlockSpec((height, width), lambda i: (0, i))


def held(height, width):
    return pl.BlockSpec((height, width), lambda i: (0, 0))


def run_project(vec, qkv_bias, x, w, c, s, n1, n2, p):
    tokens, d = x.shape
    wide = w.shape[1]

    def body(x_ref, w_ref, c_ref, s_ref, n1_ref, n2_ref, p_ref):
        normal = normalise(x_ref[...].astype(f32))
        one = (normal * vec[0:1, :] + vec[1:2, :]).astype(bf16)
        n1_ref[...] = one
        n2_ref[...] = (normal * vec[2:3, :] + vec[3:4, :]).astype(bf16)
        proj = dot(one, w_ref[...], NN) + qkv_bias[...]
        for j in range(2):
            p_ref[:, j * HD : j * HD + 128] = rope(
                proj[:, j * HD : j * HD + 128], c_ref[...], s_ref[...]
            ).astype(bf16)
            p_ref[:, j * HD + 128 : (j + 1) * HD] = proj[:, j * HD + 128 : (j + 1) * HD].astype(bf16)
        p_ref[:, 2 * HD :] = proj[:, 2 * HD :].astype(bf16)

    pltpu.emit_pipeline(
        body,
        grid=(tokens // TILE,),
        in_specs=[tiles(d), held(d, wide), tiles(128), tiles(128)],
        out_specs=[tiles(d), tiles(d), tiles(wide)],
    )(x, w, c, s, n1, n2, p)


def run_times(a, b, out, dims):
    def body(a_ref, b_ref, out_ref):
        out_ref[...] = dot(a_ref[...], b_ref[...], dims).astype(bf16)

    pltpu.emit_pipeline(
        body,
        grid=(a.shape[0] // TILE,),
        in_specs=[tiles(a.shape[1]), held(*b.shape)],
        out_specs=[tiles(out.shape[1])],
    )(a, b, out)


def run_outer(a, b, out):
    def body(a_ref, b_ref, out_ref):
        out_ref[...] = dot(a_ref[...], b_ref[...], TN).astype(bf16)

    pltpu.emit_pipeline(
        body,
        grid=(a.shape[1] // TILE,),
        in_specs=[columns(a.shape[0], TILE), held(*b.shape)],
        out_specs=[tiles(b.shape[1])],
    )(a, b, out)


def run_outer_wide(a, b, out):
    block = 2 * TILE

    def body(a_ref, b_ref, out_ref):
        out_ref[...] = dot(a_ref[...], b_ref[...], TN).astype(bf16)

    pltpu.emit_pipeline(
        body,
        grid=(b.shape[1] // block,),
        in_specs=[held(*a.shape), columns(b.shape[0], block)],
        out_specs=[columns(a.shape[1], block)],
    )(a, b, out)


def run_attention(length, bounds, p, da, c, s, a, dproj, dk, dv):
    scale = HD ** (-0.5)
    rows = pl.BlockSpec((length, HD), lambda i: (i, 0))
    wide = pl.BlockSpec((length, 3 * HD), lambda i: (i, 0))
    narrow = pl.BlockSpec((length, 128), lambda i: (i, 0))

    def body(p_ref, da_ref, c_ref, s_ref, a_ref, out_ref):
        seq = pl.program_id(0)
        first, second = bounds[seq, 0], bounds[seq, 1]

        def put(at, value, column):
            out_ref[at, column : column + 128] = rope(value[:, :128], c_ref[at, :], -s_ref[at, :]).astype(bf16)
            out_ref[at, column + 128 : column + HD] = value[:, 128:].astype(bf16)

        dk[...] = jnp.zeros_like(dk)
        dv[...] = jnp.zeros_like(dv)
        for i in range(length // TILE):
            at = slice(i * TILE, (i + 1) * TILE)
            n = (i + 1) * TILE
            q = p_ref[at, 0:HD]
            k = p_ref[0:n, HD : 2 * HD]
            v = p_ref[0:n, 2 * HD :]
            rows_da = da_ref[at, :]
            scores = dot(q, k, NT) * scale
            qi = i * TILE + lax.broadcasted_iota(jnp.int32, (TILE, n), 0)
            ki = lax.broadcasted_iota(jnp.int32, (TILE, n), 1)
            start = jnp.where(qi >= second, second, jnp.where(qi >= first, first, 0))
            scores = jnp.where((ki <= qi) & (ki >= start), scores, masked_score)
            peak = jnp.max(scores, axis=-1, keepdims=True)
            raised = jnp.exp(scores - peak)
            probs = raised * (1.0 / jnp.sum(raised, axis=-1, keepdims=True))
            weights = probs.astype(bf16)
            a_ref[at, :] = dot(weights, v, NN).astype(bf16)
            prob_grad = dot(rows_da, v, NT)
            delta = jnp.sum(probs * prob_grad, axis=-1, keepdims=True)
            score_grad = (probs * (prob_grad - delta)).astype(bf16)
            put(at, dot(score_grad, k, NN) * scale, 0)
            dk[0:n, :] += dot(score_grad, q, TN)
            dv[0:n, :] += dot(weights, rows_da, TN)
        for i in range(length // TILE):
            at = slice(i * TILE, (i + 1) * TILE)
            put(at, dk[at, :] * scale, HD)
            out_ref[at, 2 * HD :] = dv[at, :].astype(bf16)

    pltpu.emit_pipeline(
        body,
        grid=(p.shape[0] // length,),
        in_specs=[wide, rows, narrow, narrow],
        out_specs=[rows, wide],
    )(p, da, c, s, a, dproj)


def run_up(up_bias, n2, w, g, slope):
    def body(n_ref, w_ref, g_ref, s_ref):
        h = dot(n_ref[...], w_ref[...], NN) + up_bias[...]
        cdf = 0.5 + 0.5 * lax.erf(h * 0.7071067811865476)
        g_ref[...] = (h * cdf).astype(bf16)
        s_ref[...] = (cdf + h * (jnp.exp(-0.5 * h * h) * 0.3989422804014327)).astype(bf16)

    width = w.shape[1]
    pltpu.emit_pipeline(
        body,
        grid=(n2.shape[0] // TILE,),
        in_specs=[tiles(n2.shape[1]), held(*w.shape)],
        out_specs=[tiles(width), tiles(width)],
    )(n2, w, g, slope)


def run_hidden_grad(e, w, slope, dh, bias_sum):
    def body(e_ref, w_ref, s_ref, dh_ref):
        @pl.when(pl.program_id(0) == 0)
        def _():
            bias_sum[...] = jnp.zeros_like(bias_sum)

        value = (dot(e_ref[...], w_ref[...], NT) * s_ref[...].astype(f32)).astype(bf16)
        dh_ref[...] = value
        bias_sum[0:1, :] += jnp.sum(value.astype(f32), axis=0, keepdims=True)

    width = w.shape[0]
    pltpu.emit_pipeline(
        body,
        grid=(e.shape[0] // TILE,),
        in_specs=[tiles(e.shape[1]), held(*w.shape), tiles(width)],
        out_specs=[tiles(width)],
    )(e, w, slope, dh)


def run_branch(a, w_out, g, w_down, out):
    def body(a_ref, wo_ref, g_ref, wd_ref, out_ref):
        out_ref[...] = (dot(a_ref[...], wo_ref[...], NN) + dot(g_ref[...], wd_ref[...], NN)).astype(bf16)

    pltpu.emit_pipeline(
        body,
        grid=(a.shape[0] // TILE,),
        in_specs=[tiles(a.shape[1]), held(*w_out.shape), tiles(g.shape[1]), held(*w_down.shape)],
        out_specs=[tiles(out.shape[1])],
    )(a, w_out, g, w_down, out)


def run_norm_grad(vec, dh, w_up, dproj, w_qkv, x, out, sums, qkv_sum):
    def body(dh_ref, wu_ref, dp_ref, wq_ref, x_ref, out_ref):
        @pl.when(pl.program_id(0) == 0)
        def _():
            sums[...] = jnp.zeros_like(sums)
            qkv_sum[...] = jnp.zeros_like(qkv_sum)

        normal = normalise(x_ref[...].astype(f32))
        one = dot(dp_ref[...], wq_ref[...], NT)
        two = dot(dh_ref[...], wu_ref[...], NT)
        for j, value in ((0, one * normal), (1, one), (2, two * normal), (3, two)):
            sums[j : j + 1, :] += jnp.sum(value, axis=0, keepdims=True)
        out_ref[...] = (one * vec[0:1, :] + two * vec[2:3, :]).astype(bf16)
        qkv_sum[0:1, :] += jnp.sum(dp_ref[...].astype(f32), axis=0, keepdims=True)

    pltpu.emit_pipeline(
        body,
        grid=(x.shape[0] // TILE,),
        in_specs=[tiles(dh.shape[1]), held(*w_up.shape), tiles(dproj.shape[1]), held(*w_qkv.shape), tiles(x.shape[1])],
        out_specs=[tiles(out.shape[1])],
    )(dh, w_up, dproj, w_qkv, x, out)


def run_add(a, b, out):
    rows, cols = out.shape
    step = min(rows, TILE)

    def body(a_ref, b_ref, out_ref):
        out_ref[...] = (a_ref[...].astype(f32) + b_ref[...].astype(f32)).astype(bf16)

    spec = pl.BlockSpec((step, cols), lambda i: (i, 0))
    pltpu.emit_pipeline(body, grid=(rows // step,), in_specs=[spec, spec], out_specs=[spec])(a, b, out)


def block(ref, index, rows):
    return ref.at[pl.ds(pl.multiple_of(index * rows, rows), rows)]


def out_place(g, top):
    return (((g // 4) % (top // 4)) * 2 + g // top) * 2 + g % 2


def greet(f, t, masks, top):
    mid = bit_of(f, 2)
    swapped = f + (top - 2) * (mid - bit_of(f, top))
    barrier = pltpu.get_barrier_semaphore()
    peers = [(flip(f, m), t) for m in masks + [2]] + [(f, flip(t, 1)), (f, flip(t, 2))]
    for peer in peers:
        pl.semaphore_signal(barrier, inc=1, device_id=peer, device_id_type=MESH)

    @pl.when(swapped != f)
    def _():
        pl.semaphore_signal(barrier, inc=1, device_id=(swapped, t), device_id_type=MESH)

    pl.semaphore_wait(barrier, len(peers) + (mid + bit_of(f, top)) % 2)
    return swapped


def gather_kernel(
    masks, top, length,
    x, e, up, qkv, down, out, cos, sin, vec, qkv_bias, up_bias, bounds,
    xa, ea, upa, qkva, downa, outa, n1, n2, p, da, a, dproj, g_qkv, g_out, g, slope, g_down,
    send_sem, recv_sem, local_sem, dk, dv,
):
    f = lax.axis_index("fsdp")
    t = lax.axis_index("tp")
    mid = bit_of(f, 2)
    rows, feat, sub, orow = x.shape[0], up.shape[1], down.shape[0], out.shape[0]
    swapped = greet(f, t, masks, top)
    links = Links(send_sem, recv_sem)
    own = []

    def local_copy(src, dst):
        c = pltpu.make_async_copy(src, dst, local_sem.at[len(own)])
        own.append(c)
        c.start()
        return c

    mid_peer, y_peer, core_peer = (flip(f, 2), t), (f, flip(t, 2)), (f, flip(t, 1))
    qkv_block = lambda i: block(qkva, i, feat)
    up_block = lambda i: block(upa, i, feat)
    down_block = lambda i: block(downa, (i // 4) * 2 + i % 2, sub)
    out_block = lambda i: block(outa, out_place(i, top), orow)
    tok = lambda buf, m, j: block(buf, m * 4 + j, rows)
    qkv_own = Group(links, qkv_block, f, t, masks, f)
    qkv_mid = Group(links, qkv_block, f, t, masks, flip(f, 2))
    up_own = Group(links, up_block, f, t, masks, f)
    up_mid = Group(links, up_block, f, t, masks, flip(f, 2))
    down_own = Group(links, down_block, f, t, masks, f)
    out_own = Group(links, out_block, f, t, masks, f)

    def spread(group, source):
        for mask in group.masks:
            c = links.copy(source, group.at(f), (flip(f, mask), t))
            c.start()
            group.copies[mask] = c

    def tokens(source, buf):
        parts = {}
        for name, peer in (("m", mid_peer), ("y", y_peer), ("c", core_peer)):
            parts[name] = links.copy(source, tok(buf, mid, t), peer)
            parts[name].start()
        return parts

    def forward(buf, parts, name, m, j, sends):
        parts[name].wait_recv()
        ref = tok(buf, m, j)
        for new, peer in sends:
            parts[new] = links.copy(ref, ref, peer)
            parts[new].start()

    def tokens_mid(buf, parts):
        forward(buf, parts, "m", 1 - mid, t, (("my", y_peer), ("mc", core_peer)))

    def tokens_y(buf, parts):
        forward(buf, parts, "y", mid, flip(t, 2), (("yc", core_peer),))

    def tokens_last(buf, parts):
        forward(buf, parts, "my", 1 - mid, flip(t, 2), (("myc", core_peer),))

    def tokens_done(parts):
        for name in ("c", "mc", "yc", "myc"):
            parts[name].wait_recv()

    keys = all_keys(masks)[1:]
    first_qkv = links.copy(qkv.at[1 - mid], qkv_block(f), mid_peer)
    first_qkv.start()
    spread(qkv_own, qkv.at[mid])
    x_parts = tokens(x, xa)
    swap_copy = links.copy(out, out_block(swapped), (swapped, t))
    own_out = pltpu.make_async_copy(out, out_block(f), local_sem.at[5])

    @pl.when(swapped != f)
    def _():
        swap_copy.start()

    @pl.when(swapped == f)
    def _():
        own_out.start()

    first_up = links.copy(up.at[1 - mid], up_block(f), mid_peer)
    first_up.start()
    local_copy(qkv.at[mid], qkv_block(f))
    local_copy(x, tok(xa, mid, t))
    local_copy(up.at[mid], up_block(f))
    local_copy(e, tok(ea, mid, t))
    local_copy(down, down_block(f))
    first_qkv.wait_recv()
    qkv_mid.have(0)
    spread(up_own, up.at[mid])
    e_parts = tokens(e, ea)
    tokens_mid(xa, x_parts)
    tokens_y(xa, x_parts)

    @pl.when(swapped != f)
    def _():
        swap_copy.wait_recv()

    @pl.when(swapped == f)
    def _():
        own_out.wait()

    out_own.have(0)
    for key in keys:
        qkv_own.arrive(key)
    first_up.wait_recv()
    up_mid.have(0)
    for key in keys:
        qkv_mid.arrive(key)
    tokens_last(xa, x_parts)
    for key in keys:
        out_own.arrive(key)
    spread(down_own, down)
    tokens_mid(ea, e_parts)
    tokens_y(ea, e_parts)
    tokens_done(x_parts)
    own[0].wait()
    own[1].wait()
    run_project(vec, qkv_bias, xa, qkva, cos, sin, n1, n2, p)
    for key in keys:
        up_own.arrive(key)
    for key in keys:
        up_mid.arrive(key)
    tokens_last(ea, e_parts)
    tokens_done(e_parts)
    own[3].wait()
    run_times(ea, outa, da, NT)
    run_attention(length, bounds, p, da, cos, sin, a, dproj, dk, dv)
    run_outer(n1, dproj, g_qkv)
    run_outer_wide(a, ea, g_out)
    own[2].wait()
    run_up(up_bias, n2, upa, g, slope)
    run_outer(g, ea, g_down)
    for key in keys:
        down_own.arrive(key)
    own[4].wait()
    for c in links.started:
        if c is swap_copy:

            @pl.when(swapped != f)
            def _():
                swap_copy.wait_send()

        else:
            c.wait_send()


ANY = pl.BlockSpec(memory_space=pl.ANY)
VMEM = pl.BlockSpec(memory_space=pltpu.VMEM)
SMEM = pl.BlockSpec(memory_space=pltpu.SMEM)


def gather_all(masks, top, length, tp, x, e, up, qkv, down, out, cos, sin, vec, qkv_bias, up_bias, bounds):
    rows, d = x.shape
    tokens = 2 * tp * rows
    mine, wide = up.shape[2], qkv.shape[2]
    n_keys = 1 << len(masks)
    copies = 2 * 7 + 2 * (1 + 2 * (n_keys - 1)) + n_keys - 1 + n_keys
    shapes = [
        (tokens, d), (tokens, d), (d, mine), (d, wide), (mine, d), (HD, d),
        (tokens, d), (tokens, d), (tokens, wide), (tokens, HD), (tokens, HD), (tokens, wide),
        (d, wide), (HD, d), (tokens, mine), (tokens, mine), (mine, d),
    ]
    return pl.pallas_call(
        functools.partial(gather_kernel, masks, top, length),
        out_shape=[jax.ShapeDtypeStruct(shape, bf16) for shape in shapes],
        in_specs=[ANY] * 8 + [VMEM] * 3 + [SMEM],
        out_specs=[ANY] * len(shapes),
        scratch_shapes=[
            pltpu.SemaphoreType.DMA((copies,)),
            pltpu.SemaphoreType.DMA((copies,)),
            pltpu.SemaphoreType.DMA((6,)),
            pltpu.VMEM((length, HD), f32),
            pltpu.VMEM((length, HD), f32),
        ],
        compiler_params=pltpu.CompilerParams(
            collective_id=0, has_side_effects=True, vmem_limit_bytes=56 * 2**20
        ),
        name="gather_and_attend",
    )(x, e, up, qkv, down, out, cos, sin, vec, qkv_bias, up_bias, bounds)


class Scatter:
    def __init__(self, links, part, place, rows, mids, recv, sums, f, t, masks):
        self.links, self.part, self.place, self.rows, self.mids = links, part, place, rows, mids
        self.recv, self.sums, self.f, self.t = recv, sums, f, t
        self.stages = [1] + [m for m in reversed(masks) if m != 1]
        self.n_hi = 1 << (len(masks) - 1)
        self.hi, self.lo = f // 4, f % 2
        self.copies = {}

    def high(self, k):
        hi = self.hi
        b = 1
        while b < self.n_hi:
            if k & b:
                hi = flip(hi, b)
            b *= 2
        return hi

    def slot(self, level, k, m):
        n = self.n_hi >> level
        i = (self.high(k) % n) if n > 1 else 0
        return i * len(self.mids) + m

    def source(self, k, m, lo):
        mid = bit_of(self.f, 2) if m is None else m
        return block(self.part, self.place((self.high(k) * 2 + mid) * 2 + lo), self.rows)

    def start(self):
        for k in reversed(range(self.n_hi)):
            for j, m in enumerate(self.mids):
                c = self.links.copy(
                    self.source(k, m, 1 - self.lo),
                    block(self.recv[0], self.slot(0, k, j), self.rows),
                    (flip(self.f, 1), self.t),
                )
                c.start()
                self.copies[0, k, j] = c

    def add(self, level, k, out=None):
        for j, m in enumerate(self.mids):
            self.copies[level, k, j].wait_recv()
            place = self.slot(level, k, j)
            mine = (
                self.source(k, m, self.lo)
                if level == 0
                else block(self.sums[level - 1], self.slot(level - 1, k, j), self.rows)
            )
            total = block(self.sums[level], place, self.rows)
            run_add(mine, block(self.recv[level], place, self.rows), total)
            n = self.n_hi >> (level + 1)
            if n >= 1 and k & n:
                c = self.links.copy(
                    total,
                    block(self.recv[level + 1], self.slot(level + 1, k, j), self.rows),
                    (flip(self.f, self.stages[level + 1]), self.t),
                )
                c.start()
                self.copies[level + 1, k - n, j] = c

    def level(self, level):
        for k in reversed(range(self.n_hi >> level)):
            self.add(level, k)

    @property
    def last(self):
        return len(self.stages) - 1


def scatter_kernel(
    masks, top,
    e, vec, x, ea, xa, upa, qkva, downa, outa, n2, a, dproj, g_qkv, g_out, g, slope, g_down,
    *rest,
):
    n_stage = len(masks)
    (dh, g_up, norm_grad, branch), rest = rest[:4], rest[4:]
    stage_refs = []
    for _ in range(4):
        stage_refs.append((rest[:n_stage], rest[n_stage : 2 * n_stage]))
        rest = rest[2 * n_stage :]
    token_refs = [rest[:4], rest[4:8]]
    (up_new, qkv_new, out_new, small), rest = rest[8:12], rest[12:]
    (send_sem, recv_sem, local_sem, sums, qkv_sum, bias_sum, small_in) = rest
    f = lax.axis_index("fsdp")
    t = lax.axis_index("tp")
    mid = bit_of(f, 2)
    rows, d = x.shape
    fsdp = 2 << len(masks)
    feat = d // fsdp
    sub = g.shape[1] * 2 // fsdp
    orow = 2 * HD // fsdp
    mine = g.shape[1]
    swapped = greet(f, t, masks, top)
    links = Links(send_sem, recv_sem)
    mid_peer, y_peer, core_peer = (flip(f, 2), t), (f, flip(t, 2)), (f, flip(t, 1))
    down_place = lambda i: (i // 4) * 2 + i % 2
    same = lambda i: i
    qkv_s = Scatter(links, g_qkv, same, feat, (0, 1), *stage_refs[0], f, t, masks)
    out_s = Scatter(links, g_out, lambda i: out_place(i, top), orow, (None,), *stage_refs[1], f, t, masks)
    down_s = Scatter(links, g_down, down_place, sub, (None,), *stage_refs[2], f, t, masks)
    up_s = Scatter(links, g_up, same, feat, (0, 1), *stage_refs[3], f, t, masks)

    def exchange_columns(job, dst):
        total = job.sums[-1]
        c = links.copy(block(total, 1 - mid, feat), dst.at[mid], mid_peer)
        c.start()
        k = pltpu.make_async_copy(block(total, mid, feat), dst.at[mid], local_sem.at[0 if job is qkv_s else 1])
        k.start()
        return c, k

    class Tokens:
        def __init__(self, part, refs):
            self.part, (self.got, self.sum, self.got_y, self.final) = part, refs
            self.copies = {}

        def start(self):
            for y in (1, 0):
                for m in (1, 0):
                    yy, mm = (1 - t // 2 if y else t // 2), (1 - mid if m else mid)
                    c = links.copy(
                        block(self.part, mm * 4 + yy * 2 + 1 - t % 2, rows),
                        block(self.got, mm * 2 + yy, rows),
                        core_peer,
                    )
                    c.start()
                    self.copies["c", y, m] = c

        def core(self):
            for y in (1, 0):
                for m in (1, 0):
                    yy, mm = (1 - t // 2 if y else t // 2), (1 - mid if m else mid)
                    self.copies["c", y, m].wait_recv()
                    total = block(self.sum, mm * 2 + yy, rows)
                    run_add(block(self.part, mm * 4 + yy * 2 + t % 2, rows), block(self.got, mm * 2 + yy, rows), total)
                    if y:
                        c = links.copy(total, block(self.got_y, mm, rows), y_peer)
                        c.start()
                        self.copies["y", m] = c

        def across(self):
            self.copies["y", 1].wait_recv()
            self.copies["y", 1].wait_send()
            total = block(self.sum, (1 - mid) * 2 + 1 - t // 2, rows)
            run_add(block(self.sum, (1 - mid) * 2 + t // 2, rows), block(self.got_y, 1 - mid, rows), total)
            self.copies["m"] = links.copy(total, self.final.at[1], mid_peer)
            self.copies["m"].start()
            self.copies["y", 0].wait_recv()
            run_add(block(self.sum, mid * 2 + t // 2, rows), block(self.got_y, mid, rows), self.final.at[0])

        def finish(self):
            self.copies["m"].wait_recv()

        def drain(self):
            for key, c in self.copies.items():
                if key != ("y", 1):
                    c.wait_send()

    norm_t = Tokens(norm_grad, token_refs[0])
    branch_t = Tokens(branch, token_refs[1])

    qkv_s.start()
    out_s.start()
    down_s.start()
    run_hidden_grad(ea, downa, slope, dh, bias_sum)
    qkv_s.level(0)
    out_s.level(0)
    run_outer(n2, dh, g_up)
    up_s.start()
    run_norm_grad(vec, dh, upa, dproj, qkva, xa, norm_grad, sums, qkv_sum)
    norm_t.start()
    down_s.level(0)
    run_branch(a, outa, g, downa, branch)
    norm_t.core()
    branch_t.start()
    small[...] = jnp.zeros_like(small)
    small[0:4, :] = sums[0:4, :]
    small[4:5, :] = jnp.sum(e[...].astype(f32), axis=0, keepdims=True)
    n_heads = d // HD
    for c in range(3):
        for h in range(n_heads):
            small[5 + c : 6 + c, h * HD : (h + 1) * HD] = jnp.where(
                t * 2 + mid == h, qkv_sum[0:1, c * HD : (c + 1) * HD], 0.0
            )
    hi_n = fsdp // 4
    chunk = 2 * sub
    for tt in range(4):
        for hh in range(hi_n):
            for mm in range(2):
                at = (hh * 2 + mm) * chunk
                small[8 + tt : 9 + tt, at : at + chunk] = jnp.where(
                    (t == tt) & (mid == mm), bias_sum[0:1, hh * chunk : (hh + 1) * chunk], 0.0
                )
    small_peers = [core_peer, y_peer, mid_peer] + [(flip(f, m), t) for m in masks]
    small_copies = []

    def small_round(r):
        c = links.copy(small, small_in.at[r], small_peers[r])
        c.start()
        small_copies.append(c)

    def small_add(r):
        small_copies[r].wait()
        small[...] += small_in[r]

    small_round(0)
    branch_t.core()
    small_add(0)
    small_round(1)
    qkv_s.level(1)
    qkv_x = exchange_columns(qkv_s, qkv_new) if n_stage == 2 else None
    small_add(1)
    small_round(2)
    norm_t.across()
    small_add(2)
    small_round(3)
    out_s.level(1)
    down_s.level(1)
    for r in range(3, len(small_peers)):
        small_add(r)
        if r + 1 < len(small_peers):
            small_round(r + 1)
    branch_t.across()
    for level in range(2, n_stage):
        qkv_s.level(level)
        out_s.level(level)
        down_s.level(level)
    if qkv_x is None:
        qkv_x = exchange_columns(qkv_s, qkv_new)
    total = out_s.sums[-1]
    swap_copy = links.copy(total, out_new, (swapped, t))
    own_out = pltpu.make_async_copy(total, out_new, local_sem.at[2])

    @pl.when(swapped != f)
    def _():
        swap_copy.start()

    @pl.when(swapped == f)
    def _():
        own_out.start()

    for level in range(n_stage):
        up_s.level(level)
    up_x = exchange_columns(up_s, up_new)
    norm_t.finish()
    branch_t.finish()
    for c, k in (qkv_x, up_x):
        c.wait_recv()
        c.wait_send()
        k.wait()

    @pl.when(swapped != f)
    def _():
        swap_copy.wait_recv()
        swap_copy.wait_send()

    @pl.when(swapped == f)
    def _():
        own_out.wait()

    for job in (qkv_s, out_s, down_s, up_s):
        for c in job.copies.values():
            c.wait_send()
    norm_t.drain()
    branch_t.drain()


def scatter_all(masks, top, tp, e, vec, x, ea, xa, upa, qkva, downa, outa, n2, a, dproj, g_qkv, g_out, g, slope, g_down):
    rows, d = x.shape
    tokens = 2 * tp * rows
    mine, wide = upa.shape[1], qkva.shape[1]
    fsdp = 2 << len(masks)
    feat, sub, orow = d // fsdp, 2 * mine // fsdp, 2 * HD // fsdp
    hi_n = fsdp // 4
    shapes = [(tokens, mine), (d, mine), (tokens, d), (tokens, d)]
    copies = 0
    for height, width, mids in ((feat, wide, 2), (orow, d, 1), (sub, d, 1), (feat, mine, 2)):
        for _ in range(2):
            for level in range(len(masks)):
                n = max(hi_n >> level, 1)
                shapes.append((n * mids * height, width))
        copies += (2 * hi_n - 1) * mids + 1
    for _ in range(2):
        shapes += [(4 * rows, d), (4 * rows, d), (2 * rows, d), (2, rows, d)]
        copies += 7
    shapes += [(2, feat, mine), (2, feat, wide), (orow, d)]
    n_small = len(masks) + 3
    out_shape = [jax.ShapeDtypeStruct(shape, bf16) for shape in shapes]
    out_shape.append(jax.ShapeDtypeStruct((16, d), f32))
    result = pl.pallas_call(
        functools.partial(scatter_kernel, masks, top),
        out_shape=out_shape,
        in_specs=[VMEM, VMEM] + [ANY] * 15,
        out_specs=[ANY] * len(shapes) + [VMEM],
        scratch_shapes=[
            pltpu.SemaphoreType.DMA((copies + n_small,)),
            pltpu.SemaphoreType.DMA((copies + n_small,)),
            pltpu.SemaphoreType.DMA((3,)),
            pltpu.VMEM((8, d), f32),
            pltpu.VMEM((8, wide), f32),
            pltpu.VMEM((8, mine), f32),
            pltpu.VMEM((n_small, 16, d), f32),
        ],
        compiler_params=pltpu.CompilerParams(
            collective_id=1, has_side_effects=True, vmem_limit_bytes=56 * 2**20
        ),
        name="scatter_all",
    )(e, vec, x, ea, xa, upa, qkva, downa, outa, n2, a, dproj, g_qkv, g_out, g, slope, g_down)
    stage = len(masks)
    down_new = result[4 + 2 * stage * 3 - 1]
    at = 4 + 2 * stage * 4
    norm_final, branch_final = result[at + 3], result[at + 7]
    up_new, qkv_new, out_new, small = result[at + 8 : at + 12]
    return norm_final, branch_final, up_new, qkv_new, out_new, down_new, small


def make_local(fsdp, tp):
    lo_n = 2
    hi_n = fsdp // 4
    masks = [1 << b for b in range(2, fsdp.bit_length() - 1)] + [1]
    top = fsdp // 2

    def local(
        layer_input,
        out_cotangent,
        segments,
        qkv_weight,
        qkv_first,
        qkv_second,
        out_weight,
        out_first,
        out_second,
        up_weight,
        up_first,
        up_second,
        down_weight,
        down_first,
        down_second,
        small_params,
        small_first,
        small_second,
    ):
        f = lax.axis_index("fsdp")
        t = lax.axis_index("tp")
        mid = (f // 2) % 2
        rows, d = layer_input.shape
        length = segments.shape[1]
        width = qkv_weight.shape[3]
        hidden = up_weight.shape[2]
        sub = hidden // fsdp
        feat = d // fsdp
        mine = hidden // 2
        vector = small_params[0]

        up16 = up_weight[0].astype(bf16).reshape(feat, hi_n, 2, lo_n * sub)
        up16 = up16.transpose(2, 0, 1, 3).reshape(2, feat, mine)
        qkv16 = qkv_weight[0].astype(bf16).reshape(3, feat, 2, HD)
        qkv16 = qkv16.transpose(2, 1, 0, 3).reshape(2, feat, 3 * HD)
        down16 = down_weight[0].astype(bf16)
        out16 = out_weight[0].astype(bf16)

        own_bounds = jnp.stack([jnp.sum(segments[0] < 1), jnp.sum(segments[0] < 2)]).astype(f32)
        other_bounds = lax.ppermute(own_bounds, "fsdp", [(i, i ^ 2) for i in range(fsdp)])
        bounds = jnp.where(
            mid == 0, jnp.stack([own_bounds, other_bounds]), jnp.stack([other_bounds, own_bounds])
        ).astype(jnp.int32)
        index = jnp.arange(length, dtype=jnp.int32)[None]
        first, second = bounds[:, 0:1], bounds[:, 1:2]
        start = jnp.where(index >= second, second, jnp.where(index >= first, first, 0))
        position = (index - start).astype(f32).reshape(2 * length, 1)
        half = ROT // 2
        lane = jnp.arange(128)
        frequency = 10000.0 ** (-(2 * (lane % half)).astype(f32) / ROT)
        angle = position * frequency[None]
        cosine = jnp.where(lane < ROT, jnp.cos(angle), 1.0)
        sine = jnp.where(lane < ROT, jnp.where(lane < half, -1.0, 1.0) * jnp.sin(angle), 0.0)

        norms = vector[0 : 4 * d].reshape(4, d)
        vec = jnp.concatenate([norms, jnp.zeros((4, d), f32)])
        qkv_bias = lax.dynamic_slice_in_dim(
            vector[6 * d : 9 * d].reshape(3, d), t * width + mid * HD, HD, 1
        ).reshape(1, 3 * HD)
        up_bias = lax.dynamic_slice(
            vector[9 * d :].reshape(tp, hi_n, 2, lo_n * sub), (t, 0, mid, 0), (1, hi_n, 1, lo_n * sub)
        ).reshape(1, mine)

        (
            x_all, e_all, up_full, qkv_full, down_full, out_full,
            n1, n2, p, da, a, dproj, g_qkv, g_out, g, slope, g_down,
        ) = gather_all(
            masks, top, length, tp, layer_input, out_cotangent, up16, qkv16, down16, out16,
            cosine, sine, vec, qkv_bias, up_bias, bounds,
        )
        norm_final, branch_final, up_new, qkv_new, out_new, down_new, small = scatter_all(
            masks, top, tp, out_cotangent, vec, layer_input, e_all, x_all, up_full, qkv_full, down_full,
            out_full, n2, a, dproj, g_qkv, g_out, g, slope, g_down,
        )

        stream = layer_input.astype(f32)
        bias = vector[4 * d : 5 * d] + vector[5 * d : 6 * d]
        layer_output = stream + (branch_final[0].astype(f32) + branch_final[1].astype(f32)) + bias
        scaled = norm_final[0].astype(f32) + norm_final[1].astype(f32)
        centred = stream - jnp.mean(stream, axis=-1, keepdims=True)
        inverse = lax.rsqrt(jnp.mean(centred * centred, axis=-1, keepdims=True) + norm_eps)
        normal = centred * inverse
        input_grad = out_cotangent.astype(f32) + inverse * (
            scaled
            - jnp.mean(scaled, axis=-1, keepdims=True)
            - normal * jnp.mean(scaled * normal, axis=-1, keepdims=True)
        )
        qkv_total = qkv_new.reshape(2, feat, 3, HD).transpose(2, 1, 0, 3).reshape(1, 3, feat, width)
        up_total = up_new.reshape(2, feat, hi_n, lo_n * sub).transpose(1, 2, 0, 3).reshape(1, feat, hidden)
        small_total = jnp.concatenate(
            [small[0:5].reshape(-1), small[4:5].reshape(-1), small[5:12].reshape(-1)]
        )[None]
        rate_matrix = d ** (-0.5)
        rate_output = 4.0 * d ** (-0.5)
        results = [layer_output, input_grad]
        for weight, first, second, grad, rate, decay in (
            (qkv_weight, qkv_first, qkv_second, qkv_total, rate_matrix, decay_rate),
            (out_weight, out_first, out_second, out_new[None], rate_output, decay_rate),
            (up_weight, up_first, up_second, up_total, rate_matrix, decay_rate),
            (down_weight, down_first, down_second, down_new[None], rate_matrix, decay_rate),
            (small_params, small_first, small_second, small_total, rate_vector, 0.0),
        ):
            results.extend(adam_step(weight, first, second, grad.astype(f32), rate, decay))
        return tuple(results)

    return local


def solution(mesh):
    tokens = P(("fsdp", "tp"), None)
    inner = P(None, ("tp", "fsdp"), None)
    qkv = P(None, None, "fsdp", "tp")
    up = P(None, "fsdp", "tp")
    weights = (qkv,) * 3 + (inner,) * 3 + (up,) * 3 + (inner,) * 3 + (P(),) * 3
    return jax.shard_map(
        make_local(mesh.shape["fsdp"], mesh.shape["tp"]),
        mesh=mesh,
        in_specs=(tokens, tokens, P("fsdp", None)) + weights,
        out_specs=(tokens, tokens) + weights,
        check_vma=False,
    )
```

```python
import functools

import jax
import jax.numpy as jnp
from jax import lax
from jax.experimental import pallas as pl
from jax.experimental.pallas import tpu as pltpu
from jax.sharding import PartitionSpec as P

HD = 256
ROT = 64
STEP = 10

norm_eps = 1e-05
beta_one = 0.9
beta_two = 0.95
adam_eps = 1e-08
decay_rate = 0.01
rate_vector = 0.2
masked_score = -1e30
f32 = jnp.float32
bf16 = jnp.bfloat16


def adam_step(weight, first, second, grad, rate, decay):
    first_new = beta_one * first + (1.0 - beta_one) * grad
    second_new = beta_two * second + (1.0 - beta_two) * grad * grad
    first_hat = first_new / (1.0 - beta_one**STEP)
    second_hat = second_new / (1.0 - beta_two**STEP)
    weight_new = weight - rate * (first_hat / (jnp.sqrt(second_hat) + adam_eps) + decay * weight)
    return (first_new, second_new, weight_new)


MESH = pl.DeviceIdType.MESH


def bit_of(i, mask):
    return (i // mask) % 2


def flip(i, mask):
    return i + mask - 2 * mask * bit_of(i, mask)


class Links:
    def __init__(self, send_sem, recv_sem):
        self.send_sem, self.recv_sem, self.count, self.started = send_sem, recv_sem, 0, []

    def copy(self, src, dst, device):
        k = self.count
        self.count += 1
        c = pltpu.make_async_remote_copy(
            src_ref=src,
            dst_ref=dst,
            send_sem=self.send_sem.at[k],
            recv_sem=self.recv_sem.at[k],
            device_id=device,
            device_id_type=MESH,
        )
        self.started.append(c)
        return c


class Group:
    def __init__(self, links, at, f, t, masks, root, own=None):
        self.copies, self.masks = {}, masks
        for key in all_keys(masks):
            g = root
            for mask in masks:
                if key & mask:
                    g = flip(g, mask)
            ref = at(g)
            for mask in self.later(key):
                src = own if key == 0 and own is not None else ref
                self.copies[key | mask] = links.copy(src, ref, (flip(f, mask), t))

    def later(self, key):
        after = max([i + 1 for i, m in enumerate(self.masks) if key & m], default=0)
        return self.masks[after:]

    def send(self, key, mask):
        self.copies[key | mask].start()

    def send_all(self, key):
        for mask in self.later(key):
            self.send(key, mask)

    def wait(self, key):
        self.copies[key].wait_recv()

    def arrive(self, key):
        self.wait(key)
        self.send_all(key)


def all_keys(masks):
    keys = [0]
    for mask in masks:
        keys = keys + [k | mask for k in keys]
    return keys


def normalise(x):
    mean = jnp.mean(x, axis=-1, keepdims=True)
    centred = x - mean
    inverse = lax.rsqrt(jnp.mean(centred * centred, axis=-1, keepdims=True) + norm_eps)
    return centred * inverse


def rope(u, c, s):
    lane = lax.broadcasted_iota(jnp.int32, u.shape, 1)
    partner = jnp.where(lane < ROT // 2, pltpu.roll(u, 128 - ROT // 2, 1), pltpu.roll(u, ROT // 2, 1))
    return u * c + partner * s


def dot(a, b, dims):
    return lax.dot_general(a, b, (dims, ((), ())), preferred_element_type=f32)


NN = ((1,), (0,))
NT = ((1,), (1,))
TN = ((0,), (0,))
TILE = 256


def pipe(body, steps, ins, outs, hooks=()):
    hooks = list(hooks)

    def whole(*refs):
        for i, hook in enumerate(hooks):
            pl.when(pl.program_id(0) == i * steps // len(hooks))(hook)
        body(*refs)

    pltpu.emit_pipeline(
        whole,
        grid=(steps,),
        in_specs=[spec for _, spec in ins],
        out_specs=[spec for _, spec in outs],
    )(*[ref for ref, _ in ins], *[ref for ref, _ in outs])


def by_rows(ref, index=lambda i: i, rows=TILE):
    return ref, pl.BlockSpec((rows, ref.shape[1]), lambda i: (index(i), 0))


def by_columns(ref, index, width):
    return ref, pl.BlockSpec((ref.shape[0], width), lambda i: (0, index(i)))


def here(i, rows=TILE):
    return pl.ds(pl.multiple_of(i * rows, rows), rows)


def run_norms(vec, x, n1, n2, index, steps, hooks=()):
    def body(x_ref, one_ref, two_ref):
        normal = normalise(x_ref[...].astype(f32))
        one_ref[...] = (normal * vec[0:1, :] + vec[1:2, :]).astype(bf16)
        two_ref[...] = (normal * vec[2:3, :] + vec[3:4, :]).astype(bf16)

    pipe(body, steps, [by_rows(x, index)], [by_rows(n1, index), by_rows(n2, index)], hooks)


def run_project(qkv_bias, n1, w, c, s, p, hooks=()):
    def body(n_ref, c_ref, s_ref):
        at = here(pl.program_id(0))
        proj = dot(n_ref[...], w[...], NN) + qkv_bias[...]
        for j in range(2):
            p[at, j * HD : j * HD + 128] = rope(proj[:, j * HD : j * HD + 128], c_ref[...], s_ref[...]).astype(bf16)
            p[at, j * HD + 128 : (j + 1) * HD] = proj[:, j * HD + 128 : (j + 1) * HD].astype(bf16)
        p[at, 2 * HD :] = proj[:, 2 * HD :].astype(bf16)

    pipe(body, n1.shape[0] // TILE, [by_rows(n1), by_rows(c), by_rows(s)], [], hooks)


def run_up(up_bias, n2, w, g, slope, hooks=()):
    width = w.shape[1]
    part = min(width, 256)

    def body(n_ref, g_ref, s_ref):
        n = n_ref[...]
        for j in range(0, width, part):
            h = dot(n, w[:, j : j + part], NN) + up_bias[:, j : j + part]
            cdf = 0.5 + 0.5 * lax.erf(h * 0.7071067811865476)
            g_ref[:, j : j + part] = (h * cdf).astype(bf16)
            s_ref[:, j : j + part] = (cdf + h * (jnp.exp(-0.5 * h * h) * 0.3989422804014327)).astype(bf16)

    pipe(body, n2.shape[0] // TILE, [by_rows(n2)], [by_rows(g), by_rows(slope)], hooks)


def run_attention(length, seq, bounds, p, da, c, s, a, dproj, dk, dv):
    scale = HD ** (-0.5)
    base = seq * length
    first, second = bounds[seq, 0], bounds[seq, 1]

    def put(at, value, column):
        dproj[at, column : column + 128] = rope(value[:, :128], c[at, :], -s[at, :]).astype(bf16)
        dproj[at, column + 128 : column + HD] = value[:, 128:].astype(bf16)

    dk[...] = jnp.zeros_like(dk)
    dv[...] = jnp.zeros_like(dv)
    for i in range(length // TILE):
        at = slice(base + i * TILE, base + (i + 1) * TILE)
        n = (i + 1) * TILE
        q = p[at, 0:HD]
        k = p[base : base + n, HD : 2 * HD]
        v = p[base : base + n, 2 * HD :]
        rows_da = da[at, :]
        scores = dot(q, k, NT) * scale
        qi = i * TILE + lax.broadcasted_iota(jnp.int32, (TILE, n), 0)
        ki = lax.broadcasted_iota(jnp.int32, (TILE, n), 1)
        start = jnp.where(qi >= second, second, jnp.where(qi >= first, first, 0))
        scores = jnp.where((ki <= qi) & (ki >= start), scores, masked_score)
        peak = jnp.max(scores, axis=-1, keepdims=True)
        raised = jnp.exp(scores - peak)
        probs = raised * (1.0 / jnp.sum(raised, axis=-1, keepdims=True))
        weights = probs.astype(bf16)
        a[at, :] = dot(weights, v, NN).astype(bf16)
        prob_grad = dot(rows_da, v, NT)
        delta = jnp.sum(probs * prob_grad, axis=-1, keepdims=True)
        score_grad = (probs * (prob_grad - delta)).astype(bf16)
        put(at, dot(score_grad, k, NN) * scale, 0)
        dk[0:n, :] += dot(score_grad, q, TN)
        dv[0:n, :] += dot(weights, rows_da, TN)
    for i in range(length // TILE):
        at = slice(base + i * TILE, base + (i + 1) * TILE)
        local = slice(i * TILE, (i + 1) * TILE)
        put(at, dk[local, :] * scale, HD)
        dproj[at, 2 * HD :] = dv[local, :].astype(bf16)


def run_outer(a, b, out, index_in, index_out, steps, width, add=None, hooks=()):
    def body(*refs):
        value = dot(refs[0][...], b[...], TN)
        if add is not None:
            value = value + refs[1][...].astype(f32)
        refs[-1][...] = value.astype(bf16)

    ins = [by_columns(a, index_in, width)]
    if add is not None:
        ins.append(by_rows(add, index_out, width))
    pipe(body, steps, ins, [by_rows(out, index_out, width)], hooks)


def run_outer_wide(a, b, out):
    width = 2 * TILE

    def body(out_ref):
        at = pl.ds(pl.multiple_of(pl.program_id(0) * width, width), width)
        out_ref[...] = dot(a[...], b[:, at], TN).astype(bf16)

    pipe(body, b.shape[1] // width, [], [by_columns(out, lambda i: i, width)])


def run_hidden_grad(e, w, slope, dh, bias_sum, hooks=()):
    bias_sum[...] = jnp.zeros_like(bias_sum)

    def body(s_ref):
        at = here(pl.program_id(0))
        value = (dot(e[at, :], w[...], NT) * s_ref[...].astype(f32)).astype(bf16)
        dh[at, :] = value
        bias_sum[0:1, :] += jnp.sum(value.astype(f32), axis=0, keepdims=True)

    pipe(body, e.shape[0] // TILE, [by_rows(slope)], [], hooks)


def run_norm_grad(vec, dh, w_up, dproj, w_qkv, x, sums, qkv_sum):
    sums[...] = jnp.zeros_like(sums)
    qkv_sum[...] = jnp.zeros_like(qkv_sum)

    def tile(at, x_ref):
        normal = normalise(x_ref[...].astype(f32))
        rows = dproj[at, :]
        one = dot(rows, w_qkv[...], NT)
        two = dot(dh[at, :], w_up[...], NT)
        for j, value in ((0, one * normal), (1, one), (2, two * normal), (3, two)):
            sums[j : j + 1, :] += jnp.sum(value, axis=0, keepdims=True)
        qkv_sum[0:1, :] += jnp.sum(rows.astype(f32), axis=0, keepdims=True)
        return one * vec[0:1, :] + two * vec[2:3, :]

    return x, tile


def run_branch(a, w_out, g, w_down):
    def tile(at, g_ref):
        return dot(a[at, :], w_out[...], NN) + dot(g_ref[...], w_down[...], NN)

    return g, tile


def run_token_tiles(job, out, index, index_out, steps, add=None, hooks=()):
    source, tile = job

    def body(*refs):
        value = tile(here(index(pl.program_id(0))), refs[0])
        if add is not None:
            value = value + refs[1][...].astype(f32)
        refs[-1][...] = value.astype(bf16)

    ins = [by_rows(source, index)]
    if add is not None:
        ins.append(by_rows(add, index_out))
    pipe(body, steps, ins, [by_rows(out, index_out)], hooks)


def run_add(a, b, out):
    rows, cols = out.shape
    step = min(rows, TILE)

    def body(a_ref, b_ref, out_ref):
        out_ref[...] = (a_ref[...].astype(f32) + b_ref[...].astype(f32)).astype(bf16)

    pipe(body, rows // step, [by_rows(a, rows=step), by_rows(b, rows=step)], [by_rows(out, rows=step)])


def block(ref, index, rows):
    return ref.at[pl.ds(pl.multiple_of(index * rows, rows), rows)]


def out_place(g, top):
    return (((g // 4) % (top // 4)) * 2 + g // top) * 2 + g % 2


class Scatter:
    def __init__(self, links, part, place, rows, mids, recv, sums, f, t, masks):
        self.links, self.part, self.place, self.rows, self.mids = links, part, place, rows, mids
        self.recv, self.sums, self.f, self.t = recv, sums, f, t
        self.stages = [1] + [m for m in reversed(masks) if m != 1]
        self.n_hi = 1 << (len(masks) - 1)
        self.hi, self.lo, self.mid = f // 4, f % 2, bit_of(f, 2)
        self.copies = {}
        for k in range(self.n_hi):
            for j, m in enumerate(mids):
                self.copies[0, k, j] = links.copy(
                    block(part, self.at_place(self.high(k), m, 1 - self.lo), rows),
                    block(recv[0], self.slot(0, k, j), rows),
                    (flip(f, 1), t),
                )
        for level in range(len(self.stages) - 1):
            n = self.n_hi >> (level + 1)
            for k in range(n, 2 * n):
                for j in range(len(mids)):
                    self.copies[level + 1, k - n, j] = links.copy(
                        block(sums[level], self.slot(level, k, j), rows),
                        block(recv[level + 1], self.slot(level + 1, k, j), rows),
                        (flip(f, self.stages[level + 1]), t),
                    )

    def high(self, k):
        hi, b = self.hi, 1
        while b < self.n_hi:
            if k & b:
                hi = flip(hi, b)
            b *= 2
        return hi

    def slot(self, level, k, j):
        n = self.n_hi >> level
        i = (self.high(k) % n) if n > 1 else 0
        return i * len(self.mids) + j

    def at_place(self, hi, m, lo):
        return self.place((hi * 2 + (self.mid if m is None else m)) * 2 + lo)

    def ks(self, far):
        half = self.n_hi // 2
        return range(half, self.n_hi) if far else range(half)

    def each(self, far):
        return [(k, j) for k in self.ks(far) for j in range(len(self.mids))]

    def send(self, far):
        for k, j in self.each(far):
            self.copies[0, k, j].start()

    def got(self, far):
        for k, j in self.each(far):
            self.copies[0, k, j].wait_recv()

    def send_on(self):
        half = self.n_hi // 2
        for k, j in self.each(True):
            self.copies[1, k - half, j].start()

    def tile(self, i, far, lo):
        n = len(self.mids)
        half = self.n_hi // 2
        upper = self.hi // half
        hi = (1 - upper if far else upper) * half + i // n
        j = i % n
        m = None if self.mids[0] is None else j
        return self.at_place(hi, m, lo), hi * n + j

    def add(self, level, k, j):
        mine = (
            block(self.part, self.at_place(self.high(k), self.mids[j], self.lo), self.rows)
            if level == 0
            else block(self.sums[level - 1], self.slot(level - 1, k, j), self.rows)
        )
        at = self.slot(level, k, j)
        run_add(mine, block(self.recv[level], at, self.rows), block(self.sums[level], at, self.rows))

    def first_adds(self, far):
        for k, j in self.each(far):
            self.add(0, k, j)

    def finish(self):
        for level in range(1, len(self.stages)):
            n = self.n_hi >> level
            for k in reversed(range(n)):
                for j in range(len(self.mids)):
                    self.copies[level, k, j].wait_recv()
                    self.add(level, k, j)
                    if level + 1 < len(self.stages) and k & (n // 2):
                        self.copies[level + 1, k - n // 2, j].start()


class Outer:
    def __init__(self, scatter, a, b):
        self.s, self.a, self.b = scatter, a, b
        self.fused = scatter.rows % 128 == 0
        self.steps = scatter.n_hi // 2 * len(scatter.mids)

    def give(self, far, hooks=()):
        s = self.s
        if self.fused:
            at = lambda i: s.tile(i, far, 1 - s.lo)[0]
            run_outer(self.a, self.b, s.part, at, at, self.steps, s.rows, hooks=hooks)
        elif far:
            run_outer(self.a, self.b, s.part, lambda i: i, lambda i: i, self.a.shape[1] // 128, 128, hooks=hooks)

    def keep(self, far, hooks=()):
        s = self.s
        s.got(far)
        if self.fused:
            at = lambda i: s.tile(i, far, s.lo)[0]
            to = lambda i: s.tile(i, far, s.lo)[1]
            run_outer(self.a, self.b, s.sums[0], at, to, self.steps, s.rows, add=s.recv[0], hooks=hooks)
        else:
            for hook in hooks:
                hook()
            s.first_adds(far)


class Tokens:
    def __init__(self, links, refs, rows, f, t):
        self.give_buf, self.got, self.sum, self.got_y, self.sum_y, self.final = refs
        self.rows, self.mid, self.y, self.core = rows, bit_of(f, 2), t // 2, t % 2
        core_peer, y_peer, mid_peer = (f, flip(t, 1)), (f, flip(t, 2)), (flip(f, 2), t)
        self.copies = {}
        for i in range(4):
            self.copies["c", i] = links.copy(block(self.give_buf, i, rows), block(self.got, i, rows), core_peer)
        for m in range(2):
            self.copies["y", m] = links.copy(
                block(self.sum, m * 2 + 1 - self.y, rows), block(self.got_y, m, rows), y_peer
            )
        self.copies["m"] = links.copy(block(self.sum_y, 1 - self.mid, rows), self.final.at[1], mid_peer)

    def give(self, job, hooks=()):
        index = lambda i: (i // 2) * 4 + (i % 2) * 2 + 1 - self.core
        run_token_tiles(job, self.give_buf, index, lambda i: i, 4, hooks=hooks)
        for i in range(4):
            self.copies["c", i].start()

    def keep(self, job, far, hooks=()):
        yy = 1 - self.y if far else self.y
        index = lambda i: i * 4 + yy * 2 + self.core
        if far:
            for i in range(4):
                self.copies["c", i].wait_recv()
        run_token_tiles(job, self.sum, index, lambda i: i * 2 + yy, 2, add=self.got, hooks=hooks)
        if far:
            for m in range(2):
                self.copies["y", m].start()

    def across(self):
        for m in range(2):
            self.copies["y", m].wait_recv()
        for m, to, send in (
            (1 - self.mid, block(self.sum_y, 1 - self.mid, self.rows), True),
            (self.mid, self.final.at[0], False),
        ):
            run_add(block(self.sum, m * 2 + self.y, self.rows), block(self.got_y, m, self.rows), to)
            if send:
                self.copies["m"].start()

    def finish(self):
        self.copies["m"].wait_recv()


def greet(f, t, masks, top):
    mid = bit_of(f, 2)
    swapped = f + (top - 2) * (mid - bit_of(f, top))
    barrier = pltpu.get_barrier_semaphore()
    peers = [(flip(f, m), t) for m in masks + [2]] + [(f, flip(t, 1)), (f, flip(t, 2))]
    for peer in peers:
        pl.semaphore_signal(barrier, inc=1, device_id=peer, device_id_type=MESH)

    @pl.when(swapped != f)
    def _():
        pl.semaphore_signal(barrier, inc=1, device_id=(swapped, t), device_id_type=MESH)

    pl.semaphore_wait(barrier, len(peers) + (mid + bit_of(f, top)) % 2)
    return swapped


class Swap:
    def __init__(self, links, src, dst, stay, f, t, swapped, sem):
        self.move = links.copy(src, dst, (swapped, t))
        links.started = [c for c in links.started if c is not self.move]
        self.copy = pltpu.make_async_copy(src, stay, sem)
        self.moves, self.stays = swapped != f, swapped == f

    def start(self):
        pl.when(self.moves)(self.move.start)
        pl.when(self.stays)(self.copy.start)

    def wait(self):
        pl.when(self.moves)(self.move.wait_recv)
        pl.when(self.stays)(self.copy.wait)

    def drain(self):
        pl.when(self.moves)(self.move.wait_send)


N_HBM = 9


def layer_kernel(
    masks, top, length,
    x, e, up, qkv, down, out, cos, sin, e_own, vec, qkv_bias, up_bias, bounds,
    *rest,
):
    n_stage = len(masks)
    (xa, n1, n2, g, slope, g_qkv, g_out, g_down, g_up), rest = rest[:N_HBM], rest[N_HBM:]
    stage_refs = []
    for _ in range(4):
        stage_refs.append((rest[:n_stage], rest[n_stage : 2 * n_stage]))
        rest = rest[2 * n_stage :]
    token_refs, rest = [rest[:6], rest[6:12]], rest[12:]
    (up_new, qkv_new, out_new, small), rest = rest[:4], rest[4:]
    (
        ea, upa, qkva, downa, outa, p, da, a, dproj, dh, dk, dv, sums, qkv_sum, bias_sum, small_in,
        send_sem, recv_sem, local_sem,
    ) = rest
    f = lax.axis_index("fsdp")
    t = lax.axis_index("tp")
    mid = bit_of(f, 2)
    rows, d = x.shape
    feat, sub, orow = up.shape[1], down.shape[0], out.shape[0]
    mine = up.shape[2]
    swapped = greet(f, t, masks, top)
    links = Links(send_sem, recv_sem)
    own = []

    def local_copy(src, dst):
        c = pltpu.make_async_copy(src, dst, local_sem.at[len(own)])
        own.append(c)
        return c

    mid_peer, y_peer, core_peer = (flip(f, 2), t), (f, flip(t, 2)), (f, flip(t, 1))
    qkv_block = lambda i: block(qkva, i, feat)
    up_block = lambda i: block(upa, i, feat)
    half_sub = sub // 2
    down_blocks = [
        lambda i, h=h: block(downa, ((i // 4) * 2 + i % 2) * 2 + h, half_sub) for h in range(2)
    ]
    out_block = lambda i: block(outa, out_place(i, top), orow)
    tok = lambda buf, m, j: block(buf, m * 4 + j, rows)

    first_up = links.copy(up.at[1 - mid], up_block(f), mid_peer)
    first_qkv = links.copy(qkv.at[1 - mid], qkv_block(f), mid_peer)
    up_own = Group(links, up_block, f, t, masks, f, up.at[mid])
    up_mid = Group(links, up_block, f, t, masks, flip(f, 2))
    qkv_own = Group(links, qkv_block, f, t, masks, f, qkv.at[mid])
    qkv_mid = Group(links, qkv_block, f, t, masks, flip(f, 2))
    out_own = Group(links, out_block, f, t, masks, f)
    down_own = [
        Group(links, down_blocks[h], f, t, masks, f, down.at[pl.ds(h * half_sub, half_sub)]) for h in range(2)
    ]
    out_in = Swap(links, out, out_block(swapped), out_block(f), f, t, swapped, local_sem.at[6])

    def tokens(source, buf):
        c = {}
        for name, m, j, peer in (
            ("m", mid, t, mid_peer), ("y", mid, t, y_peer), ("c", mid, t, core_peer),
            ("my", 1 - mid, t, y_peer), ("mc", 1 - mid, t, core_peer),
            ("yc", mid, flip(t, 2), core_peer), ("myc", 1 - mid, flip(t, 2), core_peer),
        ):
            ref = tok(buf, m, j)
            c[name] = links.copy(source if len(name) == 1 else ref, ref, peer)
        return c

    xs = tokens(x, xa)
    es = tokens(e, ea)
    own_x = local_copy(x, tok(xa, mid, t))
    own_e = local_copy(e, tok(ea, mid, t))
    own_up = local_copy(up.at[mid], up_block(f))
    own_qkv = local_copy(qkv.at[mid], qkv_block(f))
    own_down = local_copy(down, block(downa, (f // 4) * 2 + f % 2, sub))

    def then(wait, *starts):
        def run():
            wait()
            for start in starts:
                start()

        return run

    def arrived(c, *starts):
        return then(c.wait_recv, *[s.start for s in starts])

    keys = all_keys(masks)[1:]
    inner = [k for k in keys if not k & 1]

    def passes(group):
        return [functools.partial(group.arrive, k) for k in inner]

    def ends(groups):
        for group in groups:
            for k in keys:
                if k & 1:
                    group.wait(k)

    first_up.start()
    up_own.send_all(0)
    xs["y"].start()
    xs["c"].start()
    out_in.start()
    for c in own:
        c.start()
    own_x.wait()
    then(first_up.wait_recv, functools.partial(up_mid.send_all, 0), xs["m"].start)()
    arrived(xs["y"], xs["yc"], es["y"], es["c"])()
    for hook in passes(up_own):
        hook()
    qkv_own.send_all(0)
    arrived(xs["m"], xs["my"], xs["mc"], first_qkv)()
    xs["c"].wait_recv()
    xs["yc"].wait_recv()
    run_norms(vec, xa, n1, n2, lambda i: mid * 4 + i, 4)
    out_in.wait()
    out_own.send(0, 1)
    for hook in passes(up_mid):
        hook()
    then(first_qkv.wait_recv, functools.partial(qkv_mid.send_all, 0), es["m"].start)()
    arrived(xs["my"], xs["myc"])()
    xs["mc"].wait_recv()
    xs["myc"].wait_recv()
    run_norms(vec, xa, n1, n2, lambda i: (1 - mid) * 4 + i, 4)
    ends([up_own, up_mid])
    own_up.wait()
    hooks = [arrived(es["y"], es["yc"])] + passes(qkv_own)

    def out_and_down():
        for mask in masks[:-1]:
            out_own.send(0, mask)
        down_own[0].send_all(0)

    hooks += [out_and_down, arrived(es["m"], es["my"], es["mc"])]
    hooks += passes(qkv_mid)
    hooks += [functools.partial(down_own[1].send_all, 0)]
    run_up(up_bias, n2, upa, g, slope, hooks)
    ends([qkv_own, qkv_mid])
    own_qkv.wait()
    run_project(qkv_bias, n1, qkva, cos, sin, p, passes(out_own) + [arrived(es["my"], es["myc"])])

    same = lambda i: i
    qkv_s = Scatter(links, g_qkv, same, feat, (0, 1), *stage_refs[0], f, t, masks)
    out_s = Scatter(links, g_out, lambda i: out_place(i, top), orow, (None,), *stage_refs[1], f, t, masks)
    down_s = Scatter(links, g_down, lambda i: (i // 4) * 2 + i % 2, sub, (None,), *stage_refs[2], f, t, masks)
    up_s = Scatter(links, g_up, same, feat, (0, 1), *stage_refs[3], f, t, masks)
    down_o, qkv_o, up_o = Outer(down_s, g, ea), Outer(qkv_s, n1, dproj), Outer(up_s, n2, dh)

    for name in ("c", "mc", "yc", "myc"):
        es[name].wait_recv()
    own_e.wait()
    ends([out_own])
    down_o.give(True)
    down_s.send(True)
    down_o.give(False, passes(down_own[0]))
    for i in range(ea.shape[0] // TILE):
        at = slice(i * TILE, (i + 1) * TILE)
        da[at, :] = dot(ea[at, :], outa[...], NT).astype(bf16)
    run_attention(length, 0, bounds, p, da, cos, sin, a, dproj, dk, dv)
    for hook in passes(down_own[1]):
        hook()
    run_attention(length, 1, bounds, p, da, cos, sin, a, dproj, dk, dv)
    qkv_o.give(True)
    qkv_s.send(True)
    qkv_o.give(False)
    down_o.keep(True)
    down_s.send_on()
    ends(down_own)
    own_down.wait()
    run_hidden_grad(ea, downa, slope, dh, bias_sum)
    down_s.send(False)
    up_o.give(True)
    up_s.send(True)
    up_o.give(False)
    qkv_o.keep(True)
    qkv_s.send_on()
    norm_t = Tokens(links, token_refs[0], rows, f, t)
    branch_t = Tokens(links, token_refs[1], rows, f, t)
    norm_job = run_norm_grad(vec, dh, upa, dproj, qkva, xa, sums, qkv_sum)
    branch_job = run_branch(a, outa, g, downa)
    norm_t.give(norm_job)
    qkv_s.send(False)
    norm_t.keep(norm_job, True)
    up_o.keep(True)
    up_s.send_on()
    up_s.send(False)
    norm_t.keep(norm_job, False)
    branch_t.give(branch_job)
    run_outer_wide(a, ea, g_out)
    out_s.send(True)
    out_s.send(False)
    branch_t.keep(branch_job, True)
    branch_t.keep(branch_job, False)

    small[...] = jnp.zeros_like(small)
    small[0:4, :] = sums[0:4, :]
    small[4:5, :] = jnp.sum(e_own[...].astype(f32), axis=0, keepdims=True)
    for c in range(3):
        for h in range(d // HD):
            small[5 + c : 6 + c, h * HD : (h + 1) * HD] = jnp.where(
                t * 2 + mid == h, qkv_sum[0:1, c * HD : (c + 1) * HD], 0.0
            )
    chunk = 2 * sub
    for tt in range(4):
        for hh in range(mine // chunk):
            for mm in range(2):
                at = (hh * 2 + mm) * chunk
                small[8 + tt : 9 + tt, at : at + chunk] = jnp.where(
                    (t == tt) & (mid == mm), bias_sum[0:1, hh * chunk : (hh + 1) * chunk], 0.0
                )
    small_peers = [core_peer, y_peer, mid_peer] + [(flip(f, m), t) for m in masks]
    small_copies = [links.copy(small, small_in.at[r], peer) for r, peer in enumerate(small_peers)]

    def small_add(r):
        small_copies[r].wait()
        small[...] += small_in[r]
        if r + 1 < len(small_peers):
            small_copies[r + 1].start()

    def exchange_columns(job, dst, k):
        total = job.sums[-1]
        c = links.copy(block(total, 1 - mid, feat), dst.at[mid], mid_peer)
        c.start()
        stay = pltpu.make_async_copy(block(total, mid, feat), dst.at[mid], local_sem.at[k])
        stay.start()
        return c, stay

    small_copies[0].start()
    out_s.got(True)
    out_s.first_adds(True)
    out_s.send_on()
    small_add(0)
    down_o.keep(False)
    small_add(1)
    qkv_o.keep(False)
    small_add(2)
    norm_t.across()
    small_add(3)
    up_o.keep(False)
    out_s.got(False)
    out_s.first_adds(False)
    for r in range(4, len(small_peers)):
        small_add(r)
    down_s.finish()
    qkv_s.finish()
    qkv_x = exchange_columns(qkv_s, qkv_new, 7)
    branch_t.across()
    out_s.finish()
    out_back = Swap(links, out_s.sums[-1], out_new, out_new, f, t, swapped, local_sem.at[8])
    out_back.start()
    up_s.finish()
    up_x = exchange_columns(up_s, up_new, 9)
    norm_t.finish()
    branch_t.finish()
    for c, stay in (qkv_x, up_x):
        c.wait_recv()
        stay.wait()
    out_back.wait()
    out_in.drain()
    out_back.drain()
    for c in links.started:
        if all(c is not other for other in small_copies):
            c.wait_send()


ANY = pl.BlockSpec(memory_space=pl.ANY)
VMEM = pl.BlockSpec(memory_space=pltpu.VMEM)
SMEM = pl.BlockSpec(memory_space=pltpu.SMEM)


def run_layer(masks, top, length, tp, x, e, up, qkv, down, out, cos, sin, vec, qkv_bias, up_bias, bounds):
    rows, d = x.shape
    tokens = 2 * tp * rows
    mine, wide = up.shape[2], qkv.shape[2]
    feat, sub, orow = up.shape[1], down.shape[0], out.shape[0]
    n_keys = 1 << len(masks)
    hi_n = n_keys // 2
    shapes = [
        (tokens, d), (tokens, d), (tokens, d), (tokens, mine), (tokens, mine),
        (d, wide), (HD, d), (mine, d), (d, mine),
    ]
    copies = 2 * 7 + 2 * (1 + 2 * (n_keys - 1)) + 2 * (n_keys - 1) + n_keys
    for height, width, mids in ((feat, wide, 2), (orow, d, 1), (sub, d, 1), (feat, mine, 2)):
        for _ in range(2):
            for level in range(len(masks)):
                shapes.append(((hi_n >> level) * mids * height, width))
        copies += (2 * hi_n - 1) * mids + 1
    for _ in range(2):
        shapes += [(4 * rows, d)] * 3 + [(2 * rows, d)] * 2 + [(2, rows, d)]
        copies += 7
    shapes += [(2, feat, mine), (2, feat, wide), (orow, d)]
    n_small = len(masks) + 3
    copies += n_small
    out_shape = [jax.ShapeDtypeStruct(shape, bf16) for shape in shapes]
    out_shape.append(jax.ShapeDtypeStruct((16, d), f32))
    result = pl.pallas_call(
        functools.partial(layer_kernel, masks, top, length),
        out_shape=out_shape,
        in_specs=[ANY] * 6 + [VMEM] * 6 + [SMEM],
        out_specs=[ANY] * len(shapes) + [VMEM],
        scratch_shapes=[
            pltpu.VMEM((tokens, d), bf16),
            pltpu.VMEM((d, mine), bf16),
            pltpu.VMEM((d, wide), bf16),
            pltpu.VMEM((mine, d), bf16),
            pltpu.VMEM((HD, d), bf16),
            pltpu.VMEM((tokens, wide), bf16),
            pltpu.VMEM((tokens, HD), bf16),
            pltpu.VMEM((tokens, HD), bf16),
            pltpu.VMEM((tokens, wide), bf16),
            pltpu.VMEM((tokens, mine), bf16),
            pltpu.VMEM((length, HD), f32),
            pltpu.VMEM((length, HD), f32),
            pltpu.VMEM((8, d), f32),
            pltpu.VMEM((8, wide), f32),
            pltpu.VMEM((8, mine), f32),
            pltpu.VMEM((n_small, 16, d), f32),
            pltpu.SemaphoreType.DMA((copies,)),
            pltpu.SemaphoreType.DMA((copies,)),
            pltpu.SemaphoreType.DMA((10,)),
        ],
        compiler_params=pltpu.CompilerParams(
            collective_id=0, has_side_effects=True, vmem_limit_bytes=60 * 2**20
        ),
        name="layer",
    )(x, e, up, qkv, down, out, cos, sin, e, vec, qkv_bias, up_bias, bounds)
    stage = len(masks)
    at = N_HBM + 2 * stage * 4
    down_new = result[N_HBM + 2 * stage * 3 - 1]
    norm_final, branch_final = result[at + 5], result[at + 11]
    up_new, qkv_new, out_new, small = result[at + 12 : at + 16]
    return norm_final, branch_final, up_new, qkv_new, out_new, down_new, small


def make_local(fsdp, tp):
    lo_n = 2
    hi_n = fsdp // 4
    masks = [1 << b for b in range(2, fsdp.bit_length() - 1)] + [1]
    top = fsdp // 2

    def local(
        layer_input,
        out_cotangent,
        segments,
        qkv_weight,
        qkv_first,
        qkv_second,
        out_weight,
        out_first,
        out_second,
        up_weight,
        up_first,
        up_second,
        down_weight,
        down_first,
        down_second,
        small_params,
        small_first,
        small_second,
    ):
        f = lax.axis_index("fsdp")
        t = lax.axis_index("tp")
        mid = (f // 2) % 2
        rows, d = layer_input.shape
        length = segments.shape[1]
        width = qkv_weight.shape[3]
        hidden = up_weight.shape[2]
        sub = hidden // fsdp
        feat = d // fsdp
        mine = hidden // 2
        vector = small_params[0]

        up16 = up_weight[0].astype(bf16).reshape(feat, hi_n, 2, lo_n * sub)
        up16 = up16.transpose(2, 0, 1, 3).reshape(2, feat, mine)
        qkv16 = qkv_weight[0].astype(bf16).reshape(3, feat, 2, HD)
        qkv16 = qkv16.transpose(2, 1, 0, 3).reshape(2, feat, 3 * HD)
        down16 = down_weight[0].astype(bf16)
        out16 = out_weight[0].astype(bf16)

        own_bounds = jnp.stack([jnp.sum(segments[0] < 1), jnp.sum(segments[0] < 2)]).astype(f32)
        other_bounds = lax.ppermute(own_bounds, "fsdp", [(i, i ^ 2) for i in range(fsdp)])
        bounds = jnp.where(
            mid == 0, jnp.stack([own_bounds, other_bounds]), jnp.stack([other_bounds, own_bounds])
        ).astype(jnp.int32)
        index = jnp.arange(length, dtype=jnp.int32)[None]
        first, second = bounds[:, 0:1], bounds[:, 1:2]
        start = jnp.where(index >= second, second, jnp.where(index >= first, first, 0))
        position = (index - start).astype(f32).reshape(2 * length, 1)
        half = ROT // 2
        lane = jnp.arange(128)
        frequency = 10000.0 ** (-(2 * (lane % half)).astype(f32) / ROT)
        angle = position * frequency[None]
        cosine = jnp.where(lane < ROT, jnp.cos(angle), 1.0)
        sine = jnp.where(lane < ROT, jnp.where(lane < half, -1.0, 1.0) * jnp.sin(angle), 0.0)

        norms = vector[0 : 4 * d].reshape(4, d)
        vec = jnp.concatenate([norms, jnp.zeros((4, d), f32)])
        qkv_bias = lax.dynamic_slice_in_dim(
            vector[6 * d : 9 * d].reshape(3, d), t * width + mid * HD, HD, 1
        ).reshape(1, 3 * HD)
        up_bias = lax.dynamic_slice(
            vector[9 * d :].reshape(tp, hi_n, 2, lo_n * sub), (t, 0, mid, 0), (1, hi_n, 1, lo_n * sub)
        ).reshape(1, mine)

        norm_final, branch_final, up_new, qkv_new, out_new, down_new, small = run_layer(
            masks, top, length, tp, layer_input, out_cotangent, up16, qkv16, down16, out16,
            cosine, sine, vec, qkv_bias, up_bias, bounds,
        )

        stream = layer_input.astype(f32)
        bias = vector[4 * d : 5 * d] + vector[5 * d : 6 * d]
        layer_output = stream + (branch_final[0].astype(f32) + branch_final[1].astype(f32)) + bias
        scaled = norm_final[0].astype(f32) + norm_final[1].astype(f32)
        centred = stream - jnp.mean(stream, axis=-1, keepdims=True)
        inverse = lax.rsqrt(jnp.mean(centred * centred, axis=-1, keepdims=True) + norm_eps)
        normal = centred * inverse
        input_grad = out_cotangent.astype(f32) + inverse * (
            scaled
            - jnp.mean(scaled, axis=-1, keepdims=True)
            - normal * jnp.mean(scaled * normal, axis=-1, keepdims=True)
        )
        qkv_total = qkv_new.reshape(2, feat, 3, HD).transpose(2, 1, 0, 3).reshape(1, 3, feat, width)
        up_total = up_new.reshape(2, feat, hi_n, lo_n * sub).transpose(1, 2, 0, 3).reshape(1, feat, hidden)
        small_total = jnp.concatenate(
            [small[0:5].reshape(-1), small[4:5].reshape(-1), small[5:12].reshape(-1)]
        )[None]
        rate_matrix = d ** (-0.5)
        rate_output = 4.0 * d ** (-0.5)
        results = [layer_output, input_grad]
        for weight, first, second, grad, rate, decay in (
            (qkv_weight, qkv_first, qkv_second, qkv_total, rate_matrix, decay_rate),
            (out_weight, out_first, out_second, out_new[None], rate_output, decay_rate),
            (up_weight, up_first, up_second, up_total, rate_matrix, decay_rate),
            (down_weight, down_first, down_second, down_new[None], rate_matrix, decay_rate),
            (small_params, small_first, small_second, small_total, rate_vector, 0.0),
        ):
            results.extend(adam_step(weight, first, second, grad.astype(f32), rate, decay))
        return tuple(results)

    return local


def solution(mesh):
    tokens = P(("fsdp", "tp"), None)
    inner = P(None, ("tp", "fsdp"), None)
    qkv = P(None, None, "fsdp", "tp")
    up = P(None, "fsdp", "tp")
    weights = (qkv,) * 3 + (inner,) * 3 + (up,) * 3 + (inner,) * 3 + (P(),) * 3
    return jax.shard_map(
        make_local(mesh.shape["fsdp"], mesh.shape["tp"]),
        mesh=mesh,
        in_specs=(tokens, tokens, P("fsdp", None)) + weights,
        out_specs=(tokens, tokens) + weights,
        check_vma=False,
    )
```

```python
import functools

import jax
import jax.numpy as jnp
import numpy as np
from jax import lax
from jax.experimental import pallas as pl
from jax.experimental.pallas import tpu as pltpu
from jax.sharding import PartitionSpec as P

HD = 256
ROT = 64
STEP = 10

norm_eps = 1e-05
beta_one = 0.9
beta_two = 0.95
adam_eps = 1e-08
decay_rate = 0.01
rate_vector = 0.2
masked_score = -1e30
f32 = jnp.float32
bf16 = jnp.bfloat16


def adam_step(weight, first, second, grad, rate, decay):
    first_new = beta_one * first + (1.0 - beta_one) * grad
    second_new = beta_two * second + (1.0 - beta_two) * grad * grad
    first_hat = first_new / (1.0 - beta_one**STEP)
    second_hat = second_new / (1.0 - beta_two**STEP)
    weight_new = weight - rate * (first_hat / (jnp.sqrt(second_hat) + adam_eps) + decay * weight)
    return (first_new, second_new, weight_new)


MESH = pl.DeviceIdType.MESH


def bit_of(i, mask):
    return (i // mask) % 2


def flip(i, mask):
    return i + mask - 2 * mask * bit_of(i, mask)


class Copy:
    def __init__(self, copy):
        self.copy, self.started, self.received, self.sent = copy, False, False, False

    def start(self):
        self.started = True
        self.copy.start()

    def wait_recv(self):
        self.received = True
        self.copy.wait_recv()

    def wait_send(self):
        self.sent = True
        self.copy.wait_send()


class Local:
    def __init__(self, copy):
        self.copy, self.started, self.done = copy, False, False

    def start(self):
        self.started = True
        self.copy.start()

    def wait(self):
        self.done = True
        self.copy.wait()


class Links:
    def __init__(self, send_sem, recv_sem, local_sem):
        self.send_sem, self.recv_sem, self.local_sem = send_sem, recv_sem, local_sem
        self.copies, self.locals, self.swaps, self.n_local = [], [], [], 0

    def local(self, src, dst):
        c = Local(pltpu.make_async_copy(src, dst, self.local_sem.at[self.n_local]))
        self.n_local += 1
        self.locals.append(c)
        return c

    def copy(self, src, dst, device):
        k = len(self.copies)
        c = Copy(
            pltpu.make_async_remote_copy(
                src_ref=src,
                dst_ref=dst,
                send_sem=self.send_sem.at[k],
                recv_sem=self.recv_sem.at[k],
                device_id=device,
                device_id_type=MESH,
            )
        )
        self.copies.append(c)
        return c

    def drain(self):
        for c in self.copies:
            if c.started and not c.received:
                c.wait_recv()
            if c.started and not c.sent:
                c.wait_send()
        for c in self.locals:
            if c.started and not c.done:
                c.wait()
        for c in self.swaps:
            c.drain()


class Group:
    def __init__(self, links, at, f, t, masks, root):
        self.copies, self.masks = {}, masks
        for key in all_keys(masks):
            g = root
            for mask in masks:
                if key & mask:
                    g = flip(g, mask)
            ref = at(g)
            after = max([i + 1 for i, m in enumerate(masks) if key & m], default=0)
            for mask in masks[after:]:
                self.copies[key | mask] = links.copy(ref, ref, (flip(f, mask), t))

    def low(self):
        self.copies[1].start()

    def high(self):
        self.copies[self.masks[0]].start()

    def rest(self):
        keys = all_keys(self.masks[:-1])
        for s, mask in enumerate(self.masks[1:-1]):
            for key in all_keys(self.masks[: s + 1]):
                if key:
                    self.copies[key].wait_recv()
                self.copies[key | mask].start()
        last = self.masks[-2]
        for key in keys:
            if key & last:
                self.copies[key].wait_recv()
            if key:
                self.copies[key | 1].start()

    def ends(self):
        return [c for key, c in self.copies.items() if key & 1]


def all_keys(masks):
    keys = [0]
    for mask in masks:
        keys = keys + [k | mask for k in keys]
    return keys


def normalise(x):
    mean = jnp.mean(x, axis=-1, keepdims=True)
    centred = x - mean
    inverse = lax.rsqrt(jnp.mean(centred * centred, axis=-1, keepdims=True) + norm_eps)
    return centred * inverse


def rope(u, c, s):
    lane = lax.broadcasted_iota(jnp.int32, u.shape, 1)
    partner = jnp.where(lane < ROT // 2, pltpu.roll(u, 128 - ROT // 2, 1), pltpu.roll(u, ROT // 2, 1))
    return u * c + partner * s


def dot(a, b, dims):
    return lax.dot_general(a, b, (dims, ((), ())), preferred_element_type=f32)


NN = ((1,), (0,))
NT = ((1,), (1,))
TN = ((0,), (0,))
TILE = 256


def pipe(body, steps, ins, outs, hooks=()):
    def whole(*refs):
        for i, n, run in hooks:
            pl.when(pl.program_id(0) == i * steps // n)(run)
        body(*refs)

    pltpu.emit_pipeline(
        whole,
        grid=(steps,),
        in_specs=[spec for _, spec in ins],
        out_specs=[spec for _, spec in outs],
    )(*[ref for ref, _ in ins], *[ref for ref, _ in outs])


def by_rows(ref, index=lambda i: i, rows=TILE):
    return ref, pl.BlockSpec((rows, ref.shape[1]), lambda i: (index(i), 0))


def by_columns(ref, index, width):
    return ref, pl.BlockSpec((ref.shape[0], width), lambda i: (0, index(i)))


def here(i, rows=TILE):
    return pl.ds(pl.multiple_of(i * rows, rows), rows)


def run_cast(weight, index, steps, width, dst):
    def body(w_ref):
        at = pl.ds(pl.multiple_of(pl.program_id(0) * width, width), width)
        dst[:, at] = w_ref[...].astype(bf16)

    pipe(body, steps, [by_columns(weight, index, width)], [])


def run_cast_qkv(weight, half, dst):
    def body(w_ref):
        at = pl.ds(pl.multiple_of(pl.program_id(0) * HD, HD), HD)
        dst[:, at] = w_ref[...].reshape(w_ref.shape[-2:]).astype(bf16)

    spec = pl.BlockSpec((1, weight.shape[1], HD), lambda i: (i, 0, half))
    pipe(body, 3, [(weight, spec)], [])


def run_norms(vec, x, n1, n2, index, steps, hooks=()):
    def body(x_ref, one_ref, two_ref):
        normal = normalise(x_ref[...].astype(f32))
        one_ref[...] = (normal * vec[0:1, :] + vec[1:2, :]).astype(bf16)
        two_ref[...] = (normal * vec[2:3, :] + vec[3:4, :]).astype(bf16)

    pipe(body, steps, [by_rows(x, index)], [by_rows(n1, index), by_rows(n2, index)], hooks)


class Rotary:
    def __init__(self, table, starts, seq):
        self.table, self.starts, self.seq = table, starts, seq

    def bounds(self):
        at = pl.ds(self.seq * 8, 1)
        return self.starts[at, 0:1].astype(jnp.int32), self.starts[at, 1:2].astype(jnp.int32)

    def __call__(self, tile):
        shape = (TILE, 128)
        lane = lax.broadcasted_iota(jnp.int32, (1, 128), 1)
        first, second = self.bounds()
        turning = lane < ROT
        rate = self.table[0:1, 256:384]
        one, two = first.astype(f32) * rate, second.astype(f32) * rate
        index = tile * TILE + lax.broadcasted_iota(jnp.int32, shape, 0)
        pick = lambda a, b, c: jnp.where(index >= second, c, jnp.where(index >= first, b, a))
        cos_b = pick(jnp.ones_like(one), jnp.cos(one), jnp.cos(two))
        sin_b = pick(jnp.zeros_like(one), jnp.sin(one), jnp.sin(two))
        rows = here(tile)
        cos_t, sin_t = self.table[rows, 0:128], self.table[rows, 128:256]
        sign = jnp.where(lane < ROT // 2, -1.0, 1.0)
        c = jnp.where(turning, cos_t * cos_b + sin_t * sin_b, 1.0)
        s = jnp.where(turning, sign * (sin_t * cos_b - cos_t * sin_b), 0.0)
        return c, s


def run_project(qkv_bias, n1, w, rotary, seq, p, turns, steps, hooks=()):
    def body(n_ref):
        i = pl.program_id(0)
        at = here(seq * steps + i)
        c, s = rotary(i)
        turns[at, 0:128] = c
        turns[at, 128:256] = s
        proj = dot(n_ref[...], w[...], NN) + qkv_bias()
        for j in range(2):
            p[at, j * HD : j * HD + 128] = rope(proj[:, j * HD : j * HD + 128], c, s).astype(bf16)
            p[at, j * HD + 128 : (j + 1) * HD] = proj[:, j * HD + 128 : (j + 1) * HD].astype(bf16)
        p[at, 2 * HD :] = proj[:, 2 * HD :].astype(bf16)

    pipe(body, steps, [by_rows(n1, lambda i: seq * steps + i)], [], hooks)


def run_up(up_bias, n2, w, g, slope, index, steps, hooks=()):
    width = w.shape[1]
    part = min(width, 256)

    def body(n_ref, g_ref, s_ref):
        n = n_ref[...]
        for j in range(0, width, part):
            h = dot(n, w[:, j : j + part], NN) + up_bias[0:1, j : j + part]
            cdf = 0.5 + 0.5 * lax.erf(h * 0.7071067811865476)
            g_ref[:, j : j + part] = (h * cdf).astype(bf16)
            s_ref[:, j : j + part] = (cdf + h * (jnp.exp(-0.5 * h * h) * 0.3989422804014327)).astype(bf16)

    pipe(body, steps, [by_rows(n2, index)], [by_rows(g, index), by_rows(slope, index)], hooks)


def run_attention(length, seq, rotary, p, da, turns, a, dproj, dk, dv):
    scale = HD ** (-0.5)
    tiles_n = length // TILE
    first, second = rotary.bounds()
    rows = lambda i: here(seq * tiles_n + i)

    def put(i, value, column):
        at = rows(i)
        dproj[at, column : column + 128] = rope(value[:, :128], turns[at, 0:128], -turns[at, 128:256]).astype(bf16)
        dproj[at, column + 128 : column + HD] = value[:, 128:].astype(bf16)

    dk[...] = jnp.zeros_like(dk)
    dv[...] = jnp.zeros_like(dv)
    for i in range(tiles_n):
        n = (i + 1) * TILE
        until = pl.ds(pl.multiple_of(seq * length, length), n)
        q = p[rows(i), 0:HD]
        k = p[until, HD : 2 * HD]
        v = p[until, 2 * HD :]
        rows_da = da[rows(i), :]
        scores = dot(q, k, NT) * scale
        qi = i * TILE + lax.broadcasted_iota(jnp.int32, (TILE, n), 0)
        ki = lax.broadcasted_iota(jnp.int32, (TILE, n), 1)
        start = jnp.where(qi >= second, second, jnp.where(qi >= first, first, 0))
        scores = jnp.where((ki <= qi) & (ki >= start), scores, masked_score)
        peak = jnp.max(scores, axis=-1, keepdims=True)
        raised = jnp.exp(scores - peak)
        probs = raised * (1.0 / jnp.sum(raised, axis=-1, keepdims=True))
        weights = probs.astype(bf16)
        a[rows(i), :] = dot(weights, v, NN).astype(bf16)
        prob_grad = dot(rows_da, v, NT)
        delta = jnp.sum(probs * prob_grad, axis=-1, keepdims=True)
        score_grad = (probs * (prob_grad - delta)).astype(bf16)
        put(i, dot(score_grad, k, NN) * scale, 0)
        dk[0:n, :] += dot(score_grad, q, TN)
        dv[0:n, :] += dot(weights, rows_da, TN)
    for i in range(tiles_n):
        local = slice(i * TILE, (i + 1) * TILE)
        put(i, dk[local, :] * scale, HD)
        dproj[rows(i), 2 * HD :] = dv[local, :].astype(bf16)


def run_outer(a, b, out, index_in, index_out, steps, width, add=None, hooks=()):
    def body(*refs):
        value = dot(refs[0][...], b[...], TN)
        if add is not None:
            value = value + refs[1][...].astype(f32)
        refs[-1][...] = value.astype(bf16)

    ins = [by_columns(a, index_in, width)]
    if add is not None:
        ins.append(by_rows(add, index_out, width))
    pipe(body, steps, ins, [by_rows(out, index_out, width)], hooks)


def run_outer_wide(a, b, out):
    width = 2 * TILE

    def body(out_ref):
        at = pl.ds(pl.multiple_of(pl.program_id(0) * width, width), width)
        out_ref[...] = dot(a[...], b[:, at], TN).astype(bf16)

    pipe(body, b.shape[1] // width, [], [by_columns(out, lambda i: i, width)])


def run_hidden_grad(e, w, slope, dh, bias_sum, index, steps, hooks=()):
    def body(s_ref):
        at = here(index(pl.program_id(0)))
        value = (dot(e[at, :], w[...], NT) * s_ref[...].astype(f32)).astype(bf16)
        dh[at, :] = value
        bias_sum[0:1, :] += jnp.sum(value.astype(f32), axis=0, keepdims=True)

    pipe(body, steps, [by_rows(slope, index)], [], hooks)


def run_norm_grad(vec, dh, w_up, dproj, w_qkv, x, sums, qkv_sum):
    def tile(at, x_ref):
        normal = normalise(x_ref[...].astype(f32))
        rows = dproj[at, :]
        one = dot(rows, w_qkv[...], NT)
        two = dot(dh[at, :], w_up[...], NT)
        for j, value in ((0, one * normal), (1, one), (2, two * normal), (3, two)):
            sums[j : j + 1, :] += jnp.sum(value, axis=0, keepdims=True)
        qkv_sum[0:1, :] += jnp.sum(rows.astype(f32), axis=0, keepdims=True)
        return one * vec[0:1, :] + two * vec[2:3, :]

    return x, tile


def run_branch(a, w_out, g, w_down):
    def tile(at, g_ref):
        return dot(a[at, :], w_out[...], NN) + dot(g_ref[...], w_down[...], NN)

    return g, tile


def run_token_tiles(job, out, index, index_out, steps, add=None, hooks=()):
    source, tile = job

    def body(*refs):
        value = tile(here(index(pl.program_id(0))), refs[0])
        if add is not None:
            value = value + refs[1][...].astype(f32)
        refs[-1][...] = value.astype(bf16)

    ins = [by_rows(source, index)]
    if add is not None:
        ins.append(by_rows(add, index_out))
    pipe(body, steps, ins, [by_rows(out, index_out)], hooks)


def run_add(a, b, out):
    rows, cols = out.shape
    step = min(rows, TILE)

    def body(a_ref, b_ref, out_ref):
        out_ref[...] = (a_ref[...].astype(f32) + b_ref[...].astype(f32)).astype(bf16)

    pipe(body, rows // step, [by_rows(a, rows=step), by_rows(b, rows=step)], [by_rows(out, rows=step)])


def block(ref, index, rows):
    return ref.at[pl.ds(pl.multiple_of(index * rows, rows), rows)]


def out_place(g, top):
    return (((g // 4) % (top // 4)) * 2 + g // top) * 2 + g % 2


class Scatter:
    def __init__(self, links, part, place, rows, mids, recv, sums, f, t, masks):
        self.links, self.part, self.place, self.rows, self.mids = links, part, place, rows, mids
        self.recv, self.sums, self.f, self.t = recv, sums, f, t
        self.stages = [1] + [m for m in reversed(masks) if m != 1]
        self.n_hi = 1 << (len(masks) - 1)
        self.hi, self.lo, self.mid = f // 4, f % 2, bit_of(f, 2)
        self.copies = {}
        for k in range(self.n_hi):
            for j, m in enumerate(mids):
                self.copies[0, k, j] = links.copy(
                    block(part, self.at_place(self.high(k), m, 1 - self.lo), rows),
                    block(recv[0], self.slot(0, k, j), rows),
                    (flip(f, 1), t),
                )
        for level in range(len(self.stages) - 1):
            n = self.n_hi >> (level + 1)
            for k in range(n, 2 * n):
                for j in range(len(mids)):
                    self.copies[level + 1, k - n, j] = links.copy(
                        block(sums[level], self.slot(level, k, j), rows),
                        block(recv[level + 1], self.slot(level + 1, k, j), rows),
                        (flip(f, self.stages[level + 1]), t),
                    )

    def high(self, k):
        hi, b = self.hi, 1
        while b < self.n_hi:
            if k & b:
                hi = flip(hi, b)
            b *= 2
        return hi

    def slot(self, level, k, j):
        n = self.n_hi >> level
        i = (self.high(k) % n) if n > 1 else 0
        return i * len(self.mids) + j

    def at_place(self, hi, m, lo):
        return self.place((hi * 2 + (self.mid if m is None else m)) * 2 + lo)

    def ks(self, far):
        half = self.n_hi // 2
        return range(half, self.n_hi) if far else range(half)

    def each(self, far):
        return [(k, j) for k in self.ks(far) for j in range(len(self.mids))]

    def tile(self, i, far, lo):
        n = len(self.mids)
        half = self.n_hi // 2
        upper = self.hi // half
        hi = (1 - upper if far else upper) * half + i // n
        j = i % n
        m = None if self.mids[0] is None else j
        return self.at_place(hi, m, lo), hi * n + j

    def add(self, level, k, j):
        mine = (
            block(self.part, self.at_place(self.high(k), self.mids[j], self.lo), self.rows)
            if level == 0
            else block(self.sums[level - 1], self.slot(level - 1, k, j), self.rows)
        )
        at = self.slot(level, k, j)
        run_add(mine, block(self.recv[level], at, self.rows), block(self.sums[level], at, self.rows))

    def first_adds(self, far):
        for k, j in self.each(far):
            self.add(0, k, j)

    def finish(self, waited):
        for level in range(1, len(self.stages)):
            n = self.n_hi >> level
            for k in reversed(range(n)):
                for j in range(len(self.mids)):
                    if not waited:
                        self.copies[level, k, j].wait_recv()
                    self.add(level, k, j)
                    if level + 1 < len(self.stages) and k & (n // 2):
                        self.copies[level + 1, k - n // 2, j].start()


class Outer:
    def __init__(self, scatter, a, b):
        self.s, self.a, self.b = scatter, a, b
        self.fused = scatter.rows % 128 == 0
        self.steps = scatter.n_hi // 2 * len(scatter.mids)

    def give(self, far, hooks=()):
        s = self.s
        if self.fused:
            at = lambda i: s.tile(i, far, 1 - s.lo)[0]
            run_outer(self.a, self.b, s.part, at, at, self.steps, s.rows, hooks=hooks)
        elif far:
            run_outer(self.a, self.b, s.part, lambda i: i, lambda i: i, self.a.shape[1] // 128, 128, hooks=hooks)

    def keep(self, far, hooks=()):
        s = self.s
        if self.fused:
            at = lambda i: s.tile(i, far, s.lo)[0]
            to = lambda i: s.tile(i, far, s.lo)[1]
            run_outer(self.a, self.b, s.sums[0], at, to, self.steps, s.rows, add=s.recv[0], hooks=hooks)
        else:
            s.first_adds(far)


class Tokens:
    def __init__(self, links, refs, rows, f, t, job):
        self.give_buf, self.got, self.sum, self.got_y, self.sum_y, self.final = refs
        self.rows, self.mid, self.y, self.core, self.job = rows, bit_of(f, 2), t // 2, t % 2, job
        core_peer, y_peer, mid_peer = (f, flip(t, 1)), (f, flip(t, 2)), (flip(f, 2), t)
        self.over_core = [
            links.copy(block(self.give_buf, i, rows), block(self.got, i, rows), core_peer) for i in range(4)
        ]
        self.over_y = [
            links.copy(block(self.sum, m * 2 + 1 - self.y, rows), block(self.got_y, m, rows), y_peer)
            for m in range(2)
        ]
        self.over_mid = [links.copy(block(self.sum_y, 1 - self.mid, rows), self.final.at[1], mid_peer)]

    def give(self, hooks=()):
        index = lambda i: (i // 2) * 4 + (i % 2) * 2 + 1 - self.core
        run_token_tiles(self.job, self.give_buf, index, lambda i: i, 4, hooks=hooks)

    def keep(self, far, hooks=()):
        yy = 1 - self.y if far else self.y
        index = lambda i: i * 4 + yy * 2 + self.core
        run_token_tiles(self.job, self.sum, index, lambda i: i * 2 + yy, 2, add=self.got, hooks=hooks)

    def across(self, own):
        m = self.mid if own else 1 - self.mid
        to = self.final.at[0] if own else block(self.sum_y, m, self.rows)
        run_add(block(self.sum, m * 2 + self.y, self.rows), block(self.got_y, m, self.rows), to)


def greet(f, t, masks, top):
    mid = bit_of(f, 2)
    swapped = f + (top - 2) * (mid - bit_of(f, top))
    barrier = pltpu.get_barrier_semaphore()
    peers = [(flip(f, m), t) for m in masks + [2]] + [(f, flip(t, 1)), (f, flip(t, 2))]
    for peer in peers:
        pl.semaphore_signal(barrier, inc=1, device_id=peer, device_id_type=MESH)

    @pl.when(swapped != f)
    def _():
        pl.semaphore_signal(barrier, inc=1, device_id=(swapped, t), device_id_type=MESH)

    pl.semaphore_wait(barrier, len(peers) + (mid + bit_of(f, top)) % 2)
    return swapped


class Swap:
    def __init__(self, links, src, dst, stay, f, t, swapped):
        self.move = links.copy(src, dst, (swapped, t)).copy
        self.copy = pltpu.make_async_copy(src, stay, links.local_sem.at[links.n_local])
        links.n_local += 1
        links.swaps.append(self)
        self.moves, self.stays = swapped != f, swapped == f
        self.started, self.done = False, False

    def start(self):
        self.started = True
        pl.when(self.moves)(self.move.start)
        pl.when(self.stays)(self.copy.start)

    def wait(self):
        self.done = True
        pl.when(self.moves)(self.move.wait_recv)
        pl.when(self.stays)(self.copy.wait)

    def drain(self):
        if self.started and not self.done:
            self.wait()
        if self.started:
            pl.when(self.moves)(self.move.wait_send)


class Plan:
    def __init__(self):
        self.actions, self.waits = {}, {}

    def send(self, name, needs, starts, *copies):
        self.actions[name] = (None, needs, starts)
        self.waits[name] = copies

    def compute(self, name, needs, run):
        self.actions[name] = (True, needs, run)

    def pending(self, name):
        found = []
        for need in self.actions[name][1]:
            found += self.waits.pop(need, ())
        return found

    def starter(self, name):
        pending, starts = self.pending(name), self.actions[name][2]

        def run():
            for c in pending:
                c()
            for start in starts:
                start()

        return run

    def carry_out(self, order):
        i = 0
        while i < len(order):
            name = order[i]
            i += 1
            compute, _, run = self.actions[name]
            if not compute:
                self.starter(name)()
                continue
            for wait in self.pending(name):
                wait()
            n = 1 + order[i:].count(name)
            hooks = []
            for part in range(1, n):
                while order[i] != name:
                    hooks.append((part, n, self.starter(order[i])))
                    i += 1
                i += 1
            run(hooks) if n > 1 else run(())


ORDER = [
    "xs_m", "xs_y", "cast_out", "cast_qkv", "qkv_first", "cast_down", "down1_x", "es_y", "out_swap", "xs_c",
    "down0_x", "qkv_own_zh", "qkv_mid_zh", "out_x", "qkv_own_zhx", "cast_up", "es_m", "qkv_mid_zhx", "es_c",
    "down1_zh", "xs_my", "out_zh", "qkv_own_x", "up_own_x", "qkv_mid_x", "xs_mc", "xs_yc", "out_zhx", "es_yc",
    "xs_myc", "norms_own", "up_own_zh", "up_first", "es_my", "norms_oth", "down1_zhx", "proj_own", "proj_own",
    "es_mc", "proj_oth", "proj_oth", "up_mid_zh", "up_mid_x", "es_myc", "up_own_zhx", "da_own", "da_oth",
    "attn_own", "attn_oth", "up_mid_zhx", "down0_zh", "gout", "gqkv_gf", "gqkv_f", "gqkv_gn", "up_own",
    "up_own", "up_oth", "down0_zhx", "up_oth", "gqkv_kf", "gqkv_on", "gdown_gf", "gdown_f", "branch_g",
    "branch_g", "branch_c", "dh_oth", "dh_oth", "dh_own", "dh_own", "branch_kf", "branch_y", "gqkv_n",
    "gdown_kf", "gdown_on", "gup_gf", "norm_g", "gout_n", "norm_g", "norm_c", "gout_f", "gqkv_kn", "gqkv_add",
    "gqkv_x", "gup_f", "gout_kf", "branch_kn", "norm_kf", "gout_on", "norm_y", "branch_aa", "branch_m",
    "gdown_gn", "gdown_n", "gup_kf", "gup_on", "norm_kn", "gup_gn", "small0", "gout_kn", "small1", "gdown_kn",
    "gup_n", "branch_ab", "gdown_add", "gout_add", "small2", "norm_aa", "norm_m", "norm_ab", "small3",
    "gup_kn", "small4", "gup_add", "gout_x", "gup_x", "small_end",
]

N_HBM = 9


def layer_kernel(
    masks, top, length,
    x, e, up, qkv, down, out, seg, table, e_own, vec,
    *rest,
):
    n_stage = len(masks)
    (xa, n1, n2, g, slope, g_qkv, g_out, g_down, g_up), rest = rest[:N_HBM], rest[N_HBM:]
    stage_refs = []
    for _ in range(4):
        stage_refs.append((rest[:n_stage], rest[n_stage : 2 * n_stage]))
        rest = rest[2 * n_stage :]
    token_refs, rest = [rest[:6], rest[6:12]], rest[12:]
    (up_new, qkv_new, out_new, small), rest = rest[:4], rest[4:]
    (
        ea, upa, qkva, downa, outa, up16, qkv16, out16, p, da, a, dproj, dh, turns, dk, dv,
        sums, qkv_sum, bias_sum, up_bias, starts, small_in,
        send_sem, recv_sem, local_sem,
    ) = rest
    f = lax.axis_index("fsdp")
    t = lax.axis_index("tp")
    mid = bit_of(f, 2)
    rows, d = x.shape
    feat, sub, orow = up.shape[0], down.shape[0], out.shape[0]
    mine = upa.shape[1]
    chunk = 2 * sub
    hi_n = mine // chunk
    swapped = greet(f, t, masks, top)
    links = Links(send_sem, recv_sem, local_sem)
    plan = Plan()

    mid_peer, y_peer, core_peer = (flip(f, 2), t), (f, flip(t, 2)), (f, flip(t, 1))
    qkv_block = lambda i: block(qkva, i, feat)
    up_block = lambda i: block(upa, i, feat)
    half_sub = sub // 2
    out_block = lambda i: block(outa, out_place(i, top), orow)
    tok = lambda buf, m, j: block(buf, m * 4 + j, rows)

    def sends(name, needs, *copies):
        plan.send(name, needs, [c.start for c in copies], *[c.wait_recv for c in copies])

    own_x = links.local(x, tok(xa, mid, t))
    own_e = links.local(e, tok(ea, mid, t))
    for prefix, source, buf, own in (("xs", x, xa, own_x), ("es", e, ea, own_e)):
        for name, needs, m, j, peer in (
            ("m", (), mid, t, mid_peer),
            ("y", (), mid, t, y_peer),
            ("c", (), mid, t, core_peer),
            ("my", ("m",), 1 - mid, t, y_peer),
            ("mc", ("m",), 1 - mid, t, core_peer),
            ("yc", ("y",), mid, flip(t, 2), core_peer),
            ("myc", ("my",), 1 - mid, flip(t, 2), core_peer),
        ):
            ref = tok(buf, m, j)
            c = links.copy(ref if needs else source, ref, peer)
            sends(prefix + "_" + name, [prefix + "_" + n for n in needs], c)
    plan.waits["own_x"], plan.waits["own_e"] = (own_x.wait,), (own_e.wait,)
    own_x.start()
    own_e.start()

    def spreads(name, group, need):
        sends(name + "_x", need, group.copies[1])
        plan.send(name + "_zh", need, [group.high], *([group.copies[masks[0]].wait_recv] if n_stage == 2 else []))
        if n_stage == 2:
            sends(name + "_zhx", [name + "_zh"], group.copies[masks[0] | 1])
        else:
            plan.send(name + "_zhx", [], [group.rest], *[c.wait_recv for c in group.ends() if c is not group.copies[1]])

    first_up = links.copy(up16, up_block(f), mid_peer)
    first_qkv = links.copy(qkv16, qkv_block(f), mid_peer)
    sends("up_first", [], first_up)
    sends("qkv_first", [], first_qkv)
    spreads("up_own", Group(links, up_block, f, t, masks, f), [])
    spreads("up_mid", Group(links, up_block, f, t, masks, flip(f, 2)), ["up_first"])
    spreads("qkv_own", Group(links, qkv_block, f, t, masks, f), [])
    spreads("qkv_mid", Group(links, qkv_block, f, t, masks, flip(f, 2)), ["qkv_first"])
    for h in range(2):
        at = lambda i, h=h: block(downa, ((i // 4) * 2 + i % 2) * 2 + h, half_sub)
        spreads("down" + str(h), Group(links, at, f, t, masks, f), [])
    out_in = Swap(links, out16, out_block(swapped), out_block(f), f, t, swapped)
    plan.send("out_swap", [], [out_in.start], out_in.wait)
    spreads("out", Group(links, out_block, f, t, masks, f), ["out_swap"])
    other_starts = links.copy(starts.at[pl.ds(0, 8)], starts.at[pl.ds(8, 8)], mid_peer)

    segments = seg[0:1, :]
    count = lambda n: jnp.sum((segments < n).astype(f32), axis=1, keepdims=True)
    lane = lax.broadcasted_iota(jnp.int32, (8, 128), 1)
    starts[0:8, :] = jnp.where(lane == 0, count(1), count(2))
    other_starts.start()
    for ref in (sums, qkv_sum, bias_sum):
        ref[...] = jnp.zeros_like(ref)
    for h in range(hi_n):
        at = pl.ds(pl.multiple_of((h * 2 + mid) * chunk, chunk), chunk)
        up_bias[0:1, h * chunk : (h + 1) * chunk] = sum(
            jnp.where(t == j, vec[9 + j : 10 + j, at], 0.0) for j in range(4)
        )
    head = pl.ds(pl.multiple_of((t * 2 + mid) * HD, HD), HD)
    qkv_bias = lambda: jnp.concatenate([vec[6 + c : 7 + c, head] for c in range(3)], axis=1)

    def cast_qkv(hooks):
        run_cast_qkv(qkv, 1 - mid, qkv16)
        run_cast_qkv(qkv, mid, qkv_block(f))

    def cast_up(hooks):
        run_cast(up, lambda i: i * 2 + 1 - mid, hi_n, chunk, up16)
        run_cast(up, lambda i: i * 2 + mid, hi_n, chunk, up_block(f))

    plan.compute("cast_qkv", [], cast_qkv)
    plan.compute("cast_up", [], cast_up)
    down_rows = block(downa, (f // 4) * 2 + f % 2, sub)
    plan.compute("cast_down", [], lambda hooks: run_cast(down, lambda i: i, 2, d // 2, down_rows))
    plan.compute("cast_out", [], lambda hooks: run_cast(out, lambda i: i, 1, d, out16))

    per_seq = length // TILE
    names = lambda prefix, *ends: [prefix + "_" + end for end in ends]
    of_up = names("up", "own_x", "own_zhx", "mid_x", "mid_zhx")
    of_qkv = names("qkv", "own_x", "own_zhx", "mid_x", "mid_zhx")
    of_down = ["down0_x", "down0_zhx", "down1_x", "down1_zhx"]
    of_out = ["out_x", "out_zhx"]
    plan.waits["starts"] = (other_starts.wait_recv,)
    norms = vec
    for which, seq, arrive in (("own", mid, ("c", "y", "yc")), ("oth", 1 - mid, ("m", "mc", "my", "myc"))):
        own = which == "own"
        rotary = Rotary(table, starts, 0 if own else 1)
        index = lambda i, seq=seq: seq * per_seq + i
        es = names("es", *arrive) + ["own_e"]
        plan.compute(
            "norms_" + which,
            names("xs", *arrive) + ["own_x"],
            lambda hooks, index=index: run_norms(norms, xa, n1, n2, index, per_seq, hooks),
        )
        plan.compute(
            "up_" + which,
            of_up,
            lambda hooks, index=index: run_up(up_bias, n2, upa, g, slope, index, per_seq, hooks),
        )
        plan.compute(
            "proj_" + which,
            of_qkv + ["starts"],
            lambda hooks, seq=seq, rotary=rotary: run_project(
                qkv_bias, n1, qkva, rotary, seq, p, turns, per_seq, hooks
            ),
        )

        def back(hooks, index=index):
            for i in range(per_seq):
                at = here(index(i))
                da[at, :] = dot(ea[at, :], outa[...], NT).astype(bf16)

        plan.compute("da_" + which, of_out + es, back)
        plan.compute(
            "attn_" + which,
            [],
            lambda hooks, seq=seq, rotary=rotary: run_attention(
                length, seq, rotary, p, da, turns, a, dproj, dk, dv
            ),
        )
        plan.compute(
            "dh_" + which,
            of_down + es,
            lambda hooks, index=index: run_hidden_grad(ea, downa, slope, dh, bias_sum, index, per_seq, hooks),
        )
    all_es = names("es", "c", "y", "yc", "m", "mc", "my", "myc") + ["own_e"]

    same = lambda i: i
    down_place = lambda i: (i // 4) * 2 + i % 2

    def scatter(name, part, place, height, mids, refs):
        s = Scatter(links, part, place, height, mids, *refs, f, t, masks)
        for far, end in ((True, "_f"), (False, "_n")):
            sends(name + end, [], *[s.copies[0, k, j] for k, j in s.each(far)])
        half = s.n_hi // 2
        sends(name + "_on", [], *[s.copies[1, k - half, j] for k, j in s.each(True)])
        plan.compute(name + "_add", [name + "_on"] if n_stage == 2 else [], lambda hooks: s.finish(n_stage == 2))
        return s

    def outer(name, s, left, right, needs):
        o = Outer(s, left, right)
        plan.compute(name + "_gf", needs, lambda hooks: o.give(True, hooks))
        plan.compute(name + "_gn", needs, lambda hooks: o.give(False, hooks))
        plan.compute(name + "_kf", [name + "_f"], lambda hooks: o.keep(True, hooks))
        plan.compute(name + "_kn", [name + "_n"], lambda hooks: o.keep(False, hooks))

    qkv_s = scatter("gqkv", g_qkv, same, feat, (0, 1), stage_refs[0])
    out_s = scatter("gout", g_out, lambda i: out_place(i, top), orow, (None,), stage_refs[1])
    down_s = scatter("gdown", g_down, down_place, sub, (None,), stage_refs[2])
    up_s = scatter("gup", g_up, same, feat, (0, 1), stage_refs[3])
    outer("gdown", down_s, g, ea, all_es)
    outer("gqkv", qkv_s, n1, dproj, [])
    outer("gup", up_s, n2, dh, [])
    plan.compute("gout", all_es, lambda hooks: run_outer_wide(a, ea, g_out))
    plan.compute("gout_kf", ["gout_f"], lambda hooks: out_s.first_adds(True))
    plan.compute("gout_kn", ["gout_n"], lambda hooks: out_s.first_adds(False))
    out_back = Swap(links, out_s.sums[-1], out_new, out_new, f, t, swapped)
    plan.send("gout_x", [], [out_back.start], out_back.wait)

    def exchange_columns(name, job, dst):
        total = job.sums[-1]
        c = links.copy(block(total, 1 - mid, feat), dst.at[mid], mid_peer)
        stay = links.local(block(total, mid, feat), dst.at[mid])
        plan.send(name, [], [c.start, stay.start], c.wait_recv)

    exchange_columns("gqkv_x", qkv_s, qkv_new)
    exchange_columns("gup_x", up_s, up_new)

    norm_t = Tokens(links, token_refs[0], rows, f, t, run_norm_grad(vec, dh, upa, dproj, qkva, xa, sums, qkv_sum))
    branch_t = Tokens(links, token_refs[1], rows, f, t, run_branch(a, outa, g, downa))
    for name, job, needs in (("norm", norm_t, []), ("branch", branch_t, of_down + of_out)):
        plan.compute(name + "_g", needs, lambda hooks, job=job: job.give(hooks))
        sends(name + "_c", [], *job.over_core)
        plan.compute(name + "_kf", [name + "_c"], lambda hooks, job=job: job.keep(True, hooks))
        plan.compute(name + "_kn", [name + "_c"], lambda hooks, job=job: job.keep(False, hooks))
        sends(name + "_y", [], *job.over_y)
        plan.compute(name + "_aa", [name + "_y"], lambda hooks, job=job: job.across(False))
        plan.compute(name + "_ab", [name + "_y"], lambda hooks, job=job: job.across(True))
        sends(name + "_m", [], *job.over_mid)

    small_peers = [core_peer, y_peer, mid_peer] + [(flip(f, m), t) for m in masks]
    small_copies = [links.copy(small, small_in.at[r], peer) for r, peer in enumerate(small_peers)]

    def small_fill():
        small[...] = jnp.zeros_like(small)
        small[0:4, :] = sums[0:4, :]
        small[4:5, :] = jnp.sum(e_own[...].astype(f32), axis=0, keepdims=True)
        for c in range(3):
            small[5 + c : 6 + c, head] = qkv_sum[0:1, c * HD : (c + 1) * HD]
        for h in range(hi_n):
            at = pl.ds(pl.multiple_of((h * 2 + mid) * chunk, chunk), chunk)
            for j in range(4):
                small[8 + j : 9 + j, at] = jnp.where(t == j, bias_sum[0:1, h * chunk : (h + 1) * chunk], 0.0)
        small_copies[0].start()

    def small_add(r):
        small_copies[r].wait_send()
        small[...] += small_in[r]

    def small_step(r):
        small_add(r - 1)
        small_copies[r].start()

    def small_end(hooks):
        small_add(4)
        for r in range(5, len(small_peers)):
            small_copies[r].start()
            small_copies[r].wait_recv()
            small_add(r)

    plan.send("small0", [], [small_fill], small_copies[0].wait_recv)
    for r in range(1, 5):
        name = "small" + str(r)
        step = functools.partial(small_step, r)
        plan.send(name, ["small" + str(r - 1)], [step], small_copies[r].wait_recv)
    plan.compute("small_end", ["small4"], small_end)

    plan.carry_out(ORDER)
    links.drain()


ANY = pl.BlockSpec(memory_space=pl.ANY)
VMEM = pl.BlockSpec(memory_space=pltpu.VMEM)


def run_layer(masks, top, length, tp, x, e, up, qkv, down, out, seg, table, vec):
    rows, d = x.shape
    tokens = 2 * tp * rows
    mine, wide = up.shape[1] // 2, 3 * HD
    feat, sub, orow = up.shape[0], down.shape[0], out.shape[0]
    n_keys = 1 << len(masks)
    hi_n = n_keys // 2
    shapes = [
        (tokens, d), (tokens, d), (tokens, d), (tokens, mine), (tokens, mine),
        (d, wide), (HD, d), (mine, d), (d, mine),
    ]
    copies = 2 * 7 + 2 * (1 + 2 * (n_keys - 1)) + 2 * (n_keys - 1) + n_keys + 1
    for height, width, mids in ((feat, wide, 2), (orow, d, 1), (sub, d, 1), (feat, mine, 2)):
        for _ in range(2):
            for level in range(len(masks)):
                shapes.append(((hi_n >> level) * mids * height, width))
        copies += (2 * hi_n - 1) * mids + 1
    for _ in range(2):
        shapes += [(4 * rows, d)] * 3 + [(2 * rows, d)] * 2 + [(2, rows, d)]
        copies += 7
    shapes += [(2, feat, mine), (2, feat, wide), (orow, d)]
    n_small = len(masks) + 3
    copies += n_small
    out_shape = [jax.ShapeDtypeStruct(shape, bf16) for shape in shapes]
    out_shape.append(jax.ShapeDtypeStruct((16, d), f32))
    held = [
        (tokens, d), (d, mine), (d, wide), (mine, d), (HD, d), (feat, mine), (feat, wide), (orow, d),
        (tokens, wide), (tokens, HD), (tokens, HD), (tokens, wide), (tokens, mine),
    ]
    result = pl.pallas_call(
        functools.partial(layer_kernel, masks, top, length),
        out_shape=out_shape,
        in_specs=[ANY] * 6 + [VMEM] * 4,
        out_specs=[ANY] * len(shapes) + [VMEM],
        scratch_shapes=[pltpu.VMEM(shape, bf16) for shape in held]
        + [
            pltpu.VMEM(shape, f32)
            for shape in (
                (tokens, 256), (length, HD), (length, HD), (8, d), (8, wide), (8, mine), (8, mine), (16, 128),
                (n_small, 16, d),
            )
        ]
        + [
            pltpu.SemaphoreType.DMA((copies,)),
            pltpu.SemaphoreType.DMA((copies,)),
            pltpu.SemaphoreType.DMA((8,)),
        ],
        compiler_params=pltpu.CompilerParams(
            collective_id=0, has_side_effects=True, vmem_limit_bytes=60 * 2**20
        ),
        name="layer",
    )(x, e, up, qkv, down, out, seg, table, e, vec)
    stage = len(masks)
    at = N_HBM + 2 * stage * 4
    down_new = result[N_HBM + 2 * stage * 3 - 1]
    norm_final, branch_final = result[at + 5], result[at + 11]
    up_new, qkv_new, out_new, small = result[at + 12 : at + 16]
    return norm_final, branch_final, up_new, qkv_new, out_new, down_new, small


def adam_body(rate, decay, w, m, v, grad, m_out, v_out, w_out):
    g = grad[...].astype(f32).reshape(w.shape)
    m_new, v_new, w_new = adam_step(w[...], m[...], v[...], g, rate, decay)
    w_out[...] = w_new
    m_out[...] = m_new
    v_out[...] = v_new


def update_kernel(
    chunk, rates,
    x, e, vec, norm_final, branch_final, qkv_g, out_g, up_g, down_g,
    qw, qm, qv, ow, om, ov, uw, um, uv, dw, dm, dv,
    layer_output, input_grad, qm_o, qv_o, qw_o, om_o, ov_o, ow_o, um_o, uv_o, uw_o, dm_o, dv_o, dw_o,
):
    feat = uw.shape[0]
    rate, rate_out = rates

    def pipeline(body, grid, ins, outs):
        pltpu.emit_pipeline(
            body, grid=grid, in_specs=[s for _, s in ins], out_specs=[s for _, s in outs]
        )(*[r for r, _ in ins], *[r for r, _ in outs])

    body = functools.partial(adam_body, rate, decay_rate)
    spec = pl.BlockSpec((1, feat, HD), lambda c, q: (c, 0, q))
    grad = pl.BlockSpec((1, feat, HD), lambda c, q: (q, 0, c))
    pipeline(
        body, (3, 2), [(qw, spec), (qm, spec), (qv, spec), (qkv_g, grad)], [(qm_o, spec), (qv_o, spec), (qw_o, spec)]
    )
    spec = pl.BlockSpec((feat, chunk), lambda h, q: (0, h * 2 + q))
    grad = pl.BlockSpec((1, feat, chunk), lambda h, q: (q, 0, h))
    pipeline(
        body,
        (uw.shape[1] // chunk // 2, 2),
        [(uw, spec), (um, spec), (uv, spec), (up_g, grad)],
        [(um_o, spec), (uv_o, spec), (uw_o, spec)],
    )
    rows = min(dw.shape[0], 64)
    spec = pl.BlockSpec((rows, dw.shape[1]), lambda i: (i, 0))
    pipeline(
        body,
        (dw.shape[0] // rows,),
        [(dw, spec), (dm, spec), (dv, spec), (down_g, spec)],
        [(dm_o, spec), (dv_o, spec), (dw_o, spec)],
    )
    half = ow.shape[1] // 2
    spec = pl.BlockSpec((ow.shape[0], half), lambda i: (0, i))
    pipeline(
        functools.partial(adam_body, rate_out, decay_rate),
        (2,),
        [(ow, spec), (om, spec), (ov, spec), (out_g, spec)],
        [(om_o, spec), (ov_o, spec), (ow_o, spec)],
    )

    def tokens(x_ref, e_ref, n_ref, b_ref, out_ref, grad_ref):
        stream = x_ref[...].astype(f32)
        bias = vec[4:5, :] + vec[5:6, :]
        out_ref[...] = stream + (b_ref[0].astype(f32) + b_ref[1].astype(f32)) + bias
        scaled = n_ref[0].astype(f32) + n_ref[1].astype(f32)
        centred = stream - jnp.mean(stream, axis=-1, keepdims=True)
        inverse = lax.rsqrt(jnp.mean(centred * centred, axis=-1, keepdims=True) + norm_eps)
        normal = centred * inverse
        grad_ref[...] = e_ref[...].astype(f32) + inverse * (
            scaled
            - jnp.mean(scaled, axis=-1, keepdims=True)
            - normal * jnp.mean(scaled * normal, axis=-1, keepdims=True)
        )

    rows = 64
    d = x.shape[1]
    one = pl.BlockSpec((rows, d), lambda i: (i, 0))
    two = pl.BlockSpec((2, rows, d), lambda i: (0, i, 0))
    pipeline(
        tokens,
        (x.shape[0] // rows,),
        [(x, one), (e, one), (norm_final, two), (branch_final, two)],
        [(layer_output, one), (input_grad, one)],
    )


def run_update(chunk, rates, x, e, vec, finals, grads, weights):
    flat = [w for group in weights for w in group]
    tokens = jax.ShapeDtypeStruct(x.shape, f32)
    out_shape = [tokens, tokens] + [jax.ShapeDtypeStruct(w.shape, f32) for w in flat]
    return pl.pallas_call(
        functools.partial(update_kernel, chunk, rates),
        out_shape=out_shape,
        in_specs=[ANY, ANY, VMEM] + [ANY] * (6 + len(flat)),
        out_specs=[ANY] * len(out_shape),
        compiler_params=pltpu.CompilerParams(vmem_limit_bytes=48 * 2**20),
        name="update",
    )(x, e, vec, *finals, *grads, *flat)


def make_local(fsdp, tp):
    masks = [1 << b for b in range(2, fsdp.bit_length() - 1)] + [1]
    top = fsdp // 2

    def local(
        layer_input,
        out_cotangent,
        segments,
        qkv_weight,
        qkv_first,
        qkv_second,
        out_weight,
        out_first,
        out_second,
        up_weight,
        up_first,
        up_second,
        down_weight,
        down_first,
        down_second,
        small_params,
        small_first,
        small_second,
    ):
        d = layer_input.shape[1]
        length = segments.shape[1]
        chunk = 2 * down_weight.shape[1]
        lanes = np.arange(128)
        rate = 10000.0 ** (-(2.0 * (lanes % (ROT // 2))) / ROT)
        angle = np.arange(length)[:, None] * rate[None]
        rates = np.broadcast_to(rate, angle.shape)
        table = jnp.asarray(np.concatenate([np.cos(angle), np.sin(angle), rates], 1), f32)
        vec = small_params.reshape(-1, d)
        norm_final, branch_final, up_new, qkv_new, out_new, down_new, small = run_layer(
            masks, top, length, tp, layer_input, out_cotangent, up_weight[0], qkv_weight[0], down_weight[0],
            out_weight[0], segments, table, vec,
        )
        weights = (
            (qkv_weight[0], qkv_first[0], qkv_second[0]),
            (out_weight[0], out_first[0], out_second[0]),
            (up_weight[0], up_first[0], up_second[0]),
            (down_weight[0], down_first[0], down_second[0]),
        )
        results = run_update(
            chunk, (d ** (-0.5), 4.0 * d ** (-0.5)), layer_input, out_cotangent, vec, (norm_final, branch_final),
            (qkv_new, out_new, up_new, down_new), weights,
        )
        small_total = jnp.concatenate([small[0:5], small[4:5], small[5:12]]).reshape(1, -1)
        small_updated = adam_step(small_params, small_first, small_second, small_total, rate_vector, 0.0)
        return (*results[:2], *[w[None] for w in results[2:]], *small_updated)

    return local


def solution(mesh):
    tokens = P(("fsdp", "tp"), None)
    inner = P(None, ("tp", "fsdp"), None)
    qkv = P(None, None, "fsdp", "tp")
    up = P(None, "fsdp", "tp")
    weights = (qkv,) * 3 + (inner,) * 3 + (up,) * 3 + (inner,) * 3 + (P(),) * 3
    return jax.shard_map(
        make_local(mesh.shape["fsdp"], mesh.shape["tp"]),
        mesh=mesh,
        in_specs=(tokens, tokens, P("fsdp", None)) + weights,
        out_specs=(tokens, tokens) + weights,
        check_vma=False,
    )
```

```python
import functools

import jax
import jax.numpy as jnp
import numpy as np
from jax import lax
from jax.experimental import pallas as pl
from jax.experimental.pallas import tpu as pltpu
from jax.sharding import PartitionSpec as P

HD = 256
ROT = 64
STEP = 10

norm_eps = 1e-05
beta_one = 0.9
beta_two = 0.95
adam_eps = 1e-08
decay_rate = 0.01
rate_vector = 0.2
masked_score = -1e30
f32 = jnp.float32
bf16 = jnp.bfloat16


def adam_step(weight, first, second, grad, rate, decay):
    first_new = beta_one * first + (1.0 - beta_one) * grad
    second_new = beta_two * second + (1.0 - beta_two) * grad * grad
    first_hat = first_new / (1.0 - beta_one**STEP)
    second_hat = second_new / (1.0 - beta_two**STEP)
    weight_new = weight - rate * (first_hat / (jnp.sqrt(second_hat) + adam_eps) + decay * weight)
    return (first_new, second_new, weight_new)


MESH = pl.DeviceIdType.MESH


def bit_of(i, mask):
    return (i // mask) % 2


def flip(i, mask):
    return i + mask - 2 * mask * bit_of(i, mask)


class Copy:
    def __init__(self, copy):
        self.copy, self.started, self.received, self.sent = copy, False, False, False

    def start(self):
        self.started = True
        self.copy.start()

    def wait_recv(self):
        self.received = True
        self.copy.wait_recv()

    def wait_send(self):
        self.sent = True
        self.copy.wait_send()


class Local:
    def __init__(self, copy):
        self.copy, self.started, self.done = copy, False, False

    def start(self):
        self.started = True
        self.copy.start()

    def wait(self):
        self.done = True
        self.copy.wait()


class Links:
    def __init__(self, send_sem, recv_sem, local_sem):
        self.send_sem, self.recv_sem, self.local_sem = send_sem, recv_sem, local_sem
        self.copies, self.locals, self.swaps, self.n_local = [], [], [], 0

    def local(self, src, dst):
        c = Local(pltpu.make_async_copy(src, dst, self.local_sem.at[self.n_local]))
        self.n_local += 1
        self.locals.append(c)
        return c

    def copy(self, src, dst, device):
        k = len(self.copies)
        c = Copy(
            pltpu.make_async_remote_copy(
                src_ref=src,
                dst_ref=dst,
                send_sem=self.send_sem.at[k],
                recv_sem=self.recv_sem.at[k],
                device_id=device,
                device_id_type=MESH,
            )
        )
        self.copies.append(c)
        return c

    def drain(self):
        for c in self.copies:
            if c.started and not c.received:
                c.wait_recv()
            if c.started and not c.sent:
                c.wait_send()
        for c in self.locals:
            if c.started and not c.done:
                c.wait()
        for c in self.swaps:
            c.drain()


class Group:
    def __init__(self, links, at, f, t, masks, root):
        self.copies, self.masks = {}, masks
        for key in all_keys(masks):
            g = root
            for mask in masks:
                if key & mask:
                    g = flip(g, mask)
            ref = at(g)
            after = max([i + 1 for i, m in enumerate(masks) if key & m], default=0)
            for mask in masks[after:]:
                self.copies[key | mask] = links.copy(ref, ref, (flip(f, mask), t))

    def low(self):
        self.copies[1].start()

    def high(self):
        self.copies[self.masks[0]].start()

    def rest(self):
        keys = all_keys(self.masks[:-1])
        for s, mask in enumerate(self.masks[1:-1]):
            for key in all_keys(self.masks[: s + 1]):
                if key:
                    self.copies[key].wait_recv()
                self.copies[key | mask].start()
        last = self.masks[-2]
        for key in keys:
            if key & last:
                self.copies[key].wait_recv()
            if key:
                self.copies[key | 1].start()

    def ends(self):
        return [c for key, c in self.copies.items() if key & 1]


def all_keys(masks):
    keys = [0]
    for mask in masks:
        keys = keys + [k | mask for k in keys]
    return keys


def normalise(x, with_inverse=False):
    mean = jnp.mean(x, axis=-1, keepdims=True)
    centred = x - mean
    inverse = lax.rsqrt(jnp.mean(centred * centred, axis=-1, keepdims=True) + norm_eps)
    return (centred * inverse, inverse) if with_inverse else centred * inverse


def rope(u, c, s):
    lane = lax.broadcasted_iota(jnp.int32, u.shape, 1)
    partner = jnp.where(lane < ROT // 2, pltpu.roll(u, 128 - ROT // 2, 1), pltpu.roll(u, ROT // 2, 1))
    return u * c + partner * s


def dot(a, b, dims):
    return lax.dot_general(a, b, (dims, ((), ())), preferred_element_type=f32)


NN = ((1,), (0,))
NT = ((1,), (1,))
TN = ((0,), (0,))
TILE = 256


def pipe(body, steps, ins, outs, hooks=()):
    def whole(*refs):
        for i, n, run in hooks:
            pl.when(pl.program_id(0) == i * steps // n)(run)
        body(*refs)

    pltpu.emit_pipeline(
        whole,
        grid=(steps,),
        in_specs=[spec for _, spec in ins],
        out_specs=[spec for _, spec in outs],
    )(*[ref for ref, _ in ins], *[ref for ref, _ in outs])


def by_rows(ref, index=lambda i: i, rows=TILE):
    return ref, pl.BlockSpec((rows, ref.shape[1]), lambda i: (index(i), 0))


def by_columns(ref, index, width):
    return ref, pl.BlockSpec((ref.shape[0], width), lambda i: (0, index(i)))


def here(i, rows=TILE):
    return pl.ds(pl.multiple_of(i * rows, rows), rows)


def run_cast(weight, index, steps, width, dst):
    def body(w_ref):
        at = pl.ds(pl.multiple_of(pl.program_id(0) * width, width), width)
        dst[:, at] = w_ref[...].astype(bf16)

    pipe(body, steps, [by_columns(weight, index, width)], [])


def run_cast_qkv(weight, half, dst):
    def body(w_ref):
        at = pl.ds(pl.multiple_of(pl.program_id(0) * HD, HD), HD)
        dst[:, at] = w_ref[...].reshape(w_ref.shape[-2:]).astype(bf16)

    spec = pl.BlockSpec((1, weight.shape[1], HD), lambda i: (i, 0, half))
    pipe(body, 3, [(weight, spec)], [])


class Rotary:
    def __init__(self, table, starts, seq):
        self.table, self.starts, self.seq = table, starts, seq

    def bounds(self):
        at = pl.ds(self.seq * 8, 1)
        return self.starts[at, 0:1].astype(jnp.int32), self.starts[at, 1:2].astype(jnp.int32)

    def __call__(self, tile):
        shape = (TILE, 128)
        lane = lax.broadcasted_iota(jnp.int32, (1, 128), 1)
        first, second = self.bounds()
        turning = lane < ROT
        rate = self.table[0:1, 256:384]
        one, two = first.astype(f32) * rate, second.astype(f32) * rate
        index = tile * TILE + lax.broadcasted_iota(jnp.int32, shape, 0)
        pick = lambda a, b, c: jnp.where(index >= second, c, jnp.where(index >= first, b, a))
        cos_b = pick(jnp.ones_like(one), jnp.cos(one), jnp.cos(two))
        sin_b = pick(jnp.zeros_like(one), jnp.sin(one), jnp.sin(two))
        rows = here(tile)
        cos_t, sin_t = self.table[rows, 0:128], self.table[rows, 128:256]
        sign = jnp.where(lane < ROT // 2, -1.0, 1.0)
        c = jnp.where(turning, cos_t * cos_b + sin_t * sin_b, 1.0)
        s = jnp.where(turning, sign * (sin_t * cos_b - cos_t * sin_b), 0.0)
        return c, s


def normed(vec, k, xh, at):
    return (xh[at, :].astype(f32) * vec[2 * k : 2 * k + 1, :] + vec[2 * k + 1 : 2 * k + 2, :]).astype(bf16)


def run_project(vec, qkv_bias, xh, w, rotary, seq, p, steps, hooks=()):
    def body():
        i = pl.program_id(0)
        at = here(seq * steps + i)
        c, s = rotary(i)
        proj = dot(normed(vec, 0, xh, at), w[...], NN) + qkv_bias()
        for j in range(2):
            p[at, j * HD : j * HD + 128] = rope(proj[:, j * HD : j * HD + 128], c, s).astype(bf16)
            p[at, j * HD + 128 : (j + 1) * HD] = proj[:, j * HD + 128 : (j + 1) * HD].astype(bf16)
        p[at, 2 * HD :] = proj[:, 2 * HD :].astype(bf16)

    pipe(body, steps, [], [], hooks)


def run_up(vec, up_bias, xh, w, g, slope, index, steps, hooks=()):
    width = w.shape[1]
    part = min(width, 256)

    def body(g_ref, s_ref):
        n = normed(vec, 1, xh, here(index(pl.program_id(0))))
        for j in range(0, width, part):
            h = dot(n, w[:, j : j + part], NN) + up_bias[0:1, j : j + part]
            cdf = 0.5 + 0.5 * lax.erf(h * 0.7071067811865476)
            g_ref[:, j : j + part] = (h * cdf).astype(bf16)
            s_ref[:, j : j + part] = (cdf + h * (jnp.exp(-0.5 * h * h) * 0.3989422804014327)).astype(bf16)

    pipe(body, steps, [], [by_rows(g, index), by_rows(slope, index)], hooks)


def run_attention(length, seq, rotary, p, da, a, dproj, dk, dv, sums):
    scale = HD ** (-0.5)
    tiles_n = length // TILE
    first, second = rotary.bounds()
    rows = lambda i: here(seq * tiles_n + i)

    def put(i, value, column):
        c, s = rotary(i)
        keep(i, rope(value[:, :128], c, -s), column)
        keep(i, value[:, 128:], column + 128)

    def keep(i, value, column):
        value = value.astype(bf16)
        at = slice(column, column + value.shape[1])
        dproj[rows(i), at] = value
        sums[0:1, at] += jnp.sum(value.astype(f32), axis=0, keepdims=True)

    dk[...] = jnp.zeros_like(dk)
    dv[...] = jnp.zeros_like(dv)
    for i in range(tiles_n):
        n = (i + 1) * TILE
        until = pl.ds(pl.multiple_of(seq * length, length), n)
        q = p[rows(i), 0:HD]
        k = p[until, HD : 2 * HD]
        v = p[until, 2 * HD :]
        rows_da = da[rows(i), :]
        scores = dot(q, k, NT) * scale
        qi = i * TILE + lax.broadcasted_iota(jnp.int32, (TILE, n), 0)
        ki = lax.broadcasted_iota(jnp.int32, (TILE, n), 1)
        start = jnp.where(qi >= second, second, jnp.where(qi >= first, first, 0))
        scores = jnp.where((ki <= qi) & (ki >= start), scores, masked_score)
        peak = jnp.max(scores, axis=-1, keepdims=True)
        raised = jnp.exp(scores - peak)
        probs = raised * (1.0 / jnp.sum(raised, axis=-1, keepdims=True))
        weights = probs.astype(bf16)
        a[rows(i), :] = dot(weights, v, NN).astype(bf16)
        prob_grad = dot(rows_da, v, NT)
        delta = jnp.sum(probs * prob_grad, axis=-1, keepdims=True)
        score_grad = (probs * (prob_grad - delta)).astype(bf16)
        put(i, dot(score_grad, k, NN) * scale, 0)
        dk[0:n, :] += dot(score_grad, q, TN)
        dv[0:n, :] += dot(weights, rows_da, TN)
    for i in range(tiles_n):
        local = slice(i * TILE, (i + 1) * TILE)
        put(i, dk[local, :] * scale, HD)
        keep(i, dv[local, :], 2 * HD)


def column_of(row):
    return jnp.broadcast_to(row, (128, row.shape[1])).T[:, 0:1]


def row_of(column):
    return jnp.broadcast_to(column, (column.shape[0], 128)).T[0:1, :]


class Through:
    def __init__(self, vec, k, w, d_sum, sums):
        self.vec, self.k, self.w, self.d_sum, self.sums = vec, k, w, d_sum, sums

    def __call__(self, value, index):
        n = value.shape[0]
        at = here(index, n)
        w = self.w[at, :].astype(f32)
        total = self.d_sum[0:1, :]
        self.sums[2 * self.k : 2 * self.k + 1, at] = row_of(jnp.sum(w * value, axis=1, keepdims=True))
        self.sums[2 * self.k + 1 : 2 * self.k + 2, at] = row_of(jnp.sum(w * total, axis=1, keepdims=True))
        gain = column_of(self.vec[2 * self.k : 2 * self.k + 1, at])
        shift = column_of(self.vec[2 * self.k + 1 : 2 * self.k + 2, at])
        return value * gain + shift * total


def run_outer(a, b, out, index_in, index_out, steps, width, add=None, through=None, hooks=()):
    def body(*refs):
        index = index_in(pl.program_id(0))
        left = a[:, here(index, width)] if through else refs[0][...]
        value = dot(left, b[...], TN)
        if through:
            value = through(value, index)
        if add is not None:
            value = value + refs[-2][...].astype(f32)
        refs[-1][...] = value.astype(bf16)

    ins = [] if through else [by_columns(a, index_in, width)]
    if add is not None:
        ins.append(by_rows(add, index_out, width))
    pipe(body, steps, ins, [by_rows(out, index_out, width)], hooks)


def run_outer_wide(a, b, out):
    width = 2 * TILE

    def body(out_ref):
        at = pl.ds(pl.multiple_of(pl.program_id(0) * width, width), width)
        out_ref[...] = dot(a[...], b[:, at], TN).astype(bf16)

    pipe(body, b.shape[1] // width, [], [by_columns(out, lambda i: i, width)])


def run_hidden_grad(e, w, slope, dh, bias_sum, index, steps, hooks=()):
    def body(s_ref):
        at = here(index(pl.program_id(0)))
        value = (dot(e[at, :], w[...], NT) * s_ref[...].astype(f32)).astype(bf16)
        dh[at, :] = value
        bias_sum[0:1, :] += jnp.sum(value.astype(f32), axis=0, keepdims=True)

    pipe(body, steps, [by_rows(slope, index)], [], hooks)


def run_norm_grad(vec, dh, w_up, dproj, w_qkv):
    def tile(at):
        one = dot(dproj[at, :], w_qkv[...], NT)
        two = dot(dh[at, :], w_up[...], NT)
        return one * vec[0:1, :] + two * vec[2:3, :]

    return None, tile


def run_branch(a, w_out, g, w_down):
    def tile(at, g_ref):
        return dot(a[at, :], w_out[...], NN) + dot(g_ref[...], w_down[...], NN)

    return g, tile


def run_token_tiles(job, out, index, index_out, steps, add=None, hooks=()):
    source, tile = job

    def body(*refs):
        value = tile(here(index(pl.program_id(0))), *([] if source is None else refs[:1]))
        if add is not None:
            value = value + refs[-2][...].astype(f32)
        refs[-1][...] = value.astype(bf16)

    ins = [] if source is None else [by_rows(source, index)]
    if add is not None:
        ins.append(by_rows(add, index_out))
    pipe(body, steps, ins, [by_rows(out, index_out)], hooks)


def run_add(a, b, out):
    rows, cols = out.shape
    step = min(rows, TILE)

    def body(a_ref, b_ref, out_ref):
        out_ref[...] = (a_ref[...].astype(f32) + b_ref[...].astype(f32)).astype(bf16)

    pipe(body, rows // step, [by_rows(a, rows=step), by_rows(b, rows=step)], [by_rows(out, rows=step)])


def block(ref, index, rows):
    return ref.at[pl.ds(pl.multiple_of(index * rows, rows), rows)]


def out_place(g, top):
    return (((g // 4) % (top // 4)) * 2 + g // top) * 2 + g % 2


class Scatter:
    def __init__(self, links, part, place, rows, mids, recv, sums, f, t, masks):
        self.links, self.part, self.place, self.rows, self.mids = links, part, place, rows, mids
        self.recv, self.sums, self.f, self.t = recv, sums, f, t
        self.stages = [1] + [m for m in reversed(masks) if m != 1]
        self.n_hi = 1 << (len(masks) - 1)
        self.hi, self.lo, self.mid = f // 4, f % 2, bit_of(f, 2)
        self.half = self.hi % 2
        self.to = None
        self.copies = {}
        for k in range(self.n_hi):
            for j, m in enumerate(mids):
                self.copies[0, k, j] = links.copy(
                    block(part, self.at_place(self.high(k), m, 1 - self.lo), rows),
                    block(recv[0], self.slot(0, k, j), rows),
                    (flip(f, 1), t),
                )
        for level in range(len(self.stages) - 1):
            n = self.n_hi >> (level + 1)
            for k in range(n, 2 * n):
                for j in range(len(mids)):
                    self.copies[level + 1, k - n, j] = links.copy(
                        block(sums[level], self.slot(level, k, j), rows),
                        block(recv[level + 1], self.slot(level + 1, k, j), rows),
                        (flip(f, self.stages[level + 1]), t),
                    )

    def high(self, k):
        hi, b = self.hi, 1
        while b < self.n_hi:
            if k & b:
                hi = flip(hi, b)
            b *= 2
        return hi

    def slot(self, level, k, j):
        n = self.n_hi >> level
        i = (self.high(k) % n) if n > 1 else 0
        return i * len(self.mids) + j

    def at_place(self, hi, m, lo):
        return self.place((hi * 2 + (self.mid if m is None else m)) * 2 + lo)

    def ks(self, far):
        half = self.n_hi // 2
        return range(half, self.n_hi) if far else range(half)

    def each(self, far):
        return [(k, j) for k in self.ks(far) for j in range(len(self.mids))]

    def tile(self, i, far, lo):
        n = len(self.mids)
        half = self.n_hi // 2
        upper = self.hi // half
        hi = (1 - upper if far else upper) * half + i // n
        j = i % n
        m = None if self.mids[0] is None else j
        return self.at_place(hi, m, lo), hi * n + j

    def add(self, level, k, j):
        mine = (
            block(self.part, self.at_place(self.high(k), self.mids[j], self.lo), self.rows)
            if level == 0
            else block(self.sums[level - 1], self.slot(level - 1, k, j), self.rows)
        )
        at = self.slot(level, k, j)
        run_add(mine, block(self.recv[level], at, self.rows), block(self.sums[level], at, self.rows))

    def first_adds(self, far):
        for k, j in self.each(far):
            self.add(0, k, j)

    def finish(self, waited):
        if waited:
            if len(self.mids) == 1:
                self.add(1, 0, 0)
            else:
                other = 1 - self.mid
                at = self.half * 2 + other
                to = block(self.sums[1], other, self.rows) if self.to is None else self.to
                run_add(block(self.sums[0], at, self.rows), block(self.recv[1], other, self.rows), to)
            return
        for level in range(1, len(self.stages)):
            n = self.n_hi >> level
            for k in reversed(range(n)):
                for j in range(len(self.mids)):
                    self.copies[level, k, j].wait_recv()
                    self.add(level, k, j)
                    if level + 1 < len(self.stages) and k & (n // 2):
                        self.copies[level + 1, k - n // 2, j].start()
        if self.to is not None:
            self.links.local(block(self.sums[-1], 1 - self.mid, self.rows), self.to).start()


class Outer:
    def __init__(self, scatter, a, b, through=None):
        self.s, self.a, self.b, self.through = scatter, a, b, through
        self.fused = scatter.rows % 128 == 0
        self.steps = scatter.n_hi // 2 * len(scatter.mids)

    def give(self, far, hooks=()):
        s = self.s
        if self.fused:
            at = lambda i: s.tile(i, far, 1 - s.lo)[0]
            run_outer(self.a, self.b, s.part, at, at, self.steps, s.rows, through=self.through, hooks=hooks)
        elif far:
            same = lambda i: i
            run_outer(self.a, self.b, s.part, same, same, self.a.shape[1] // 128, 128, through=self.through, hooks=hooks)

    def keep(self, far, hooks=()):
        s = self.s
        if self.fused:
            at = lambda i: s.tile(i, far, s.lo)[0]
            to = lambda i: s.tile(i, far, s.lo)[1]
            run_outer(
                self.a, self.b, s.sums[0], at, to, self.steps, s.rows, add=s.recv[0], through=self.through, hooks=hooks
            )
        else:
            s.first_adds(far)


class Tokens:
    def __init__(self, links, refs, rows, f, t, job):
        self.give_buf, self.got, self.sum, self.got_y, self.sum_y, self.final = refs
        self.rows, self.mid, self.y, self.core, self.job = rows, bit_of(f, 2), t // 2, t % 2, job
        core_peer, y_peer, mid_peer = (f, flip(t, 1)), (f, flip(t, 2)), (flip(f, 2), t)
        self.over_core = [
            links.copy(block(self.give_buf, i, rows), block(self.got, i, rows), core_peer) for i in range(4)
        ]
        self.over_y = [
            links.copy(block(self.sum, m * 2 + 1 - self.y, rows), block(self.got_y, m, rows), y_peer)
            for m in range(2)
        ]
        self.over_mid = [links.copy(block(self.sum_y, 1 - self.mid, rows), self.final, mid_peer)]

    def give(self, hooks=()):
        index = lambda i: (i // 2) * 4 + (i % 2) * 2 + 1 - self.core
        run_token_tiles(self.job, self.give_buf, index, lambda i: i, 4, hooks=hooks)

    def keep(self, far, hooks=()):
        yy = 1 - self.y if far else self.y
        index = lambda i: i * 4 + yy * 2 + self.core
        run_token_tiles(self.job, self.sum, index, lambda i: i * 2 + yy, 2, add=self.got, hooks=hooks)

    def across(self):
        m = 1 - self.mid
        run_add(block(self.sum, m * 2 + self.y, self.rows), block(self.got_y, m, self.rows), block(self.sum_y, m, self.rows))


def greet(f, t, masks, top):
    mid = bit_of(f, 2)
    swapped = f + (top - 2) * (mid - bit_of(f, top))
    barrier = pltpu.get_barrier_semaphore()
    peers = [(flip(f, m), t) for m in masks + [2]] + [(f, flip(t, 1)), (f, flip(t, 2))]
    for peer in peers:
        pl.semaphore_signal(barrier, inc=1, device_id=peer, device_id_type=MESH)

    @pl.when(swapped != f)
    def _():
        pl.semaphore_signal(barrier, inc=1, device_id=(swapped, t), device_id_type=MESH)

    pl.semaphore_wait(barrier, len(peers) + (mid + bit_of(f, top)) % 2)
    return swapped


class Swap:
    def __init__(self, links, src, dst, stay, f, t, swapped):
        self.move = links.copy(src, dst, (swapped, t)).copy
        self.copy = pltpu.make_async_copy(src, stay, links.local_sem.at[links.n_local])
        links.n_local += 1
        links.swaps.append(self)
        self.moves, self.stays = swapped != f, swapped == f
        self.started, self.done = False, False

    def start(self):
        self.started = True
        pl.when(self.moves)(self.move.start)
        pl.when(self.stays)(self.copy.start)

    def wait(self):
        self.done = True
        pl.when(self.moves)(self.move.wait_recv)
        pl.when(self.stays)(self.copy.wait)

    def drain(self):
        if self.started and not self.done:
            self.wait()
        if self.started:
            pl.when(self.moves)(self.move.wait_send)


class Plan:
    def __init__(self):
        self.actions, self.waits = {}, {}

    def send(self, name, needs, starts, *copies):
        self.actions[name] = (None, needs, starts)
        self.waits[name] = copies

    def compute(self, name, needs, run):
        self.actions[name] = (True, needs, run)

    def pending(self, name):
        found = []
        for need in self.actions[name][1]:
            found += self.waits.pop(need, ())
        return found

    def starter(self, name):
        pending, starts = self.pending(name), self.actions[name][2]

        def run():
            for c in pending:
                c()
            for start in starts:
                start()

        return run

    def carry_out(self, order):
        i = 0
        while i < len(order):
            name = order[i]
            i += 1
            compute, _, run = self.actions[name]
            if not compute:
                self.starter(name)()
                continue
            for wait in self.pending(name):
                wait()
            n = 1 + order[i:].count(name)
            hooks = []
            for part in range(1, n):
                while order[i] != name:
                    hooks.append((part, n, self.starter(order[i])))
                    i += 1
                i += 1
            run(hooks) if n > 1 else run(())


ORDER = [
    "es_m", "cast_up", "norm_own", "es_c", "cast_qkv", "qkv_first", "xs_c", "cast_out", "out_swap",
    "cast_down", "qkv_own_zh", "down0_x", "up_own_x", "es_y", "qkv_mid_x", "qkv_mid_zh", "xs_y", "down0_zh",
    "xs_m", "es_yc", "qkv_own_zhx", "es_my", "down1_x", "qkv_own_x", "out_zh", "out_x", "es_mc", "out_zhx",
    "up_first", "xs_yc", "qkv_mid_zhx", "up_own_zh", "xs_my", "es_myc", "xs_mc", "da_own", "down0_zhx",
    "up_mid_zh", "up_mid_x", "da_oth", "proj_own", "proj_own", "xs_myc", "up_own_zhx", "proj_own", "proj_own",
    "attn_own", "proj_oth", "proj_oth", "proj_oth", "proj_oth", "attn_oth", "up_mid_zhx", "gout", "down1_zh",
    "gqkv_gn", "gqkv_gn", "gqkv_gf", "gout_f", "gqkv_gf", "gqkv_f", "up_oth", "up_oth", "up_oth", "up_oth",
    "gout_kf", "up_own", "gout_on", "up_own", "down1_zhx", "up_own", "up_own", "gdown_gf", "gqkv_kf",
    "gqkv_kf", "gdown_f", "gqkv_on", "branch_g", "branch_g", "branch_g", "branch_g", "branch_c", "dh_oth",
    "dh_oth", "dh_oth", "dh_oth", "dh_own", "gqkv_n", "dh_own", "dh_own", "dh_own", "branch_kf", "branch_kf",
    "branch_y", "gdown_kf", "gdown_on", "gup_gf", "gup_gf", "gup_f", "norm_g", "norm_g", "norm_g", "norm_g",
    "gqkv_kn", "gqkv_kn", "gup_gn", "norm_c", "gup_gn", "gqkv_add", "gup_n", "gqkv_x", "branch_kn",
    "branch_kn", "norm_kf", "norm_kf", "gup_kf", "norm_y", "gup_kf", "gup_on", "branch_aa", "branch_m",
    "gout_n", "gdown_gn", "gup_kn", "gup_kn", "small0", "gout_kn", "gdown_n", "norm_kn", "small1", "small2",
    "norm_kn", "gout_add", "small3", "norm_aa", "norm_m", "gdown_kn", "small4", "gout_x", "gup_add",
    "small_end",
]

N_HBM = 6


def layer_kernel(
    masks, top, length,
    e, up, qkv, down, out, seg, table, x, vec,
    *rest,
):
    n_stage = len(masks)
    (g, slope, g_qkv, g_out, g_down, g_up), rest = rest[:N_HBM], rest[N_HBM:]
    stage_refs = []
    for _ in range(4):
        stage_refs.append((rest[:n_stage], rest[n_stage : 2 * n_stage]))
        rest = rest[2 * n_stage :]
    token_refs, rest = [rest[:6], rest[6:12]], rest[12:]
    (up_new, qkv_new, out_new, small), rest = rest[:4], rest[4:]
    (
        xh, ea, upa, qkva, downa, outa, up16, qkv16, out16, p, da, a, dproj, dh, dk, dv,
        sums, qkv_sum, bias_sum, up_bias, starts, small_in,
        send_sem, recv_sem, local_sem,
    ) = rest
    f = lax.axis_index("fsdp")
    t = lax.axis_index("tp")
    mid = bit_of(f, 2)
    rows, d = x.shape
    feat, sub, orow = up.shape[0], down.shape[0], out.shape[0]
    mine = upa.shape[1]
    chunk = 2 * sub
    hi_n = mine // chunk
    swapped = greet(f, t, masks, top)
    links = Links(send_sem, recv_sem, local_sem)
    plan = Plan()

    mid_peer, y_peer, core_peer = (flip(f, 2), t), (f, flip(t, 2)), (f, flip(t, 1))
    qkv_block = lambda i: block(qkva, i, feat)
    up_block = lambda i: block(upa, i, feat)
    half_sub = sub // 2
    out_block = lambda i: block(outa, out_place(i, top), orow)
    tok = lambda buf, m, j: block(buf, m * 4 + j, rows)

    def sends(name, needs, *copies):
        plan.send(name, needs, [c.start for c in copies], *[c.wait_recv for c in copies])

    own_e = links.local(e, tok(ea, mid, t))
    for prefix, source, buf in (("xs", None, xh), ("es", e, ea)):
        for name, needs, m, j, peer in (
            ("m", (), mid, t, mid_peer),
            ("y", (), mid, t, y_peer),
            ("c", (), mid, t, core_peer),
            ("my", ("m",), 1 - mid, t, y_peer),
            ("mc", ("m",), 1 - mid, t, core_peer),
            ("yc", ("y",), mid, flip(t, 2), core_peer),
            ("myc", ("my",), 1 - mid, flip(t, 2), core_peer),
        ):
            ref = tok(buf, m, j)
            c = links.copy(ref if needs or source is None else source, ref, peer)
            sends(prefix + "_" + name, [prefix + "_" + n for n in needs], c)
    plan.waits["own_e"] = (own_e.wait,)
    own_e.start()

    def spreads(name, group, need):
        sends(name + "_x", need, group.copies[1])
        plan.send(name + "_zh", need, [group.high], *([group.copies[masks[0]].wait_recv] if n_stage == 2 else []))
        if n_stage == 2:
            sends(name + "_zhx", [name + "_zh"], group.copies[masks[0] | 1])
        else:
            plan.send(name + "_zhx", [], [group.rest], *[c.wait_recv for c in group.ends() if c is not group.copies[1]])

    first_up = links.copy(up16, up_block(f), mid_peer)
    first_qkv = links.copy(qkv16, qkv_block(f), mid_peer)
    sends("up_first", [], first_up)
    sends("qkv_first", [], first_qkv)
    spreads("up_own", Group(links, up_block, f, t, masks, f), [])
    spreads("up_mid", Group(links, up_block, f, t, masks, flip(f, 2)), ["up_first"])
    spreads("qkv_own", Group(links, qkv_block, f, t, masks, f), [])
    spreads("qkv_mid", Group(links, qkv_block, f, t, masks, flip(f, 2)), ["qkv_first"])
    for h in range(2):
        at = lambda i, h=h: block(downa, ((i // 4) * 2 + i % 2) * 2 + h, half_sub)
        spreads("down" + str(h), Group(links, at, f, t, masks, f), [])
    out_in = Swap(links, out16, out_block(swapped), out_block(f), f, t, swapped)
    plan.send("out_swap", [], [out_in.start], out_in.wait)
    spreads("out", Group(links, out_block, f, t, masks, f), ["out_swap"])
    other_starts = links.copy(starts.at[pl.ds(0, 8)], starts.at[pl.ds(8, 8)], mid_peer)

    segments = seg[0:1, :]
    count = lambda n: jnp.sum((segments < n).astype(f32), axis=1, keepdims=True)
    lane = lax.broadcasted_iota(jnp.int32, (8, 128), 1)
    starts[0:8, :] = jnp.where(lane == 0, count(1), count(2))
    other_starts.start()
    for ref in (sums, qkv_sum, bias_sum):
        ref[...] = jnp.zeros_like(ref)
    for h in range(hi_n):
        at = pl.ds(pl.multiple_of((h * 2 + mid) * chunk, chunk), chunk)
        up_bias[0:1, h * chunk : (h + 1) * chunk] = sum(
            jnp.where(t == j, vec[9 + j : 10 + j, at], 0.0) for j in range(4)
        )
    head = pl.ds(pl.multiple_of((t * 2 + mid) * HD, HD), HD)
    qkv_bias = lambda: jnp.concatenate([vec[6 + c : 7 + c, head] for c in range(3)], axis=1)

    def cast_qkv(hooks):
        run_cast_qkv(qkv, 1 - mid, qkv16)
        run_cast_qkv(qkv, mid, qkv_block(f))

    def cast_up(hooks):
        run_cast(up, lambda i: i * 2 + 1 - mid, hi_n, chunk, up16)
        run_cast(up, lambda i: i * 2 + mid, hi_n, chunk, up_block(f))

    def norm_own(hooks):
        xh[here(mid * 4 + t, rows), :] = normalise(x[...].astype(f32)).astype(bf16)

    plan.compute("norm_own", [], norm_own)
    plan.compute("cast_qkv", [], cast_qkv)
    plan.compute("cast_up", [], cast_up)
    down_rows = block(downa, (f // 4) * 2 + f % 2, sub)
    plan.compute("cast_down", [], lambda hooks: run_cast(down, lambda i: i, 2, d // 2, down_rows))
    plan.compute("cast_out", [], lambda hooks: run_cast(out, lambda i: i, 1, d, out16))

    per_seq = length // TILE
    names = lambda prefix, *ends: [prefix + "_" + end for end in ends]
    of_up = names("up", "own_x", "own_zhx", "mid_x", "mid_zhx")
    of_qkv = names("qkv", "own_x", "own_zhx", "mid_x", "mid_zhx")
    of_down = ["down0_x", "down0_zhx", "down1_x", "down1_zhx"]
    of_out = ["out_x", "out_zhx"]
    plan.waits["starts"] = (other_starts.wait_recv,)
    for which, seq, arrive in (("own", mid, ("c", "y", "yc")), ("oth", 1 - mid, ("m", "mc", "my", "myc"))):
        own = which == "own"
        rotary = Rotary(table, starts, 0 if own else 1)
        index = lambda i, seq=seq: seq * per_seq + i
        es = names("es", *arrive) + ["own_e"]
        xs = names("xs", *arrive)
        plan.compute(
            "up_" + which,
            of_up + xs,
            lambda hooks, index=index: run_up(vec, up_bias, xh, upa, g, slope, index, per_seq, hooks),
        )
        plan.compute(
            "proj_" + which,
            of_qkv + xs + ["starts"],
            lambda hooks, seq=seq, rotary=rotary: run_project(vec, qkv_bias, xh, qkva, rotary, seq, p, per_seq, hooks),
        )

        def back(hooks, index=index):
            for i in range(per_seq):
                at = here(index(i))
                da[at, :] = dot(ea[at, :], outa[...], NT).astype(bf16)

        plan.compute("da_" + which, of_out + es, back)
        plan.compute(
            "attn_" + which,
            [],
            lambda hooks, seq=seq, rotary=rotary: run_attention(
                length, seq, rotary, p, da, a, dproj, dk, dv, qkv_sum
            ),
        )
        plan.compute(
            "dh_" + which,
            of_down + es,
            lambda hooks, index=index: run_hidden_grad(ea, downa, slope, dh, bias_sum, index, per_seq, hooks),
        )
    all_es = names("es", "c", "y", "yc", "m", "mc", "my", "myc") + ["own_e"]

    same = lambda i: i
    down_place = lambda i: (i // 4) * 2 + i % 2

    def scatter(name, part, place, height, mids, refs):
        s = Scatter(links, part, place, height, mids, *refs, f, t, masks)
        for far, end in ((True, "_f"), (False, "_n")):
            sends(name + end, [], *[s.copies[0, k, j] for k, j in s.each(far)])
        half = s.n_hi // 2
        sends(name + "_on", [], *[s.copies[1, k - half, j] for k, j in s.each(True)])
        plan.compute(name + "_add", [name + "_on"] if n_stage == 2 else [], lambda hooks: s.finish(n_stage == 2))
        return s

    def outer(name, s, left, right, needs, through=None):
        o = Outer(s, left, right, through)
        plan.compute(name + "_gf", needs, lambda hooks: o.give(True, hooks))
        plan.compute(name + "_gn", needs, lambda hooks: o.give(False, hooks))
        plan.compute(name + "_kf", [name + "_f"], lambda hooks: o.keep(True, hooks))
        plan.compute(name + "_kn", [name + "_n"], lambda hooks: o.keep(False, hooks))

    qkv_s = scatter("gqkv", g_qkv, same, feat, (0, 1), stage_refs[0])
    out_s = scatter("gout", g_out, lambda i: out_place(i, top), orow, (None,), stage_refs[1])
    down_s = scatter("gdown", g_down, down_place, sub, (None,), stage_refs[2])
    up_s = scatter("gup", g_up, same, feat, (0, 1), stage_refs[3])
    up_s.to = up_new
    outer("gdown", down_s, g, ea, all_es)
    outer("gqkv", qkv_s, xh, dproj, [], Through(vec, 0, qkva, qkv_sum, sums))
    outer("gup", up_s, xh, dh, [], Through(vec, 1, upa, bias_sum, sums))
    plan.compute("gout", all_es, lambda hooks: run_outer_wide(a, ea, g_out))
    plan.compute("gout_kf", ["gout_f"], lambda hooks: out_s.first_adds(True))
    plan.compute("gout_kn", ["gout_n"], lambda hooks: out_s.first_adds(False))
    out_back = Swap(links, out_s.sums[-1], out_new, out_new, f, t, swapped)
    plan.send("gout_x", [], [out_back.start], out_back.wait)

    def exchange_columns(name, job, dst):
        total = job.sums[-1]
        c = links.copy(block(total, 1 - mid, feat), dst, mid_peer)
        sends(name, [], c)

    exchange_columns("gqkv_x", qkv_s, qkv_new)

    norm_t = Tokens(links, token_refs[0], rows, f, t, run_norm_grad(vec, dh, upa, dproj, qkva))
    branch_t = Tokens(links, token_refs[1], rows, f, t, run_branch(a, outa, g, downa))
    for name, job, needs in (("norm", norm_t, []), ("branch", branch_t, of_down + of_out)):
        plan.compute(name + "_g", needs, lambda hooks, job=job: job.give(hooks))
        sends(name + "_c", [], *job.over_core)
        plan.compute(name + "_kf", [name + "_c"], lambda hooks, job=job: job.keep(True, hooks))
        plan.compute(name + "_kn", [name + "_c"], lambda hooks, job=job: job.keep(False, hooks))
        sends(name + "_y", [], *job.over_y)
        plan.compute(name + "_aa", [name + "_y"], lambda hooks, job=job: job.across())
        sends(name + "_m", [], *job.over_mid)

    small_peers = [core_peer, y_peer, mid_peer] + [(flip(f, m), t) for m in masks]
    small_copies = [links.copy(small, small_in.at[r], peer) for r, peer in enumerate(small_peers)]

    def small_fill():
        small[...] = jnp.zeros_like(small)
        small[0:4, :] = sums[0:4, :]
        small[4:5, :] = jnp.sum(ea[here(mid * 4 + t, rows), :].astype(f32), axis=0, keepdims=True)
        for c in range(3):
            small[5 + c : 6 + c, head] = qkv_sum[0:1, c * HD : (c + 1) * HD]
        for h in range(hi_n):
            at = pl.ds(pl.multiple_of((h * 2 + mid) * chunk, chunk), chunk)
            for j in range(4):
                small[8 + j : 9 + j, at] = jnp.where(t == j, bias_sum[0:1, h * chunk : (h + 1) * chunk], 0.0)
        small_copies[0].start()

    def small_add(r):
        small_copies[r].wait_send()
        small[...] += small_in[r]

    def small_step(r):
        small_add(r - 1)
        small_copies[r].start()

    def small_end(hooks):
        small_add(4)
        for r in range(5, len(small_peers)):
            small_copies[r].start()
            small_copies[r].wait_recv()
            small_add(r)

    plan.send("small0", [], [small_fill], small_copies[0].wait_recv)
    for r in range(1, 5):
        name = "small" + str(r)
        step = functools.partial(small_step, r)
        plan.send(name, ["small" + str(r - 1)], [step], small_copies[r].wait_recv)
    plan.compute("small_end", ["small4"], small_end)

    plan.carry_out(ORDER)
    links.drain()


ANY = pl.BlockSpec(memory_space=pl.ANY)
VMEM = pl.BlockSpec(memory_space=pltpu.VMEM)


def run_layer(masks, top, length, tp, x, e, up, qkv, down, out, seg, table, vec):
    rows, d = x.shape
    tokens = 2 * tp * rows
    mine, wide = up.shape[1] // 2, 3 * HD
    feat, sub, orow = up.shape[0], down.shape[0], out.shape[0]
    n_keys = 1 << len(masks)
    hi_n = n_keys // 2
    shapes = [
        (tokens, mine), (tokens, mine), (d, wide), (HD, d), (mine, d), (d, mine),
    ]
    copies = 2 * 7 + 2 * (1 + 2 * (n_keys - 1)) + 2 * (n_keys - 1) + n_keys + 1
    for height, width, mids in ((feat, wide, 2), (orow, d, 1), (sub, d, 1), (feat, mine, 2)):
        for _ in range(2):
            for level in range(len(masks)):
                shapes.append(((hi_n >> level) * mids * height, width))
        copies += (2 * hi_n - 1) * mids + 1
    for _ in range(2):
        shapes += [(4 * rows, d)] * 3 + [(2 * rows, d)] * 2 + [(rows, d)]
        copies += 7
    shapes += [(feat, mine), (feat, wide), (orow, d)]
    n_small = len(masks) + 3
    copies += n_small
    out_shape = [jax.ShapeDtypeStruct(shape, bf16) for shape in shapes]
    out_shape.append(jax.ShapeDtypeStruct((16, d), f32))
    held = [
        (tokens, d), (tokens, d), (d, mine), (d, wide), (mine, d), (HD, d), (feat, mine), (feat, wide), (orow, d),
        (tokens, wide), (tokens, HD), (tokens, HD), (tokens, wide), (tokens, mine),
    ]
    result = pl.pallas_call(
        functools.partial(layer_kernel, masks, top, length),
        out_shape=out_shape,
        in_specs=[ANY] * 5 + [VMEM] * 4,
        out_specs=[ANY] * len(shapes) + [VMEM],
        scratch_shapes=[pltpu.VMEM(shape, bf16) for shape in held]
        + [
            pltpu.VMEM(shape, f32)
            for shape in (
                (length, HD), (length, HD), (8, d), (8, wide), (8, mine), (8, mine), (16, 128),
                (n_small, 16, d),
            )
        ]
        + [
            pltpu.SemaphoreType.DMA((copies,)),
            pltpu.SemaphoreType.DMA((copies,)),
            pltpu.SemaphoreType.DMA((8,)),
        ],
        compiler_params=pltpu.CompilerParams(
            collective_id=0, has_side_effects=True, vmem_limit_bytes=60 * 2**20
        ),
        name="layer",
    )(e, up, qkv, down, out, seg, table, x, vec)
    stage = len(masks)
    at = N_HBM + 2 * stage * 4
    up_new, qkv_new, out_new, small = result[at + 12 : at + 16]

    def last(i):
        first = N_HBM + 2 * stage * i
        recv, sums = result[first : first + stage], result[first + stage : first + 2 * stage]
        return (sums[0], recv[1]) if stage == 2 else (sums[-1],)

    norm, branch = result[at : at + 6], result[at + 6 : at + 12]
    tokens = [(part[2], part[3], part[5]) for part in (norm, branch)]
    return tokens, (last(0), qkv_new), out_new, (last(3), up_new), last(2), small


class Moves:
    def __init__(self, sem):
        self.sem, self.count, self.out = sem, 0, []

    def copy(self, src, dst):
        c = pltpu.make_async_copy(src, dst, self.sem.at[self.count])
        self.count += 1
        c.start()
        return c

    def load(self, pairs):
        return [self.copy(src, dst) for src, dst in pairs]

    def store(self, pairs):
        self.out += [self.copy(src, dst) for src, dst in pairs]

    def drain(self):
        for c in self.out:
            c.wait()


def adam_loop(bufs, grads, rate, steps, at):
    w, m, v = bufs

    @pl.loop(0, steps)
    def _(i):
        to, of = at(i)
        g = sum(grad[of].astype(f32) for grad in grads)
        m_new, v_new, w_new = adam_step(w[to], m[to], v[to], g, rate, decay_rate)
        w[to] = w_new
        m[to] = m_new
        v[to] = v_new


ROWS = 32


def by_chunks(i):
    at = here(i, ROWS)
    return at, at


def last_blocks(refs, first, second, rows):
    return [block(ref, i, rows) for ref, i in zip(refs, (second,) if len(refs) == 1 else (first, second))]


def columns_of(ref, q, chunk):
    n = ref.shape[1] // (2 * chunk)
    return [ref.at[:, pl.ds(pl.multiple_of((h * 2 + q) * chunk, chunk), chunk)] for h in range(n)]


def side_by_side(buf, chunk):
    return [buf.at[:, h * chunk : (h + 1) * chunk] for h in range(buf.shape[1] // chunk)]


def update_kernel(chunk, rates, n, *refs):
    take = lambda k: [refs.pop(0) for _ in range(k)]
    refs = list(refs)
    qkv, out, up, down = take(3), take(3), take(3), take(3)
    qkv_last, up_last, down_last, (qkv_new, out_new) = take(n), take(n), take(n), take(2)
    qkv_o, out_o, up_o, down_o = take(3), take(3), take(3), take(3)
    qkv_b, out_b, up_b, down_b = take(3), take(3), take(3), take(3)
    qkv_g, up_g, down_g, (qkv_n, out_n) = take(n), take(n), take(n), take(2)
    moves = Moves(refs.pop(0))
    f = lax.axis_index("fsdp")
    mid, half = bit_of(f, 2), bit_of(f, 4)
    feat, sub = up[0].shape[0], down[0].shape[0]
    rate, rate_out = rates
    pair = (half * 2 + mid, mid)
    loads = {}
    loads["qkv"] = moves.load(
        [*zip(qkv, qkv_b), *zip(last_blocks(qkv_last, *pair, feat), qkv_g), (qkv_new, qkv_n)]
    )
    loads["down"] = moves.load([*zip(down, down_b), *zip(last_blocks(down_last, half, 0, sub), down_g)])
    loads["up"] = moves.load(
        [
            move
            for src, dst in zip(up, up_b)
            for move in zip(columns_of(src, mid, chunk), side_by_side(dst, chunk))
        ]
        + [*zip(last_blocks(up_last, *pair, feat), up_g)]
    )
    loads["out"] = moves.load([*zip(out, out_b), (out_new, out_n)])

    def arrive(name):
        for c in loads[name]:
            c.wait()

    arrive("qkv")
    for c in range(3):
        for q, grads in ((mid, qkv_g), (1 - mid, [qkv_n])):

            def at(i, c=c, q=q):
                rows = here(i, ROWS)
                return (c, rows, pl.ds(pl.multiple_of(q * HD, HD), HD)), (rows, slice(c * HD, (c + 1) * HD))

            adam_loop(qkv_b, grads, rate, feat // ROWS, at)
    moves.store(zip((qkv_b[1], qkv_b[2], qkv_b[0]), qkv_o))
    arrive("down")
    adam_loop(down_b, down_g, rate, sub // ROWS, by_chunks)
    moves.store(zip((down_b[1], down_b[2], down_b[0]), down_o))
    arrive("up")
    adam_loop(up_b, up_g, rate, feat // ROWS, by_chunks)
    moves.store(
        [
            move
            for src, dst in zip((up_b[1], up_b[2], up_b[0]), up_o)
            for move in zip(side_by_side(src, chunk), columns_of(dst, mid, chunk))
        ]
    )
    arrive("out")
    rows = min(out[0].shape[0], ROWS)
    adam_loop(out_b, [out_n], rate_out, out[0].shape[0] // rows, lambda i: (here(i, rows), here(i, rows)))
    moves.store(zip((out_b[1], out_b[2], out_b[0]), out_o))
    moves.drain()


def finish_kernel(chunk, rate, x, e, vec, *refs):
    take = lambda k: [refs.pop(0) for _ in range(k)]
    refs = list(refs)
    norm, branch, up, (up_new,), _ = take(3), take(3), take(3), take(1), take(3)
    tokens_o, up_o = take(2), take(3)
    x_b, e_b = take(2)
    parts_b, up_b, (up_g,), out_b = take(6), take(3), take(1), take(2)
    moves = Moves(refs.pop(0))
    f = lax.axis_index("fsdp")
    t = lax.axis_index("tp")
    mid = bit_of(f, 2)
    rows, feat = x.shape[0], up[0].shape[0]
    up_loads = moves.load(
        [
            move
            for src, dst in zip(up, up_b)
            for move in zip(columns_of(src, 1 - mid, chunk), side_by_side(dst, chunk))
        ]
        + [(up_new, up_g)]
    )
    where = lambda part: [block(part[0], mid * 2 + t // 2, rows), block(part[1], mid, rows), part[2]]
    token_loads = moves.load([(x, x_b), (e, e_b), *zip(where(norm) + where(branch), parts_b)])
    for c in up_loads:
        c.wait()
    adam_loop(up_b, [up_g], rate, feat // ROWS, by_chunks)
    moves.store(
        [
            move
            for src, dst in zip((up_b[1], up_b[2], up_b[0]), up_o)
            for move in zip(side_by_side(src, chunk), columns_of(dst, 1 - mid, chunk))
        ]
    )
    for c in token_loads:
        c.wait()
    bias = vec[4:5, :] + vec[5:6, :]

    @pl.loop(0, rows // ROWS)
    def _(i):
        at = here(i, ROWS)
        add = lambda part: sum(ref[at, :].astype(f32) for ref in part)
        stream = x_b[at, :].astype(f32)
        out_b[0][at, :] = stream + add(parts_b[3:]) + bias
        scaled = add(parts_b[:3])
        normal, inverse = normalise(stream, True)
        out_b[1][at, :] = e_b[at, :].astype(f32) + inverse * (
            scaled
            - jnp.mean(scaled, axis=-1, keepdims=True)
            - normal * jnp.mean(scaled * normal, axis=-1, keepdims=True)
        )

    moves.store(zip(out_b, tokens_o))
    moves.drain()


def run_update(chunk, rates, qkv, out_new, up_last, down_last, weights):
    n = len(up_last)
    flat = [w for group in weights for w in group]
    grads = [*qkv[0], *up_last, *down_last, qkv[1], out_new]
    feat, sub = weights[2][0].shape[0], weights[3][0].shape[0]
    wide, mine, d = qkv[1].shape[1], up_last[0].shape[1], weights[3][0].shape[1]
    half_up = (feat, mine)
    held = [w.shape for w in flat[:6]] + [half_up] * 3 + [w.shape for w in flat[9:]]
    held_grads = [(feat, wide)] * n + [half_up] * n + [(sub, d)] * n + [(feat, wide), out_new.shape]
    pieces = weights[2][0].shape[1] // (2 * chunk)
    n_bytes = 8 * sum(w.size for w in flat)
    return pl.pallas_call(
        functools.partial(update_kernel, chunk, rates, n),
        out_shape=[jax.ShapeDtypeStruct(w.shape, f32) for w in flat],
        in_specs=[ANY] * (len(flat) + len(grads)),
        out_specs=[ANY] * len(flat),
        scratch_shapes=[pltpu.VMEM(shape, f32) for shape in held]
        + [pltpu.VMEM(shape, bf16) for shape in held_grads]
        + [pltpu.SemaphoreType.DMA((2 * 9 + 2 * 3 * pieces + 3 * n + 2,))],
        compiler_params=pltpu.CompilerParams(vmem_limit_bytes=56 * 2**20),
        cost_estimate=pl.CostEstimate(flops=0, bytes_accessed=n_bytes, transcendentals=0),
        name="update",
    )(*flat, *grads)


def run_finish(chunk, rate, x, e, vec, tokens, up, up_new, up_done):
    rows, d = x.shape
    half_up = up_new.shape
    token = jax.ShapeDtypeStruct(x.shape, f32)
    pieces = up[0].shape[1] // (2 * chunk)
    return pl.pallas_call(
        functools.partial(finish_kernel, chunk, rate),
        out_shape=[token, token] + [jax.ShapeDtypeStruct(w.shape, f32) for w in up],
        in_specs=[ANY, ANY, VMEM] + [ANY] * 13,
        out_specs=[ANY] * 5,
        input_output_aliases={13: 2, 14: 3, 15: 4},
        scratch_shapes=[pltpu.VMEM((rows, d), bf16)] * 8
        + [pltpu.VMEM(half_up, f32)] * 3
        + [pltpu.VMEM(half_up, bf16)]
        + [pltpu.VMEM((rows, d), f32)] * 2
        + [pltpu.SemaphoreType.DMA((2 * 3 * pieces + 1 + 8 + 2,))],
        compiler_params=pltpu.CompilerParams(vmem_limit_bytes=56 * 2**20),
        name="finish",
    )(x, e, vec, *tokens[0], *tokens[1], *up, up_new, *up_done)


def make_local(fsdp, tp):
    masks = [1 << b for b in range(2, fsdp.bit_length() - 1)] + [1]
    top = fsdp // 2

    def local(
        layer_input,
        out_cotangent,
        segments,
        qkv_weight,
        qkv_first,
        qkv_second,
        out_weight,
        out_first,
        out_second,
        up_weight,
        up_first,
        up_second,
        down_weight,
        down_first,
        down_second,
        small_params,
        small_first,
        small_second,
    ):
        d = layer_input.shape[1]
        length = segments.shape[1]
        chunk = 2 * down_weight.shape[1]
        lanes = np.arange(128)
        rate = 10000.0 ** (-(2.0 * (lanes % (ROT // 2))) / ROT)
        angle = np.arange(length)[:, None] * rate[None]
        rates = np.broadcast_to(rate, angle.shape)
        table = jnp.asarray(np.concatenate([np.cos(angle), np.sin(angle), rates], 1), f32)
        vec = small_params.reshape(-1, d)
        token_parts, qkv_parts, out_new, up_parts, down_last, small = run_layer(
            masks, top, length, tp, layer_input, out_cotangent, up_weight[0], qkv_weight[0], down_weight[0],
            out_weight[0], segments, table, vec,
        )
        weights = (
            (qkv_weight[0], qkv_first[0], qkv_second[0]),
            (out_weight[0], out_first[0], out_second[0]),
            (up_weight[0], up_first[0], up_second[0]),
            (down_weight[0], down_first[0], down_second[0]),
        )
        rates = (d ** (-0.5), 4.0 * d ** (-0.5))
        up_last, up_give = up_parts
        up_new = lax.ppermute(up_give, "fsdp", [(i, i ^ 2) for i in range(fsdp)])
        updated = run_update(chunk, rates, qkv_parts, out_new, up_last, down_last, weights)
        finished = run_finish(
            chunk, rates[0], layer_input, out_cotangent, vec, token_parts, weights[2], up_new, updated[6:9]
        )
        results = [*finished[:2], *updated[:6], *finished[2:], *updated[9:]]
        small_total = jnp.concatenate([small[0:5], small[4:5], small[5:12]]).reshape(1, -1)
        small_updated = adam_step(small_params, small_first, small_second, small_total, rate_vector, 0.0)
        return (*results[:2], *[w[None] for w in results[2:]], *small_updated)

    return local


def solution(mesh):
    tokens = P(("fsdp", "tp"), None)
    inner = P(None, ("tp", "fsdp"), None)
    qkv = P(None, None, "fsdp", "tp")
    up = P(None, "fsdp", "tp")
    weights = (qkv,) * 3 + (inner,) * 3 + (up,) * 3 + (inner,) * 3 + (P(),) * 3
    return jax.shard_map(
        make_local(mesh.shape["fsdp"], mesh.shape["tp"]),
        mesh=mesh,
        in_specs=(tokens, tokens, P("fsdp", None)) + weights,
        out_specs=(tokens, tokens) + weights,
        check_vma=False,
    )
```

```python
import enum
import functools

import jax
import jax.numpy as jnp
import numpy as np
from jax import lax
from jax.experimental import pallas as pl
from jax.experimental.pallas import tpu as pltpu
from jax.sharding import PartitionSpec as P

HD = 256
ROT = 64
STEP = 10

norm_eps = 1e-05
beta_one = 0.9
beta_two = 0.95
adam_eps = 1e-08
decay_rate = 0.01
rate_vector = 0.2
masked_score = -1e30
f32 = jnp.float32
bf16 = jnp.bfloat16


def adam_step(weight, first, second, grad, rate, decay):
    first_new = beta_one * first + (1.0 - beta_one) * grad
    second_new = beta_two * second + (1.0 - beta_two) * grad * grad
    first_hat = first_new / (1.0 - beta_one**STEP)
    second_hat = second_new / (1.0 - beta_two**STEP)
    weight_new = weight - rate * (first_hat / (jnp.sqrt(second_hat) + adam_eps) + decay * weight)
    return (first_new, second_new, weight_new)


MESH = pl.DeviceIdType.MESH


def bit_of(i, mask):
    return (i // mask) % 2


def flip(i, mask):
    return i + mask - 2 * mask * bit_of(i, mask)


class Copy:
    def __init__(self, copy):
        self.copy, self.started, self.received, self.sent = copy, False, False, False

    def start(self):
        self.started = True
        self.copy.start()

    def wait_recv(self):
        self.received = True
        self.copy.wait_recv()

    def wait_send(self):
        self.sent = True
        self.copy.wait_send()


class Local:
    def __init__(self, copy):
        self.copy, self.started, self.done = copy, False, False

    def start(self):
        self.started = True
        self.copy.start()

    def wait(self):
        self.done = True
        self.copy.wait()


class Links:
    def __init__(self, send_sem, recv_sem, local_sem):
        self.send_sem, self.recv_sem, self.local_sem = send_sem, recv_sem, local_sem
        self.copies, self.locals, self.swaps, self.n_local = [], [], [], 0

    def local(self, src, dst):
        c = Local(pltpu.make_async_copy(src, dst, self.local_sem.at[self.n_local]))
        self.n_local += 1
        self.locals.append(c)
        return c

    def copy(self, src, dst, device):
        k = len(self.copies)
        c = Copy(
            pltpu.make_async_remote_copy(
                src_ref=src,
                dst_ref=dst,
                send_sem=self.send_sem.at[k],
                recv_sem=self.recv_sem.at[k],
                device_id=device,
                device_id_type=MESH,
            )
        )
        self.copies.append(c)
        return c

    def drain(self):
        for c in self.copies:
            if c.started and not c.received:
                c.wait_recv()
            if c.started and not c.sent:
                c.wait_send()
        for c in self.locals:
            if c.started and not c.done:
                c.wait()
        for c in self.swaps:
            c.drain()


class Group:
    def __init__(self, links, at, f, t, masks, root):
        self.copies, self.masks = {}, masks
        for key in all_keys(masks):
            g = root
            for mask in masks:
                if key & mask:
                    g = flip(g, mask)
            ref = at(g)
            after = max([i + 1 for i, m in enumerate(masks) if key & m], default=0)
            for mask in masks[after:]:
                self.copies[key | mask] = links.copy(ref, ref, (flip(f, mask), t))

    def low(self):
        self.copies[1].start()

    def high(self):
        self.copies[self.masks[0]].start()

    def rest(self):
        keys = all_keys(self.masks[:-1])
        for s, mask in enumerate(self.masks[1:-1]):
            for key in all_keys(self.masks[: s + 1]):
                if key:
                    self.copies[key].wait_recv()
                self.copies[key | mask].start()
        last = self.masks[-2]
        for key in keys:
            if key & last:
                self.copies[key].wait_recv()
            if key:
                self.copies[key | 1].start()

    def ends(self):
        return [c for key, c in self.copies.items() if key & 1]


def all_keys(masks):
    keys = [0]
    for mask in masks:
        keys = keys + [k | mask for k in keys]
    return keys


def normalise(x, with_inverse=False):
    mean = jnp.mean(x, axis=-1, keepdims=True)
    centred = x - mean
    inverse = lax.rsqrt(jnp.mean(centred * centred, axis=-1, keepdims=True) + norm_eps)
    return (centred * inverse, inverse) if with_inverse else centred * inverse


def rope(u, c, s):
    lane = lax.broadcasted_iota(jnp.int32, u.shape, 1)
    partner = jnp.where(lane < ROT // 2, pltpu.roll(u, 128 - ROT // 2, 1), pltpu.roll(u, ROT // 2, 1))
    return u * c + partner * s


def dot(a, b, dims):
    return lax.dot_general(a, b, (dims, ((), ())), preferred_element_type=f32)


NN = ((1,), (0,))
NT = ((1,), (1,))
TN = ((0,), (0,))
TILE = 256


def pipe(body, steps, ins, outs, hooks=()):
    def whole(*refs):
        for i, n, run in hooks:
            pl.when(pl.program_id(0) == i * steps // n)(run)
        body(*refs)

    pltpu.emit_pipeline(
        whole,
        grid=(steps,),
        in_specs=[spec for _, spec in ins],
        out_specs=[spec for _, spec in outs],
    )(*[ref for ref, _ in ins], *[ref for ref, _ in outs])


def by_rows(ref, index=lambda i: i, rows=TILE):
    return ref, pl.BlockSpec((rows, ref.shape[1]), lambda i: (index(i), 0))


def by_columns(ref, index, width):
    return ref, pl.BlockSpec((ref.shape[0], width), lambda i: (0, index(i)))


def here(i, rows=TILE):
    return pl.ds(pl.multiple_of(i * rows, rows), rows)


def run_cast(weight, index, steps, width, dst):
    def body(w_ref):
        at = pl.ds(pl.multiple_of(pl.program_id(0) * width, width), width)
        dst[:, at] = w_ref[...].astype(bf16)

    pipe(body, steps, [by_columns(weight, index, width)], [])


def run_cast_qkv(weight, half, dst):
    def body(w_ref):
        at = pl.ds(pl.multiple_of(pl.program_id(0) * HD, HD), HD)
        dst[:, at] = w_ref[...].reshape(w_ref.shape[-2:]).astype(bf16)

    spec = pl.BlockSpec((1, weight.shape[1], HD), lambda i: (i, 0, half))
    pipe(body, 3, [(weight, spec)], [])


class Rotary:
    def __init__(self, table, starts, seq):
        self.table, self.starts, self.seq = table, starts, seq

    def bounds(self):
        at = pl.ds(self.seq * 8, 1)
        return self.starts[at, 0:1].astype(jnp.int32), self.starts[at, 1:2].astype(jnp.int32)

    def __call__(self, tile):
        shape = (TILE, 128)
        lane = lax.broadcasted_iota(jnp.int32, (1, 128), 1)
        first, second = self.bounds()
        turning = lane < ROT
        rate = self.table[0:1, 256:384]
        one, two = first.astype(f32) * rate, second.astype(f32) * rate
        index = tile * TILE + lax.broadcasted_iota(jnp.int32, shape, 0)
        pick = lambda a, b, c: jnp.where(index >= second, c, jnp.where(index >= first, b, a))
        cos_b = pick(jnp.ones_like(one), jnp.cos(one), jnp.cos(two))
        sin_b = pick(jnp.zeros_like(one), jnp.sin(one), jnp.sin(two))
        rows = here(tile)
        cos_t, sin_t = self.table[rows, 0:128], self.table[rows, 128:256]
        sign = jnp.where(lane < ROT // 2, -1.0, 1.0)
        c = jnp.where(turning, cos_t * cos_b + sin_t * sin_b, 1.0)
        s = jnp.where(turning, sign * (sin_t * cos_b - cos_t * sin_b), 0.0)
        return c, s


def normed(vec, k, xh, at):
    return (xh[at, :].astype(f32) * vec[2 * k : 2 * k + 1, :] + vec[2 * k + 1 : 2 * k + 2, :]).astype(bf16)


def run_project(vec, qkv_bias, xh, w, rotary, seq, p, steps, hooks=()):
    def body():
        i = pl.program_id(0)
        at = here(seq * steps + i)
        c, s = rotary(i)
        proj = dot(normed(vec, 0, xh, at), w[...], NN) + qkv_bias()
        for j in range(2):
            p[at, j * HD : j * HD + 128] = rope(proj[:, j * HD : j * HD + 128], c, s).astype(bf16)
            p[at, j * HD + 128 : (j + 1) * HD] = proj[:, j * HD + 128 : (j + 1) * HD].astype(bf16)
        p[at, 2 * HD :] = proj[:, 2 * HD :].astype(bf16)

    pipe(body, steps, [], [], hooks)


def run_up(vec, up_bias, xh, w, g, slope, index, steps, hooks=()):
    width = w.shape[1]
    part = min(width, 256)

    def body(g_ref, s_ref):
        n = normed(vec, 1, xh, here(index(pl.program_id(0))))
        for j in range(0, width, part):
            h = dot(n, w[:, j : j + part], NN) + up_bias[0:1, j : j + part]
            cdf = 0.5 + 0.5 * lax.erf(h * 0.7071067811865476)
            g_ref[:, j : j + part] = (h * cdf).astype(bf16)
            s_ref[:, j : j + part] = (cdf + h * (jnp.exp(-0.5 * h * h) * 0.3989422804014327)).astype(bf16)

    pipe(body, steps, [], [by_rows(g, index), by_rows(slope, index)], hooks)


def run_attention(length, seq, rotary, p, da, a, dproj, dk, dv, sums):
    scale = HD ** (-0.5)
    tiles_n = length // TILE
    first, second = rotary.bounds()
    rows = lambda i: here(seq * tiles_n + i)

    def put(i, value, column):
        c, s = rotary(i)
        keep(i, rope(value[:, :128], c, -s), column)
        keep(i, value[:, 128:], column + 128)

    def keep(i, value, column):
        value = value.astype(bf16)
        at = slice(column, column + value.shape[1])
        dproj[rows(i), at] = value
        sums[0:1, at] += jnp.sum(value.astype(f32), axis=0, keepdims=True)

    dk[...] = jnp.zeros_like(dk)
    dv[...] = jnp.zeros_like(dv)
    for i in range(tiles_n):
        n = (i + 1) * TILE
        until = pl.ds(pl.multiple_of(seq * length, length), n)
        q = p[rows(i), 0:HD]
        k = p[until, HD : 2 * HD]
        v = p[until, 2 * HD :]
        rows_da = da[rows(i), :]
        scores = dot(q, k, NT) * scale
        qi = i * TILE + lax.broadcasted_iota(jnp.int32, (TILE, n), 0)
        ki = lax.broadcasted_iota(jnp.int32, (TILE, n), 1)
        start = jnp.where(qi >= second, second, jnp.where(qi >= first, first, 0))
        scores = jnp.where((ki <= qi) & (ki >= start), scores, masked_score)
        peak = jnp.max(scores, axis=-1, keepdims=True)
        raised = jnp.exp(scores - peak)
        probs = raised * (1.0 / jnp.sum(raised, axis=-1, keepdims=True))
        weights = probs.astype(bf16)
        a[rows(i), :] = dot(weights, v, NN).astype(bf16)
        prob_grad = dot(rows_da, v, NT)
        delta = jnp.sum(probs * prob_grad, axis=-1, keepdims=True)
        score_grad = (probs * (prob_grad - delta)).astype(bf16)
        put(i, dot(score_grad, k, NN) * scale, 0)
        dk[0:n, :] += dot(score_grad, q, TN)
        dv[0:n, :] += dot(weights, rows_da, TN)
    for i in range(tiles_n):
        local = slice(i * TILE, (i + 1) * TILE)
        put(i, dk[local, :] * scale, HD)
        keep(i, dv[local, :], 2 * HD)


def column_of(row):
    return jnp.broadcast_to(row, (128, row.shape[1])).T[:, 0:1]


def row_of(column):
    return jnp.broadcast_to(column, (column.shape[0], 128)).T[0:1, :]


class Through:
    def __init__(self, vec, k, w, d_sum, sums):
        self.vec, self.k, self.w, self.d_sum, self.sums = vec, k, w, d_sum, sums

    def __call__(self, value, index):
        n = value.shape[0]
        at = here(index, n)
        w = self.w[at, :].astype(f32)
        total = self.d_sum[0:1, :]
        self.sums[2 * self.k : 2 * self.k + 1, at] = row_of(jnp.sum(w * value, axis=1, keepdims=True))
        self.sums[2 * self.k + 1 : 2 * self.k + 2, at] = row_of(jnp.sum(w * total, axis=1, keepdims=True))
        gain = column_of(self.vec[2 * self.k : 2 * self.k + 1, at])
        shift = column_of(self.vec[2 * self.k + 1 : 2 * self.k + 2, at])
        return value * gain + shift * total


def run_outer(a, b, out, index_in, index_out, steps, width, add=None, through=None, hooks=()):
    def body(*refs):
        index = index_in(pl.program_id(0))
        left = a[:, here(index, width)] if through else refs[0][...]
        value = dot(left, b[...], TN)
        if through:
            value = through(value, index)
        if add is not None:
            value = value + refs[-2][...].astype(f32)
        refs[-1][...] = value.astype(bf16)

    ins = [] if through else [by_columns(a, index_in, width)]
    if add is not None:
        ins.append(by_rows(add, index_out, width))
    pipe(body, steps, ins, [by_rows(out, index_out, width)], hooks)


def run_outer_wide(a, b, out):
    width = 2 * TILE

    def body(out_ref):
        at = pl.ds(pl.multiple_of(pl.program_id(0) * width, width), width)
        out_ref[...] = dot(a[...], b[:, at], TN).astype(bf16)

    pipe(body, b.shape[1] // width, [], [by_columns(out, lambda i: i, width)])


def run_hidden_grad(e, w, slope, dh, bias_sum, index, steps, hooks=()):
    def body(s_ref):
        at = here(index(pl.program_id(0)))
        value = (dot(e[at, :], w[...], NT) * s_ref[...].astype(f32)).astype(bf16)
        dh[at, :] = value
        bias_sum[0:1, :] += jnp.sum(value.astype(f32), axis=0, keepdims=True)

    pipe(body, steps, [by_rows(slope, index)], [], hooks)


def run_norm_grad(vec, dh, w_up, dproj, w_qkv):
    def tile(at):
        one = dot(dproj[at, :], w_qkv[...], NT)
        two = dot(dh[at, :], w_up[...], NT)
        return one * vec[0:1, :] + two * vec[2:3, :]

    return None, tile


def run_branch(a, w_out, g, w_down):
    def tile(at, g_ref):
        return dot(a[at, :], w_out[...], NN) + dot(g_ref[...], w_down[...], NN)

    return g, tile


def run_token_tiles(job, out, index, index_out, steps, add=None, hooks=()):
    source, tile = job

    def body(*refs):
        value = tile(here(index(pl.program_id(0))), *([] if source is None else refs[:1]))
        if add is not None:
            value = value + refs[-2][...].astype(f32)
        refs[-1][...] = value.astype(bf16)

    ins = [] if source is None else [by_rows(source, index)]
    if add is not None:
        ins.append(by_rows(add, index_out))
    pipe(body, steps, ins, [by_rows(out, index_out)], hooks)


def run_add(a, b, out):
    rows, cols = out.shape
    step = min(rows, TILE)

    def body(a_ref, b_ref, out_ref):
        out_ref[...] = (a_ref[...].astype(f32) + b_ref[...].astype(f32)).astype(bf16)

    pipe(body, rows // step, [by_rows(a, rows=step), by_rows(b, rows=step)], [by_rows(out, rows=step)])


def block(ref, index, rows):
    return ref.at[pl.ds(pl.multiple_of(index * rows, rows), rows)]


def out_place(g, top):
    return (((g // 4) % (top // 4)) * 2 + g // top) * 2 + g % 2


class Scatter:
    def __init__(self, links, part, place, rows, mids, recv, sums, f, t, masks):
        self.links, self.part, self.place, self.rows, self.mids = links, part, place, rows, mids
        self.recv, self.sums, self.f, self.t = recv, sums, f, t
        self.stages = [1] + [m for m in reversed(masks) if m != 1]
        self.n_hi = 1 << (len(masks) - 1)
        self.hi, self.lo, self.mid = f // 4, f % 2, bit_of(f, 2)
        self.half = self.hi % 2
        self.to = None
        self.copies = {}
        for k in range(self.n_hi):
            for j, m in enumerate(mids):
                self.copies[0, k, j] = links.copy(
                    block(part, self.at_place(self.high(k), m, 1 - self.lo), rows),
                    block(recv[0], self.slot(0, k, j), rows),
                    (flip(f, 1), t),
                )
        for level in range(len(self.stages) - 1):
            n = self.n_hi >> (level + 1)
            for k in range(n, 2 * n):
                for j in range(len(mids)):
                    self.copies[level + 1, k - n, j] = links.copy(
                        block(sums[level], self.slot(level, k, j), rows),
                        block(recv[level + 1], self.slot(level + 1, k, j), rows),
                        (flip(f, self.stages[level + 1]), t),
                    )

    def high(self, k):
        hi, b = self.hi, 1
        while b < self.n_hi:
            if k & b:
                hi = flip(hi, b)
            b *= 2
        return hi

    def slot(self, level, k, j):
        n = self.n_hi >> level
        i = (self.high(k) % n) if n > 1 else 0
        return i * len(self.mids) + j

    def at_place(self, hi, m, lo):
        return self.place((hi * 2 + (self.mid if m is None else m)) * 2 + lo)

    def ks(self, far):
        half = self.n_hi // 2
        return range(half, self.n_hi) if far else range(half)

    def each(self, far):
        return [(k, j) for k in self.ks(far) for j in range(len(self.mids))]

    def tile(self, i, far, lo):
        n = len(self.mids)
        half = self.n_hi // 2
        upper = self.hi // half
        hi = (1 - upper if far else upper) * half + i // n
        j = i % n
        m = None if self.mids[0] is None else j
        return self.at_place(hi, m, lo), hi * n + j

    def add(self, level, k, j):
        mine = (
            block(self.part, self.at_place(self.high(k), self.mids[j], self.lo), self.rows)
            if level == 0
            else block(self.sums[level - 1], self.slot(level - 1, k, j), self.rows)
        )
        at = self.slot(level, k, j)
        run_add(mine, block(self.recv[level], at, self.rows), block(self.sums[level], at, self.rows))

    def first_adds(self, far):
        for k, j in self.each(far):
            self.add(0, k, j)

    def finish(self, waited):
        if waited:
            if len(self.mids) == 1:
                self.add(1, 0, 0)
            else:
                other = 1 - self.mid
                at = self.half * 2 + other
                to = block(self.sums[1], other, self.rows) if self.to is None else self.to
                run_add(block(self.sums[0], at, self.rows), block(self.recv[1], other, self.rows), to)
            return
        for level in range(1, len(self.stages)):
            n = self.n_hi >> level
            for k in reversed(range(n)):
                for j in range(len(self.mids)):
                    self.copies[level, k, j].wait_recv()
                    self.add(level, k, j)
                    if level + 1 < len(self.stages) and k & (n // 2):
                        self.copies[level + 1, k - n // 2, j].start()
        if self.to is not None:
            self.links.local(block(self.sums[-1], 1 - self.mid, self.rows), self.to).start()


class Outer:
    def __init__(self, scatter, a, b, through=None):
        self.s, self.a, self.b, self.through = scatter, a, b, through
        self.fused = scatter.rows % 128 == 0
        self.steps = scatter.n_hi // 2 * len(scatter.mids)

    def give(self, far, hooks=()):
        s = self.s
        if self.fused:
            at = lambda i: s.tile(i, far, 1 - s.lo)[0]
            run_outer(self.a, self.b, s.part, at, at, self.steps, s.rows, through=self.through, hooks=hooks)
        elif far:
            same = lambda i: i
            run_outer(self.a, self.b, s.part, same, same, self.a.shape[1] // 128, 128, through=self.through, hooks=hooks)

    def keep(self, far, hooks=()):
        s = self.s
        if self.fused:
            at = lambda i: s.tile(i, far, s.lo)[0]
            to = lambda i: s.tile(i, far, s.lo)[1]
            run_outer(
                self.a, self.b, s.sums[0], at, to, self.steps, s.rows, add=s.recv[0], through=self.through, hooks=hooks
            )
        else:
            s.first_adds(far)


class Tokens:
    def __init__(self, links, refs, rows, f, t, job):
        self.give_buf, self.got, self.sum, self.got_y, self.sum_y, self.final = refs
        self.rows, self.mid, self.y, self.core, self.job = rows, bit_of(f, 2), t // 2, t % 2, job
        core_peer, y_peer, mid_peer = (f, flip(t, 1)), (f, flip(t, 2)), (flip(f, 2), t)
        self.over_core = [
            links.copy(block(self.give_buf, i, rows), block(self.got, i, rows), core_peer) for i in range(4)
        ]
        self.over_y = [
            links.copy(block(self.sum, m * 2 + 1 - self.y, rows), block(self.got_y, m, rows), y_peer)
            for m in range(2)
        ]
        self.over_mid = [links.copy(block(self.sum_y, 1 - self.mid, rows), self.final, mid_peer)]

    def give(self, hooks=()):
        index = lambda i: (i // 2) * 4 + (i % 2) * 2 + 1 - self.core
        run_token_tiles(self.job, self.give_buf, index, lambda i: i, 4, hooks=hooks)

    def keep(self, far, hooks=()):
        yy = 1 - self.y if far else self.y
        index = lambda i: i * 4 + yy * 2 + self.core
        run_token_tiles(self.job, self.sum, index, lambda i: i * 2 + yy, 2, add=self.got, hooks=hooks)

    def across(self):
        m = 1 - self.mid
        run_add(block(self.sum, m * 2 + self.y, self.rows), block(self.got_y, m, self.rows), block(self.sum_y, m, self.rows))


def greet(f, t, masks, top):
    mid = bit_of(f, 2)
    swapped = f + (top - 2) * (mid - bit_of(f, top))
    barrier = pltpu.get_barrier_semaphore()
    peers = [(flip(f, m), t) for m in masks + [2]] + [(f, flip(t, 1)), (f, flip(t, 2))]
    for peer in peers:
        pl.semaphore_signal(barrier, inc=1, device_id=peer, device_id_type=MESH)

    @pl.when(swapped != f)
    def _():
        pl.semaphore_signal(barrier, inc=1, device_id=(swapped, t), device_id_type=MESH)

    pl.semaphore_wait(barrier, len(peers) + (mid + bit_of(f, top)) % 2)
    return swapped


class Swap:
    def __init__(self, links, src, dst, stay, f, t, swapped):
        self.move = links.copy(src, dst, (swapped, t)).copy
        self.copy = pltpu.make_async_copy(src, stay, links.local_sem.at[links.n_local])
        links.n_local += 1
        links.swaps.append(self)
        self.moves, self.stays = swapped != f, swapped == f
        self.started, self.done = False, False

    def start(self):
        self.started = True
        pl.when(self.moves)(self.move.start)
        pl.when(self.stays)(self.copy.start)

    def wait(self):
        self.done = True
        pl.when(self.moves)(self.move.wait_recv)
        pl.when(self.stays)(self.copy.wait)

    def drain(self):
        if self.started and not self.done:
            self.wait()
        if self.started:
            pl.when(self.moves)(self.move.wait_send)


class S(enum.Enum):
    (
        attn_oth, attn_own, branch_aa, branch_c, branch_g, branch_kf, branch_kn, branch_m, branch_y,
        cast_down, cast_out, cast_qkv, cast_up, da_oth, da_own, dh_oth, dh_own, down0_x, down0_zh, down0_zhx,
        down1_x, down1_zh, down1_zhx, es_c, es_m, es_mc, es_my, es_myc, es_y, es_yc, gdown_f, gdown_gf,
        gdown_gn, gdown_kf, gdown_kn, gdown_n, gdown_on, gout, gout_add, gout_f, gout_kf, gout_kn, gout_n,
        gout_on, gout_x, gqkv_add, gqkv_f, gqkv_gf, gqkv_gn, gqkv_kf, gqkv_kn, gqkv_n, gqkv_on, gqkv_x,
        gup_add, gup_f, gup_gf, gup_gn, gup_kf, gup_kn, gup_n, gup_on, norm_aa, norm_c, norm_g, norm_kf,
        norm_kn, norm_m, norm_own, norm_y, out_swap, out_x, out_zh, out_zhx, proj_oth, proj_own, qkv_first,
        qkv_mid_x, qkv_mid_zh, qkv_mid_zhx, qkv_own_x, qkv_own_zh, qkv_own_zhx, small0, small1, small2,
        small3, small4, small_end, up_first, up_mid_x, up_mid_zh, up_mid_zhx, up_oth, up_own, up_own_x,
        up_own_zh, up_own_zhx, xs_c, xs_m, xs_mc, xs_my, xs_myc, xs_y, xs_yc,
    ) = range(105)


ORDER = [
    S.es_m, S.cast_up, S.norm_own, S.es_c, S.cast_qkv, S.qkv_first, S.xs_c, S.cast_out, S.out_swap,
    S.cast_down, S.qkv_own_zh, S.down0_x, S.up_own_x, S.es_y, S.qkv_mid_x, S.qkv_mid_zh, S.xs_y, S.down0_zh,
    S.xs_m, S.es_yc, S.qkv_own_zhx, S.es_my, S.down1_x, S.qkv_own_x, S.out_zh, S.out_x, S.es_mc, S.out_zhx,
    S.up_first, S.xs_yc, S.qkv_mid_zhx, S.up_own_zh, S.xs_my, S.es_myc, S.xs_mc, S.da_own, S.down0_zhx,
    S.up_mid_zh, S.up_mid_x, S.da_oth, S.proj_own, S.proj_own, S.xs_myc, S.up_own_zhx, S.proj_own,
    S.proj_own, S.attn_own, S.proj_oth, S.proj_oth, S.proj_oth, S.proj_oth, S.attn_oth, S.up_mid_zhx, S.gout,
    S.down1_zh, S.gqkv_gn, S.gqkv_gn, S.gqkv_gf, S.gout_f, S.gqkv_gf, S.gqkv_f, S.up_oth, S.up_oth, S.up_oth,
    S.up_oth, S.gout_kf, S.up_own, S.gout_on, S.up_own, S.down1_zhx, S.up_own, S.up_own, S.gdown_gf,
    S.gqkv_kf, S.gqkv_kf, S.gdown_f, S.gqkv_on, S.branch_g, S.branch_g, S.branch_g, S.branch_g, S.branch_c,
    S.dh_oth, S.dh_oth, S.dh_oth, S.dh_oth, S.dh_own, S.gqkv_n, S.dh_own, S.dh_own, S.dh_own, S.branch_kf,
    S.branch_kf, S.branch_y, S.gdown_kf, S.gdown_on, S.gup_gf, S.gup_gf, S.gup_f, S.norm_g, S.norm_g,
    S.norm_g, S.norm_g, S.gqkv_kn, S.gqkv_kn, S.gup_gn, S.norm_c, S.gup_gn, S.gqkv_add, S.gup_n, S.gqkv_x,
    S.branch_kn, S.branch_kn, S.norm_kf, S.norm_kf, S.gup_kf, S.norm_y, S.gup_kf, S.gup_on, S.branch_aa,
    S.branch_m, S.gout_n, S.gdown_gn, S.gup_kn, S.gup_kn, S.small0, S.gout_kn, S.gdown_n, S.norm_kn,
    S.small1, S.small2, S.norm_kn, S.gout_add, S.small3, S.norm_aa, S.norm_m, S.gdown_kn, S.small4, S.gout_x,
    S.gup_add, S.small_end,
]


class Plan:
    def __init__(self):
        self.actions, self.waits = {}, {}

    def send(self, name, needs, starts, *copies):
        self.actions[name] = (None, needs, starts)
        self.waits[name] = copies

    def compute(self, name, needs, run):
        self.actions[name] = (True, needs, run)

    def pending(self, name):
        found = []
        for need in self.actions[name][1]:
            found += self.waits.pop(need, ())
        return found

    def starter(self, name):
        pending, starts = self.pending(name), self.actions[name][2]

        def run():
            for c in pending:
                c()
            for start in starts:
                start()

        return run

    def carry_out(self, order):
        i = 0
        while i < len(order):
            name = order[i]
            i += 1
            compute, _, run = self.actions[name]
            if not compute:
                self.starter(name)()
                continue
            for wait in self.pending(name):
                wait()
            n = 1 + order[i:].count(name)
            hooks = []
            for part in range(1, n):
                while order[i] != name:
                    hooks.append((part, n, self.starter(order[i])))
                    i += 1
                i += 1
            run(hooks) if n > 1 else run(())


N_HBM = 6


def layer_kernel(
    masks, top, length,
    e, up, qkv, down, out, seg, table, x, vec,
    *rest,
):
    n_stage = len(masks)
    (g, slope, g_qkv, g_out, g_down, g_up), rest = rest[:N_HBM], rest[N_HBM:]
    stage_refs = []
    for _ in range(4):
        stage_refs.append((rest[:n_stage], rest[n_stage : 2 * n_stage]))
        rest = rest[2 * n_stage :]
    token_refs, rest = [rest[:6], rest[6:12]], rest[12:]
    (up_new, qkv_new, out_new, small), rest = rest[:4], rest[4:]
    (
        xh, ea, upa, qkva, downa, outa, up16, qkv16, out16, p, da, a, dproj, dh, dk, dv,
        sums, qkv_sum, bias_sum, up_bias, starts, small_in,
        send_sem, recv_sem, local_sem,
    ) = rest
    f = lax.axis_index("fsdp")
    t = lax.axis_index("tp")
    mid = bit_of(f, 2)
    rows, d = x.shape
    feat, sub, orow = up.shape[0], down.shape[0], out.shape[0]
    mine = upa.shape[1]
    chunk = 2 * sub
    hi_n = mine // chunk
    swapped = greet(f, t, masks, top)
    links = Links(send_sem, recv_sem, local_sem)
    plan = Plan()

    mid_peer, y_peer, core_peer = (flip(f, 2), t), (f, flip(t, 2)), (f, flip(t, 1))
    qkv_block = lambda i: block(qkva, i, feat)
    up_block = lambda i: block(upa, i, feat)
    half_sub = sub // 2
    out_block = lambda i: block(outa, out_place(i, top), orow)
    tok = lambda buf, m, j: block(buf, m * 4 + j, rows)

    def sends(name, needs, *copies):
        plan.send(name, needs, [c.start for c in copies], *[c.wait_recv for c in copies])

    own_e = links.local(e, tok(ea, mid, t))
    for prefix, source, buf in (("xs", None, xh), ("es", e, ea)):
        for name, needs, m, j, peer in (
            ("m", (), mid, t, mid_peer),
            ("y", (), mid, t, y_peer),
            ("c", (), mid, t, core_peer),
            ("my", ("m",), 1 - mid, t, y_peer),
            ("mc", ("m",), 1 - mid, t, core_peer),
            ("yc", ("y",), mid, flip(t, 2), core_peer),
            ("myc", ("my",), 1 - mid, flip(t, 2), core_peer),
        ):
            ref = tok(buf, m, j)
            c = links.copy(ref if needs or source is None else source, ref, peer)
            sends(prefix + "_" + name, [prefix + "_" + n for n in needs], c)
    plan.waits["own_e"] = (own_e.wait,)
    own_e.start()

    def spreads(name, group, need):
        sends(name + "_x", need, group.copies[1])
        plan.send(name + "_zh", need, [group.high], *([group.copies[masks[0]].wait_recv] if n_stage == 2 else []))
        if n_stage == 2:
            sends(name + "_zhx", [name + "_zh"], group.copies[masks[0] | 1])
        else:
            plan.send(name + "_zhx", [], [group.rest], *[c.wait_recv for c in group.ends() if c is not group.copies[1]])

    first_up = links.copy(up16, up_block(f), mid_peer)
    first_qkv = links.copy(qkv16, qkv_block(f), mid_peer)
    sends("up_first", [], first_up)
    sends("qkv_first", [], first_qkv)
    spreads("up_own", Group(links, up_block, f, t, masks, f), [])
    spreads("up_mid", Group(links, up_block, f, t, masks, flip(f, 2)), ["up_first"])
    spreads("qkv_own", Group(links, qkv_block, f, t, masks, f), [])
    spreads("qkv_mid", Group(links, qkv_block, f, t, masks, flip(f, 2)), ["qkv_first"])
    for h in range(2):
        at = lambda i, h=h: block(downa, ((i // 4) * 2 + i % 2) * 2 + h, half_sub)
        spreads("down" + str(h), Group(links, at, f, t, masks, f), [])
    out_in = Swap(links, out16, out_block(swapped), out_block(f), f, t, swapped)
    plan.send("out_swap", [], [out_in.start], out_in.wait)
    spreads("out", Group(links, out_block, f, t, masks, f), ["out_swap"])
    other_starts = links.copy(starts.at[pl.ds(0, 8)], starts.at[pl.ds(8, 8)], mid_peer)

    segments = seg[0:1, :]
    count = lambda n: jnp.sum((segments < n).astype(f32), axis=1, keepdims=True)
    lane = lax.broadcasted_iota(jnp.int32, (8, 128), 1)
    starts[0:8, :] = jnp.where(lane == 0, count(1), count(2))
    other_starts.start()
    for ref in (sums, qkv_sum, bias_sum):
        ref[...] = jnp.zeros_like(ref)
    for h in range(hi_n):
        at = pl.ds(pl.multiple_of((h * 2 + mid) * chunk, chunk), chunk)
        up_bias[0:1, h * chunk : (h + 1) * chunk] = sum(
            jnp.where(t == j, vec[9 + j : 10 + j, at], 0.0) for j in range(4)
        )
    head = pl.ds(pl.multiple_of((t * 2 + mid) * HD, HD), HD)
    qkv_bias = lambda: jnp.concatenate([vec[6 + c : 7 + c, head] for c in range(3)], axis=1)

    def cast_qkv(hooks):
        run_cast_qkv(qkv, 1 - mid, qkv16)
        run_cast_qkv(qkv, mid, qkv_block(f))

    def cast_up(hooks):
        run_cast(up, lambda i: i * 2 + 1 - mid, hi_n, chunk, up16)
        run_cast(up, lambda i: i * 2 + mid, hi_n, chunk, up_block(f))

    def norm_own(hooks):
        xh[here(mid * 4 + t, rows), :] = normalise(x[...].astype(f32)).astype(bf16)

    plan.compute("norm_own", [], norm_own)
    plan.compute("cast_qkv", [], cast_qkv)
    plan.compute("cast_up", [], cast_up)
    down_rows = block(downa, (f // 4) * 2 + f % 2, sub)
    plan.compute("cast_down", [], lambda hooks: run_cast(down, lambda i: i, 2, d // 2, down_rows))
    plan.compute("cast_out", [], lambda hooks: run_cast(out, lambda i: i, 1, d, out16))

    per_seq = length // TILE
    names = lambda prefix, *ends: [prefix + "_" + end for end in ends]
    of_up = names("up", "own_x", "own_zhx", "mid_x", "mid_zhx")
    of_qkv = names("qkv", "own_x", "own_zhx", "mid_x", "mid_zhx")
    of_down = ["down0_x", "down0_zhx", "down1_x", "down1_zhx"]
    of_out = ["out_x", "out_zhx"]
    plan.waits["starts"] = (other_starts.wait_recv,)
    for which, seq, arrive in (("own", mid, ("c", "y", "yc")), ("oth", 1 - mid, ("m", "mc", "my", "myc"))):
        own = which == "own"
        rotary = Rotary(table, starts, 0 if own else 1)
        index = lambda i, seq=seq: seq * per_seq + i
        es = names("es", *arrive) + ["own_e"]
        xs = names("xs", *arrive)
        plan.compute(
            "up_" + which,
            of_up + xs,
            lambda hooks, index=index: run_up(vec, up_bias, xh, upa, g, slope, index, per_seq, hooks),
        )
        plan.compute(
            "proj_" + which,
            of_qkv + xs + ["starts"],
            lambda hooks, seq=seq, rotary=rotary: run_project(vec, qkv_bias, xh, qkva, rotary, seq, p, per_seq, hooks),
        )

        def back(hooks, index=index):
            for i in range(per_seq):
                at = here(index(i))
                da[at, :] = dot(ea[at, :], outa[...], NT).astype(bf16)

        plan.compute("da_" + which, of_out + es, back)
        plan.compute(
            "attn_" + which,
            [],
            lambda hooks, seq=seq, rotary=rotary: run_attention(
                length, seq, rotary, p, da, a, dproj, dk, dv, qkv_sum
            ),
        )
        plan.compute(
            "dh_" + which,
            of_down + es,
            lambda hooks, index=index: run_hidden_grad(ea, downa, slope, dh, bias_sum, index, per_seq, hooks),
        )
    all_es = names("es", "c", "y", "yc", "m", "mc", "my", "myc") + ["own_e"]

    same = lambda i: i
    down_place = lambda i: (i // 4) * 2 + i % 2

    def scatter(name, part, place, height, mids, refs):
        s = Scatter(links, part, place, height, mids, *refs, f, t, masks)
        for far, end in ((True, "_f"), (False, "_n")):
            sends(name + end, [], *[s.copies[0, k, j] for k, j in s.each(far)])
        half = s.n_hi // 2
        sends(name + "_on", [], *[s.copies[1, k - half, j] for k, j in s.each(True)])
        plan.compute(name + "_add", [name + "_on"] if n_stage == 2 else [], lambda hooks: s.finish(n_stage == 2))
        return s

    def outer(name, s, left, right, needs, through=None):
        o = Outer(s, left, right, through)
        plan.compute(name + "_gf", needs, lambda hooks: o.give(True, hooks))
        plan.compute(name + "_gn", needs, lambda hooks: o.give(False, hooks))
        plan.compute(name + "_kf", [name + "_f"], lambda hooks: o.keep(True, hooks))
        plan.compute(name + "_kn", [name + "_n"], lambda hooks: o.keep(False, hooks))

    qkv_s = scatter("gqkv", g_qkv, same, feat, (0, 1), stage_refs[0])
    out_s = scatter("gout", g_out, lambda i: out_place(i, top), orow, (None,), stage_refs[1])
    down_s = scatter("gdown", g_down, down_place, sub, (None,), stage_refs[2])
    up_s = scatter("gup", g_up, same, feat, (0, 1), stage_refs[3])
    up_s.to = up_new
    outer("gdown", down_s, g, ea, all_es)
    outer("gqkv", qkv_s, xh, dproj, [], Through(vec, 0, qkva, qkv_sum, sums))
    outer("gup", up_s, xh, dh, [], Through(vec, 1, upa, bias_sum, sums))
    plan.compute("gout", all_es, lambda hooks: run_outer_wide(a, ea, g_out))
    plan.compute("gout_kf", ["gout_f"], lambda hooks: out_s.first_adds(True))
    plan.compute("gout_kn", ["gout_n"], lambda hooks: out_s.first_adds(False))
    out_back = Swap(links, out_s.sums[-1], out_new, out_new, f, t, swapped)
    plan.send("gout_x", [], [out_back.start], out_back.wait)

    def exchange_columns(name, job, dst):
        total = job.sums[-1]
        c = links.copy(block(total, 1 - mid, feat), dst, mid_peer)
        sends(name, [], c)

    exchange_columns("gqkv_x", qkv_s, qkv_new)

    norm_t = Tokens(links, token_refs[0], rows, f, t, run_norm_grad(vec, dh, upa, dproj, qkva))
    branch_t = Tokens(links, token_refs[1], rows, f, t, run_branch(a, outa, g, downa))
    for name, job, needs in (("norm", norm_t, []), ("branch", branch_t, of_down + of_out)):
        plan.compute(name + "_g", needs, lambda hooks, job=job: job.give(hooks))
        sends(name + "_c", [], *job.over_core)
        plan.compute(name + "_kf", [name + "_c"], lambda hooks, job=job: job.keep(True, hooks))
        plan.compute(name + "_kn", [name + "_c"], lambda hooks, job=job: job.keep(False, hooks))
        sends(name + "_y", [], *job.over_y)
        plan.compute(name + "_aa", [name + "_y"], lambda hooks, job=job: job.across())
        sends(name + "_m", [], *job.over_mid)

    small_peers = [core_peer, y_peer, mid_peer] + [(flip(f, m), t) for m in masks]
    small_copies = [links.copy(small, small_in.at[r], peer) for r, peer in enumerate(small_peers)]

    def small_fill():
        small[...] = jnp.zeros_like(small)
        small[0:4, :] = sums[0:4, :]
        small[4:5, :] = jnp.sum(ea[here(mid * 4 + t, rows), :].astype(f32), axis=0, keepdims=True)
        for c in range(3):
            small[5 + c : 6 + c, head] = qkv_sum[0:1, c * HD : (c + 1) * HD]
        for h in range(hi_n):
            at = pl.ds(pl.multiple_of((h * 2 + mid) * chunk, chunk), chunk)
            for j in range(4):
                small[8 + j : 9 + j, at] = jnp.where(t == j, bias_sum[0:1, h * chunk : (h + 1) * chunk], 0.0)
        small_copies[0].start()

    def small_add(r):
        small_copies[r].wait_send()
        small[...] += small_in[r]

    def small_step(r):
        small_add(r - 1)
        small_copies[r].start()

    def small_end(hooks):
        small_add(4)
        for r in range(5, len(small_peers)):
            small_copies[r].start()
            small_copies[r].wait_recv()
            small_add(r)

    plan.send("small0", [], [small_fill], small_copies[0].wait_recv)
    for r in range(1, 5):
        name = "small" + str(r)
        step = functools.partial(small_step, r)
        plan.send(name, ["small" + str(r - 1)], [step], small_copies[r].wait_recv)
    plan.compute("small_end", ["small4"], small_end)

    plan.carry_out([step.name for step in ORDER])
    links.drain()


ANY = pl.BlockSpec(memory_space=pl.ANY)
VMEM = pl.BlockSpec(memory_space=pltpu.VMEM)


def run_layer(masks, top, length, tp, x, e, up, qkv, down, out, seg, table, vec):
    rows, d = x.shape
    tokens = 2 * tp * rows
    mine, wide = up.shape[1] // 2, 3 * HD
    feat, sub, orow = up.shape[0], down.shape[0], out.shape[0]
    n_keys = 1 << len(masks)
    hi_n = n_keys // 2
    shapes = [
        (tokens, mine), (tokens, mine), (d, wide), (HD, d), (mine, d), (d, mine),
    ]
    copies = 2 * 7 + 2 * (1 + 2 * (n_keys - 1)) + 2 * (n_keys - 1) + n_keys + 1
    for height, width, mids in ((feat, wide, 2), (orow, d, 1), (sub, d, 1), (feat, mine, 2)):
        for _ in range(2):
            for level in range(len(masks)):
                shapes.append(((hi_n >> level) * mids * height, width))
        copies += (2 * hi_n - 1) * mids + 1
    for _ in range(2):
        shapes += [(4 * rows, d)] * 3 + [(2 * rows, d)] * 2 + [(rows, d)]
        copies += 7
    shapes += [(feat, mine), (feat, wide), (orow, d)]
    n_small = len(masks) + 3
    copies += n_small
    out_shape = [jax.ShapeDtypeStruct(shape, bf16) for shape in shapes]
    out_shape.append(jax.ShapeDtypeStruct((16, d), f32))
    held = [
        (tokens, d), (tokens, d), (d, mine), (d, wide), (mine, d), (HD, d), (feat, mine), (feat, wide), (orow, d),
        (tokens, wide), (tokens, HD), (tokens, HD), (tokens, wide), (tokens, mine),
    ]
    result = pl.pallas_call(
        functools.partial(layer_kernel, masks, top, length),
        out_shape=out_shape,
        in_specs=[ANY] * 5 + [VMEM] * 4,
        out_specs=[ANY] * len(shapes) + [VMEM],
        scratch_shapes=[pltpu.VMEM(shape, bf16) for shape in held]
        + [
            pltpu.VMEM(shape, f32)
            for shape in (
                (length, HD), (length, HD), (8, d), (8, wide), (8, mine), (8, mine), (16, 128),
                (n_small, 16, d),
            )
        ]
        + [
            pltpu.SemaphoreType.DMA((copies,)),
            pltpu.SemaphoreType.DMA((copies,)),
            pltpu.SemaphoreType.DMA((8,)),
        ],
        compiler_params=pltpu.CompilerParams(
            collective_id=0, has_side_effects=True, vmem_limit_bytes=60 * 2**20
        ),
        name="layer",
    )(e, up, qkv, down, out, seg, table, x, vec)
    stage = len(masks)
    at = N_HBM + 2 * stage * 4
    up_new, qkv_new, out_new, small = result[at + 12 : at + 16]

    def last(i):
        first = N_HBM + 2 * stage * i
        recv, sums = result[first : first + stage], result[first + stage : first + 2 * stage]
        return (sums[0], recv[1]) if stage == 2 else (sums[-1],)

    norm, branch = result[at : at + 6], result[at + 6 : at + 12]
    tokens = [(part[2], part[3], part[5]) for part in (norm, branch)]
    return tokens, (last(0), qkv_new), out_new, (last(3), up_new), last(2), small


class Moves:
    def __init__(self, sem):
        self.sem, self.count, self.out = sem, 0, []

    def copy(self, src, dst):
        c = pltpu.make_async_copy(src, dst, self.sem.at[self.count])
        self.count += 1
        c.start()
        return c

    def load(self, pairs):
        return [self.copy(src, dst) for src, dst in pairs]

    def store(self, pairs):
        self.out += [self.copy(src, dst) for src, dst in pairs]

    def drain(self):
        for c in self.out:
            c.wait()


def adam_loop(bufs, grads, rate, steps, at):
    w, m, v = bufs

    @pl.loop(0, steps)
    def _(i):
        to, of = at(i)
        g = sum(grad[of].astype(f32) for grad in grads)
        m_new, v_new, w_new = adam_step(w[to], m[to], v[to], g, rate, decay_rate)
        w[to] = w_new
        m[to] = m_new
        v[to] = v_new


ROWS = 32


def by_chunks(i):
    at = here(i, ROWS)
    return at, at


def last_blocks(refs, first, second, rows):
    return [block(ref, i, rows) for ref, i in zip(refs, (second,) if len(refs) == 1 else (first, second))]


def columns_of(ref, q, chunk):
    n = ref.shape[1] // (2 * chunk)
    return [ref.at[:, pl.ds(pl.multiple_of((h * 2 + q) * chunk, chunk), chunk)] for h in range(n)]


def side_by_side(buf, chunk):
    return [buf.at[:, h * chunk : (h + 1) * chunk] for h in range(buf.shape[1] // chunk)]


def update_kernel(chunk, rates, n, *refs):
    take = lambda k: [refs.pop(0) for _ in range(k)]
    refs = list(refs)
    qkv, out, up, down = take(3), take(3), take(3), take(3)
    qkv_last, up_last, down_last, (qkv_new, out_new) = take(n), take(n), take(n), take(2)
    qkv_o, out_o, up_o, down_o = take(3), take(3), take(3), take(3)
    qkv_b, out_b, up_b, down_b = take(3), take(3), take(3), take(3)
    qkv_g, up_g, down_g, (qkv_n, out_n) = take(n), take(n), take(n), take(2)
    moves = Moves(refs.pop(0))
    f = lax.axis_index("fsdp")
    mid, half = bit_of(f, 2), bit_of(f, 4)
    feat, sub = up[0].shape[0], down[0].shape[0]
    rate, rate_out = rates
    pair = (half * 2 + mid, mid)
    loads = {}
    loads["qkv"] = moves.load(
        [*zip(qkv, qkv_b), *zip(last_blocks(qkv_last, *pair, feat), qkv_g), (qkv_new, qkv_n)]
    )
    loads["down"] = moves.load([*zip(down, down_b), *zip(last_blocks(down_last, half, 0, sub), down_g)])
    loads["up"] = moves.load(
        [
            move
            for src, dst in zip(up, up_b)
            for move in zip(columns_of(src, mid, chunk), side_by_side(dst, chunk))
        ]
        + [*zip(last_blocks(up_last, *pair, feat), up_g)]
    )
    loads["out"] = moves.load([*zip(out, out_b), (out_new, out_n)])

    def arrive(name):
        for c in loads[name]:
            c.wait()

    arrive("qkv")
    for c in range(3):
        for q, grads in ((mid, qkv_g), (1 - mid, [qkv_n])):

            def at(i, c=c, q=q):
                rows = here(i, ROWS)
                return (c, rows, pl.ds(pl.multiple_of(q * HD, HD), HD)), (rows, slice(c * HD, (c + 1) * HD))

            adam_loop(qkv_b, grads, rate, feat // ROWS, at)
    moves.store(zip((qkv_b[1], qkv_b[2], qkv_b[0]), qkv_o))
    arrive("down")
    adam_loop(down_b, down_g, rate, sub // ROWS, by_chunks)
    moves.store(zip((down_b[1], down_b[2], down_b[0]), down_o))
    arrive("up")
    adam_loop(up_b, up_g, rate, feat // ROWS, by_chunks)
    moves.store(
        [
            move
            for src, dst in zip((up_b[1], up_b[2], up_b[0]), up_o)
            for move in zip(side_by_side(src, chunk), columns_of(dst, mid, chunk))
        ]
    )
    arrive("out")
    rows = min(out[0].shape[0], ROWS)
    adam_loop(out_b, [out_n], rate_out, out[0].shape[0] // rows, lambda i: (here(i, rows), here(i, rows)))
    moves.store(zip((out_b[1], out_b[2], out_b[0]), out_o))
    moves.drain()


def finish_kernel(chunk, rate, x, e, vec, *refs):
    take = lambda k: [refs.pop(0) for _ in range(k)]
    refs = list(refs)
    norm, branch, up, (up_new,), _ = take(3), take(3), take(3), take(1), take(3)
    tokens_o, up_o = take(2), take(3)
    x_b, e_b = take(2)
    parts_b, up_b, (up_g,), out_b = take(6), take(3), take(1), take(2)
    moves = Moves(refs.pop(0))
    f = lax.axis_index("fsdp")
    t = lax.axis_index("tp")
    mid = bit_of(f, 2)
    rows, feat = x.shape[0], up[0].shape[0]
    up_loads = moves.load(
        [
            move
            for src, dst in zip(up, up_b)
            for move in zip(columns_of(src, 1 - mid, chunk), side_by_side(dst, chunk))
        ]
        + [(up_new, up_g)]
    )
    where = lambda part: [block(part[0], mid * 2 + t // 2, rows), block(part[1], mid, rows), part[2]]
    token_loads = moves.load([(x, x_b), (e, e_b), *zip(where(norm) + where(branch), parts_b)])
    for c in up_loads:
        c.wait()
    adam_loop(up_b, [up_g], rate, feat // ROWS, by_chunks)
    moves.store(
        [
            move
            for src, dst in zip((up_b[1], up_b[2], up_b[0]), up_o)
            for move in zip(side_by_side(src, chunk), columns_of(dst, 1 - mid, chunk))
        ]
    )
    for c in token_loads:
        c.wait()
    bias = vec[4:5, :] + vec[5:6, :]

    @pl.loop(0, rows // ROWS)
    def _(i):
        at = here(i, ROWS)
        add = lambda part: sum(ref[at, :].astype(f32) for ref in part)
        stream = x_b[at, :].astype(f32)
        out_b[0][at, :] = stream + add(parts_b[3:]) + bias
        scaled = add(parts_b[:3])
        normal, inverse = normalise(stream, True)
        out_b[1][at, :] = e_b[at, :].astype(f32) + inverse * (
            scaled
            - jnp.mean(scaled, axis=-1, keepdims=True)
            - normal * jnp.mean(scaled * normal, axis=-1, keepdims=True)
        )

    moves.store(zip(out_b, tokens_o))
    moves.drain()


def run_update(chunk, rates, qkv, out_new, up_last, down_last, weights):
    n = len(up_last)
    flat = [w for group in weights for w in group]
    grads = [*qkv[0], *up_last, *down_last, qkv[1], out_new]
    feat, sub = weights[2][0].shape[0], weights[3][0].shape[0]
    wide, mine, d = qkv[1].shape[1], up_last[0].shape[1], weights[3][0].shape[1]
    half_up = (feat, mine)
    held = [w.shape for w in flat[:6]] + [half_up] * 3 + [w.shape for w in flat[9:]]
    held_grads = [(feat, wide)] * n + [half_up] * n + [(sub, d)] * n + [(feat, wide), out_new.shape]
    pieces = weights[2][0].shape[1] // (2 * chunk)
    n_bytes = 8 * sum(w.size for w in flat)
    return pl.pallas_call(
        functools.partial(update_kernel, chunk, rates, n),
        out_shape=[jax.ShapeDtypeStruct(w.shape, f32) for w in flat],
        in_specs=[ANY] * (len(flat) + len(grads)),
        out_specs=[ANY] * len(flat),
        scratch_shapes=[pltpu.VMEM(shape, f32) for shape in held]
        + [pltpu.VMEM(shape, bf16) for shape in held_grads]
        + [pltpu.SemaphoreType.DMA((2 * 9 + 2 * 3 * pieces + 3 * n + 2,))],
        compiler_params=pltpu.CompilerParams(vmem_limit_bytes=56 * 2**20),
        cost_estimate=pl.CostEstimate(flops=0, bytes_accessed=n_bytes, transcendentals=0),
        name="update",
    )(*flat, *grads)


def run_finish(chunk, rate, x, e, vec, tokens, up, up_new, up_done):
    rows, d = x.shape
    half_up = up_new.shape
    token = jax.ShapeDtypeStruct(x.shape, f32)
    pieces = up[0].shape[1] // (2 * chunk)
    return pl.pallas_call(
        functools.partial(finish_kernel, chunk, rate),
        out_shape=[token, token] + [jax.ShapeDtypeStruct(w.shape, f32) for w in up],
        in_specs=[ANY, ANY, VMEM] + [ANY] * 13,
        out_specs=[ANY] * 5,
        input_output_aliases={13: 2, 14: 3, 15: 4},
        scratch_shapes=[pltpu.VMEM((rows, d), bf16)] * 8
        + [pltpu.VMEM(half_up, f32)] * 3
        + [pltpu.VMEM(half_up, bf16)]
        + [pltpu.VMEM((rows, d), f32)] * 2
        + [pltpu.SemaphoreType.DMA((2 * 3 * pieces + 1 + 8 + 2,))],
        compiler_params=pltpu.CompilerParams(vmem_limit_bytes=56 * 2**20),
        name="finish",
    )(x, e, vec, *tokens[0], *tokens[1], *up, up_new, *up_done)


def make_local(fsdp, tp):
    masks = [1 << b for b in range(2, fsdp.bit_length() - 1)] + [1]
    top = fsdp // 2

    def local(
        layer_input,
        out_cotangent,
        segments,
        qkv_weight,
        qkv_first,
        qkv_second,
        out_weight,
        out_first,
        out_second,
        up_weight,
        up_first,
        up_second,
        down_weight,
        down_first,
        down_second,
        small_params,
        small_first,
        small_second,
    ):
        d = layer_input.shape[1]
        length = segments.shape[1]
        chunk = 2 * down_weight.shape[1]
        lanes = np.arange(128)
        rate = 10000.0 ** (-(2.0 * (lanes % (ROT // 2))) / ROT)
        angle = np.arange(length)[:, None] * rate[None]
        rates = np.broadcast_to(rate, angle.shape)
        table = jnp.asarray(np.concatenate([np.cos(angle), np.sin(angle), rates], 1), f32)
        vec = small_params.reshape(-1, d)
        token_parts, qkv_parts, out_new, up_parts, down_last, small = run_layer(
            masks, top, length, tp, layer_input, out_cotangent, up_weight[0], qkv_weight[0], down_weight[0],
            out_weight[0], segments, table, vec,
        )
        weights = (
            (qkv_weight[0], qkv_first[0], qkv_second[0]),
            (out_weight[0], out_first[0], out_second[0]),
            (up_weight[0], up_first[0], up_second[0]),
            (down_weight[0], down_first[0], down_second[0]),
        )
        rates = (d ** (-0.5), 4.0 * d ** (-0.5))
        up_last, up_give = up_parts
        up_new = lax.ppermute(up_give, "fsdp", [(i, i ^ 2) for i in range(fsdp)])
        updated = run_update(chunk, rates, qkv_parts, out_new, up_last, down_last, weights)
        finished = run_finish(
            chunk, rates[0], layer_input, out_cotangent, vec, token_parts, weights[2], up_new, updated[6:9]
        )
        results = [*finished[:2], *updated[:6], *finished[2:], *updated[9:]]
        small_total = jnp.concatenate([small[0:5], small[4:5], small[5:12]]).reshape(1, -1)
        small_updated = adam_step(small_params, small_first, small_second, small_total, rate_vector, 0.0)
        return (*results[:2], *[w[None] for w in results[2:]], *small_updated)

    return local


def solution(mesh):
    tokens = P(("fsdp", "tp"), None)
    inner = P(None, ("tp", "fsdp"), None)
    qkv = P(None, None, "fsdp", "tp")
    up = P(None, "fsdp", "tp")
    weights = (qkv,) * 3 + (inner,) * 3 + (up,) * 3 + (inner,) * 3 + (P(),) * 3
    return jax.shard_map(
        make_local(mesh.shape["fsdp"], mesh.shape["tp"]),
        mesh=mesh,
        in_specs=(tokens, tokens, P("fsdp", None)) + weights,
        out_specs=(tokens, tokens) + weights,
        check_vma=False,
    )
```

```python
import enum
import functools

import jax
import jax.numpy as jnp
import numpy as np
from jax import lax
from jax.experimental import pallas as pl
from jax.experimental.pallas import tpu as pltpu
from jax.sharding import PartitionSpec as P

HD = 256
ROT = 64
STEP = 10

norm_eps = 1e-05
beta_one = 0.9
beta_two = 0.95
adam_eps = 1e-08
decay_rate = 0.01
rate_vector = 0.2
masked_score = -1e30
f32 = jnp.float32
bf16 = jnp.bfloat16


def adam_step(weight, first, second, grad, rate, decay):
    first_new = beta_one * first + (1.0 - beta_one) * grad
    second_new = beta_two * second + (1.0 - beta_two) * grad * grad
    first_hat = first_new / (1.0 - beta_one**STEP)
    second_hat = second_new / (1.0 - beta_two**STEP)
    weight_new = weight - rate * (first_hat / (jnp.sqrt(second_hat) + adam_eps) + decay * weight)
    return (first_new, second_new, weight_new)


MESH = pl.DeviceIdType.MESH


def bit_of(i, mask):
    return (i // mask) % 2


def flip(i, mask):
    return i + mask - 2 * mask * bit_of(i, mask)


class Copy:
    def __init__(self, copy):
        self.copy, self.started, self.received, self.sent = copy, False, False, False

    def start(self):
        self.started = True
        self.copy.start()

    def wait_recv(self):
        self.received = True
        self.copy.wait_recv()

    def wait_send(self):
        self.sent = True
        self.copy.wait_send()


class Local:
    def __init__(self, copy):
        self.copy, self.started, self.done = copy, False, False

    def start(self):
        self.started = True
        self.copy.start()

    def wait(self):
        self.done = True
        self.copy.wait()


class Links:
    def __init__(self, send_sem, recv_sem, local_sem):
        self.send_sem, self.recv_sem, self.local_sem = send_sem, recv_sem, local_sem
        self.copies, self.locals, self.swaps, self.n_local = [], [], [], 0

    def local(self, src, dst):
        c = Local(pltpu.make_async_copy(src, dst, self.local_sem.at[self.n_local]))
        self.n_local += 1
        self.locals.append(c)
        return c

    def copy(self, src, dst, device):
        k = len(self.copies)
        c = Copy(
            pltpu.make_async_remote_copy(
                src_ref=src,
                dst_ref=dst,
                send_sem=self.send_sem.at[k],
                recv_sem=self.recv_sem.at[k],
                device_id=device,
                device_id_type=MESH,
            )
        )
        self.copies.append(c)
        return c

    def drain(self):
        for c in self.copies:
            if c.started and not c.received:
                c.wait_recv()
            if c.started and not c.sent:
                c.wait_send()
        for c in self.locals:
            if c.started and not c.done:
                c.wait()
        for c in self.swaps:
            c.drain()


class Group:
    def __init__(self, links, at, f, t, masks, root):
        self.copies, self.masks = {}, masks
        for key in all_keys(masks):
            g = root
            for mask in masks:
                if key & mask:
                    g = flip(g, mask)
            ref = at(g)
            after = max([i + 1 for i, m in enumerate(masks) if key & m], default=0)
            for mask in masks[after:]:
                self.copies[key | mask] = links.copy(ref, ref, (flip(f, mask), t))

    def low(self):
        self.copies[1].start()

    def high(self):
        self.copies[self.masks[0]].start()

    def rest(self):
        keys = all_keys(self.masks[:-1])
        for s, mask in enumerate(self.masks[1:-1]):
            for key in all_keys(self.masks[: s + 1]):
                if key:
                    self.copies[key].wait_recv()
                self.copies[key | mask].start()
        last = self.masks[-2]
        for key in keys:
            if key & last:
                self.copies[key].wait_recv()
            if key:
                self.copies[key | 1].start()

    def ends(self):
        return [c for key, c in self.copies.items() if key & 1]


def all_keys(masks):
    keys = [0]
    for mask in masks:
        keys = keys + [k | mask for k in keys]
    return keys


def normalise(x, with_inverse=False):
    mean = jnp.mean(x, axis=-1, keepdims=True)
    centred = x - mean
    inverse = lax.rsqrt(jnp.mean(centred * centred, axis=-1, keepdims=True) + norm_eps)
    return (centred * inverse, inverse) if with_inverse else centred * inverse


def rope(u, c, s):
    lane = lax.broadcasted_iota(jnp.int32, u.shape, 1)
    partner = jnp.where(lane < ROT // 2, pltpu.roll(u, 128 - ROT // 2, 1), pltpu.roll(u, ROT // 2, 1))
    return u * c + partner * s


def dot(a, b, dims):
    return lax.dot_general(a, b, (dims, ((), ())), preferred_element_type=f32)


NN = ((1,), (0,))
NT = ((1,), (1,))
TN = ((0,), (0,))
TILE = 256


def pipe(body, steps, ins, outs, hooks=()):
    def whole(*refs):
        for i, n, run in hooks:
            pl.when(pl.program_id(0) == i * steps // n)(run)
        body(*refs)

    pltpu.emit_pipeline(
        whole,
        grid=(steps,),
        in_specs=[spec for _, spec in ins],
        out_specs=[spec for _, spec in outs],
    )(*[ref for ref, _ in ins], *[ref for ref, _ in outs])


def by_rows(ref, index=lambda i: i, rows=TILE):
    return ref, pl.BlockSpec((rows, ref.shape[1]), lambda i: (index(i), 0))


def by_columns(ref, index, width):
    return ref, pl.BlockSpec((ref.shape[0], width), lambda i: (0, index(i)))


def here(i, rows=TILE):
    return pl.ds(pl.multiple_of(i * rows, rows), rows)


def run_cast(weight, index, steps, width, dst):
    def body(w_ref):
        at = pl.ds(pl.multiple_of(pl.program_id(0) * width, width), width)
        dst[:, at] = w_ref[...].astype(bf16)

    pipe(body, steps, [by_columns(weight, index, width)], [])


def run_cast_qkv(weight, half, dst):
    def body(w_ref):
        at = pl.ds(pl.multiple_of(pl.program_id(0) * HD, HD), HD)
        dst[:, at] = w_ref[...].reshape(w_ref.shape[-2:]).astype(bf16)

    spec = pl.BlockSpec((1, weight.shape[1], HD), lambda i: (i, 0, half))
    pipe(body, 3, [(weight, spec)], [])


class Rotary:
    def __init__(self, table, starts, seq):
        self.table, self.starts, self.seq = table, starts, seq

    def bounds(self):
        at = pl.ds(self.seq * 8, 1)
        return self.starts[at, 0:1].astype(jnp.int32), self.starts[at, 1:2].astype(jnp.int32)

    def __call__(self, tile):
        shape = (TILE, 128)
        lane = lax.broadcasted_iota(jnp.int32, (1, 128), 1)
        first, second = self.bounds()
        turning = lane < ROT
        rate = self.table[0:1, 256:384]
        one, two = first.astype(f32) * rate, second.astype(f32) * rate
        index = tile * TILE + lax.broadcasted_iota(jnp.int32, shape, 0)
        pick = lambda a, b, c: jnp.where(index >= second, c, jnp.where(index >= first, b, a))
        cos_b = pick(jnp.ones_like(one), jnp.cos(one), jnp.cos(two))
        sin_b = pick(jnp.zeros_like(one), jnp.sin(one), jnp.sin(two))
        rows = here(tile)
        cos_t, sin_t = self.table[rows, 0:128], self.table[rows, 128:256]
        sign = jnp.where(lane < ROT // 2, -1.0, 1.0)
        c = jnp.where(turning, cos_t * cos_b + sin_t * sin_b, 1.0)
        s = jnp.where(turning, sign * (sin_t * cos_b - cos_t * sin_b), 0.0)
        return c, s


def normed(vec, k, xh, at):
    return (xh[at, :].astype(f32) * vec[2 * k : 2 * k + 1, :] + vec[2 * k + 1 : 2 * k + 2, :]).astype(bf16)


def run_project(vec, qkv_bias, xh, w, rotary, seq, p, steps, hooks=()):
    def body():
        i = pl.program_id(0)
        at = here(seq * steps + i)
        c, s = rotary(i)
        proj = dot(normed(vec, 0, xh, at), w[...], NN) + qkv_bias()
        for j in range(2):
            p[at, j * HD : j * HD + 128] = rope(proj[:, j * HD : j * HD + 128], c, s).astype(bf16)
            p[at, j * HD + 128 : (j + 1) * HD] = proj[:, j * HD + 128 : (j + 1) * HD].astype(bf16)
        p[at, 2 * HD :] = proj[:, 2 * HD :].astype(bf16)

    pipe(body, steps, [], [], hooks)


def run_up(vec, up_bias, xh, w, g, slope, index, steps, hooks=()):
    width = w.shape[1]
    part = min(width, 256)

    def body(g_ref, s_ref):
        n = normed(vec, 1, xh, here(index(pl.program_id(0))))
        for j in range(0, width, part):
            h = dot(n, w[:, j : j + part], NN) + up_bias[0:1, j : j + part]
            cdf = 0.5 + 0.5 * lax.erf(h * 0.7071067811865476)
            g_ref[:, j : j + part] = (h * cdf).astype(bf16)
            s_ref[:, j : j + part] = (cdf + h * (jnp.exp(-0.5 * h * h) * 0.3989422804014327)).astype(bf16)

    pipe(body, steps, [], [by_rows(g, index), by_rows(slope, index)], hooks)


def run_attention(length, seq, rotary, p, da, a, dproj, dk, dv, sums):
    scale = HD ** (-0.5)
    tiles_n = length // TILE
    first, second = rotary.bounds()
    rows = lambda i: here(seq * tiles_n + i)

    def put(i, value, column):
        c, s = rotary(i)
        keep(i, rope(value[:, :128], c, -s), column)
        keep(i, value[:, 128:], column + 128)

    def keep(i, value, column):
        value = value.astype(bf16)
        at = slice(column, column + value.shape[1])
        dproj[rows(i), at] = value
        sums[0:1, at] += jnp.sum(value.astype(f32), axis=0, keepdims=True)

    dk[...] = jnp.zeros_like(dk)
    dv[...] = jnp.zeros_like(dv)
    for i in range(tiles_n):
        n = (i + 1) * TILE
        until = pl.ds(pl.multiple_of(seq * length, length), n)
        q = p[rows(i), 0:HD]
        k = p[until, HD : 2 * HD]
        v = p[until, 2 * HD :]
        rows_da = da[rows(i), :]
        scores = dot(q, k, NT) * scale
        qi = i * TILE + lax.broadcasted_iota(jnp.int32, (TILE, n), 0)
        ki = lax.broadcasted_iota(jnp.int32, (TILE, n), 1)
        start = jnp.where(qi >= second, second, jnp.where(qi >= first, first, 0))
        scores = jnp.where((ki <= qi) & (ki >= start), scores, masked_score)
        peak = jnp.max(scores, axis=-1, keepdims=True)
        raised = jnp.exp(scores - peak)
        probs = raised * (1.0 / jnp.sum(raised, axis=-1, keepdims=True))
        weights = probs.astype(bf16)
        a[rows(i), :] = dot(weights, v, NN).astype(bf16)
        prob_grad = dot(rows_da, v, NT)
        delta = jnp.sum(probs * prob_grad, axis=-1, keepdims=True)
        score_grad = (probs * (prob_grad - delta)).astype(bf16)
        put(i, dot(score_grad, k, NN) * scale, 0)
        dk[0:n, :] += dot(score_grad, q, TN)
        dv[0:n, :] += dot(weights, rows_da, TN)
    for i in range(tiles_n):
        local = slice(i * TILE, (i + 1) * TILE)
        put(i, dk[local, :] * scale, HD)
        keep(i, dv[local, :], 2 * HD)


def column_of(row):
    return jnp.broadcast_to(row, (128, row.shape[1])).T[:, 0:1]


def row_of(column):
    return jnp.broadcast_to(column, (column.shape[0], 128)).T[0:1, :]


class Through:
    def __init__(self, vec, k, w, d_sum, sums):
        self.vec, self.k, self.w, self.d_sum, self.sums = vec, k, w, d_sum, sums

    def __call__(self, value, index):
        n = value.shape[0]
        at = here(index, n)
        w = self.w[at, :].astype(f32)
        total = self.d_sum[0:1, :]
        self.sums[2 * self.k : 2 * self.k + 1, at] = row_of(jnp.sum(w * value, axis=1, keepdims=True))
        self.sums[2 * self.k + 1 : 2 * self.k + 2, at] = row_of(jnp.sum(w * total, axis=1, keepdims=True))
        gain = column_of(self.vec[2 * self.k : 2 * self.k + 1, at])
        shift = column_of(self.vec[2 * self.k + 1 : 2 * self.k + 2, at])
        return value * gain + shift * total


def run_outer(a, b, out, index_in, index_out, steps, width, add=None, through=None, hooks=()):
    def body(*refs):
        index = index_in(pl.program_id(0))
        left = a[:, here(index, width)] if through else refs[0][...]
        value = dot(left, b[...], TN)
        if through:
            value = through(value, index)
        if add is not None:
            value = value + refs[-2][...].astype(f32)
        refs[-1][...] = value.astype(bf16)

    ins = [] if through else [by_columns(a, index_in, width)]
    if add is not None:
        ins.append(by_rows(add, index_out, width))
    pipe(body, steps, ins, [by_rows(out, index_out, width)], hooks)


def run_outer_wide(a, b, out):
    width = 2 * TILE

    def body(out_ref):
        at = pl.ds(pl.multiple_of(pl.program_id(0) * width, width), width)
        out_ref[...] = dot(a[...], b[:, at], TN).astype(bf16)

    pipe(body, b.shape[1] // width, [], [by_columns(out, lambda i: i, width)])


def run_hidden_grad(e, w, slope, dh, bias_sum, index, steps, hooks=()):
    def body(s_ref):
        at = here(index(pl.program_id(0)))
        value = (dot(e[at, :], w[...], NT) * s_ref[...].astype(f32)).astype(bf16)
        dh[at, :] = value
        bias_sum[0:1, :] += jnp.sum(value.astype(f32), axis=0, keepdims=True)

    pipe(body, steps, [by_rows(slope, index)], [], hooks)


def run_norm_grad(vec, dh, w_up, dproj, w_qkv):
    def tile(at):
        one = dot(dproj[at, :], w_qkv[...], NT)
        two = dot(dh[at, :], w_up[...], NT)
        return one * vec[0:1, :] + two * vec[2:3, :]

    return None, tile


def run_branch(a, w_out, g, w_down):
    def tile(at, g_ref):
        return dot(a[at, :], w_out[...], NN) + dot(g_ref[...], w_down[...], NN)

    return g, tile


def run_token_tiles(job, out, index, index_out, steps, add=None, hooks=()):
    source, tile = job

    def body(*refs):
        value = tile(here(index(pl.program_id(0))), *([] if source is None else refs[:1]))
        if add is not None:
            value = value + refs[-2][...].astype(f32)
        refs[-1][...] = value.astype(bf16)

    ins = [] if source is None else [by_rows(source, index)]
    if add is not None:
        ins.append(by_rows(add, index_out))
    pipe(body, steps, ins, [by_rows(out, index_out)], hooks)


def run_add(a, b, out):
    rows, cols = out.shape
    step = min(rows, TILE)

    def body(a_ref, b_ref, out_ref):
        out_ref[...] = (a_ref[...].astype(f32) + b_ref[...].astype(f32)).astype(bf16)

    pipe(body, rows // step, [by_rows(a, rows=step), by_rows(b, rows=step)], [by_rows(out, rows=step)])


def block(ref, index, rows):
    return ref.at[pl.ds(pl.multiple_of(index * rows, rows), rows)]


def out_place(g, top):
    return (((g // 4) % (top // 4)) * 2 + g // top) * 2 + g % 2


class Scatter:
    def __init__(self, links, part, place, rows, mids, recv, sums, f, t, masks):
        self.links, self.part, self.place, self.rows, self.mids = links, part, place, rows, mids
        self.recv, self.sums, self.f, self.t = recv, sums, f, t
        self.stages = [1] + [m for m in reversed(masks) if m != 1]
        self.n_hi = 1 << (len(masks) - 1)
        self.hi, self.lo, self.mid = f // 4, f % 2, bit_of(f, 2)
        self.half = self.hi % 2
        self.to = None
        self.copies = {}
        for k in range(self.n_hi):
            for j, m in enumerate(mids):
                self.copies[0, k, j] = links.copy(
                    block(part, self.at_place(self.high(k), m, 1 - self.lo), rows),
                    block(recv[0], self.slot(0, k, j), rows),
                    (flip(f, 1), t),
                )
        for level in range(len(self.stages) - 1):
            n = self.n_hi >> (level + 1)
            for k in range(n, 2 * n):
                for j in range(len(mids)):
                    self.copies[level + 1, k - n, j] = links.copy(
                        block(sums[level], self.slot(level, k, j), rows),
                        block(recv[level + 1], self.slot(level + 1, k, j), rows),
                        (flip(f, self.stages[level + 1]), t),
                    )

    def high(self, k):
        hi, b = self.hi, 1
        while b < self.n_hi:
            if k & b:
                hi = flip(hi, b)
            b *= 2
        return hi

    def slot(self, level, k, j):
        n = self.n_hi >> level
        i = (self.high(k) % n) if n > 1 else 0
        return i * len(self.mids) + j

    def at_place(self, hi, m, lo):
        return self.place((hi * 2 + (self.mid if m is None else m)) * 2 + lo)

    def ks(self, far):
        half = self.n_hi // 2
        return range(half, self.n_hi) if far else range(half)

    def each(self, far):
        return [(k, j) for k in self.ks(far) for j in range(len(self.mids))]

    def tile(self, i, far, lo):
        n = len(self.mids)
        half = self.n_hi // 2
        upper = self.hi // half
        hi = (1 - upper if far else upper) * half + i // n
        j = i % n
        m = None if self.mids[0] is None else j
        return self.at_place(hi, m, lo), hi * n + j

    def add(self, level, k, j):
        mine = (
            block(self.part, self.at_place(self.high(k), self.mids[j], self.lo), self.rows)
            if level == 0
            else block(self.sums[level - 1], self.slot(level - 1, k, j), self.rows)
        )
        at = self.slot(level, k, j)
        run_add(mine, block(self.recv[level], at, self.rows), block(self.sums[level], at, self.rows))

    def first_adds(self, far):
        for k, j in self.each(far):
            self.add(0, k, j)

    def finish(self, waited):
        if waited:
            if len(self.mids) == 1:
                self.add(1, 0, 0)
            else:
                other = 1 - self.mid
                at = self.half * 2 + other
                to = block(self.sums[1], other, self.rows) if self.to is None else self.to
                run_add(block(self.sums[0], at, self.rows), block(self.recv[1], other, self.rows), to)
            return
        for level in range(1, len(self.stages)):
            n = self.n_hi >> level
            for k in reversed(range(n)):
                for j in range(len(self.mids)):
                    self.copies[level, k, j].wait_recv()
                    self.add(level, k, j)
                    if level + 1 < len(self.stages) and k & (n // 2):
                        self.copies[level + 1, k - n // 2, j].start()
        if self.to is not None:
            self.links.local(block(self.sums[-1], 1 - self.mid, self.rows), self.to).start()


class Outer:
    def __init__(self, scatter, a, b, through=None):
        self.s, self.a, self.b, self.through = scatter, a, b, through
        self.fused = scatter.rows % 128 == 0
        self.steps = scatter.n_hi // 2 * len(scatter.mids)

    def give(self, far, hooks=()):
        s = self.s
        if self.fused:
            at = lambda i: s.tile(i, far, 1 - s.lo)[0]
            run_outer(self.a, self.b, s.part, at, at, self.steps, s.rows, through=self.through, hooks=hooks)
        elif far:
            same = lambda i: i
            run_outer(self.a, self.b, s.part, same, same, self.a.shape[1] // 128, 128, through=self.through, hooks=hooks)

    def keep(self, far, hooks=()):
        s = self.s
        if self.fused:
            at = lambda i: s.tile(i, far, s.lo)[0]
            to = lambda i: s.tile(i, far, s.lo)[1]
            run_outer(
                self.a, self.b, s.sums[0], at, to, self.steps, s.rows, add=s.recv[0], through=self.through, hooks=hooks
            )
        else:
            s.first_adds(far)


class Tokens:
    def __init__(self, links, refs, rows, f, t, job):
        self.give_buf, self.got, self.sum, self.got_y, self.sum_y, self.final = refs
        self.rows, self.mid, self.y, self.core, self.job = rows, bit_of(f, 2), t // 2, t % 2, job
        core_peer, y_peer, mid_peer = (f, flip(t, 1)), (f, flip(t, 2)), (flip(f, 2), t)
        self.over_core = [
            links.copy(block(self.give_buf, i, rows), block(self.got, i, rows), core_peer) for i in range(4)
        ]
        self.over_y = [
            links.copy(block(self.sum, m * 2 + 1 - self.y, rows), block(self.got_y, m, rows), y_peer)
            for m in range(2)
        ]
        self.over_mid = [links.copy(block(self.sum_y, 1 - self.mid, rows), self.final, mid_peer)]

    def give(self, hooks=()):
        index = lambda i: (i // 2) * 4 + (i % 2) * 2 + 1 - self.core
        run_token_tiles(self.job, self.give_buf, index, lambda i: i, 4, hooks=hooks)

    def keep(self, far, hooks=()):
        yy = 1 - self.y if far else self.y
        index = lambda i: i * 4 + yy * 2 + self.core
        run_token_tiles(self.job, self.sum, index, lambda i: i * 2 + yy, 2, add=self.got, hooks=hooks)

    def across(self):
        m = 1 - self.mid
        run_add(block(self.sum, m * 2 + self.y, self.rows), block(self.got_y, m, self.rows), block(self.sum_y, m, self.rows))


def greet(f, t, masks, top):
    mid = bit_of(f, 2)
    swapped = f + (top - 2) * (mid - bit_of(f, top))
    barrier = pltpu.get_barrier_semaphore()
    peers = [(flip(f, m), t) for m in masks + [2]] + [(f, flip(t, 1)), (f, flip(t, 2))]
    for peer in peers:
        pl.semaphore_signal(barrier, inc=1, device_id=peer, device_id_type=MESH)

    @pl.when(swapped != f)
    def _():
        pl.semaphore_signal(barrier, inc=1, device_id=(swapped, t), device_id_type=MESH)

    pl.semaphore_wait(barrier, len(peers) + (mid + bit_of(f, top)) % 2)
    return swapped


class Swap:
    def __init__(self, links, src, dst, stay, f, t, swapped):
        self.move = links.copy(src, dst, (swapped, t)).copy
        self.copy = pltpu.make_async_copy(src, stay, links.local_sem.at[links.n_local])
        links.n_local += 1
        links.swaps.append(self)
        self.moves, self.stays = swapped != f, swapped == f
        self.started, self.done = False, False

    def start(self):
        self.started = True
        pl.when(self.moves)(self.move.start)
        pl.when(self.stays)(self.copy.start)

    def wait(self):
        self.done = True
        pl.when(self.moves)(self.move.wait_recv)
        pl.when(self.stays)(self.copy.wait)

    def drain(self):
        if self.started and not self.done:
            self.wait()
        if self.started:
            pl.when(self.moves)(self.move.wait_send)


class S(enum.Enum):
    (
        attn_oth, attn_own, branch_aa, branch_c, branch_g, branch_kf, branch_kn, branch_m, branch_y,
        cast_down, cast_out, cast_qkv, cast_up, da_oth, da_own, dh_oth, dh_own, down0_x, down0_zh, down0_zhx,
        down1_x, down1_zh, down1_zhx, es_c, es_m, es_mc, es_my, es_myc, es_y, es_yc, gdown_f, gdown_gf,
        gdown_gn, gdown_kf, gdown_kn, gdown_n, gdown_on, gout, gout_add, gout_f, gout_kf, gout_kn, gout_n,
        gout_on, gout_x, gqkv_add, gqkv_f, gqkv_gf, gqkv_gn, gqkv_kf, gqkv_kn, gqkv_n, gqkv_on, gqkv_x,
        gup_add, gup_f, gup_gf, gup_gn, gup_kf, gup_kn, gup_n, gup_on, norm_aa, norm_c, norm_g, norm_kf,
        norm_kn, norm_m, norm_own, norm_y, out_swap, out_x, out_zh, out_zhx, proj_oth, proj_own, qkv_first,
        qkv_mid_x, qkv_mid_zh, qkv_mid_zhx, qkv_own_x, qkv_own_zh, qkv_own_zhx, small0, small1, small2,
        small3, small4, small_end, up_first, up_mid_x, up_mid_zh, up_mid_zhx, up_oth, up_own, up_own_x,
        up_own_zh, up_own_zhx, xs_c, xs_m, xs_mc, xs_my, xs_myc, xs_y, xs_yc,
    ) = range(105)


ORDER = [
    S.es_m, S.cast_up, S.norm_own, S.es_c, S.cast_qkv, S.qkv_first, S.xs_c, S.cast_out, S.out_swap,
    S.cast_down, S.qkv_own_zh, S.down0_x, S.up_own_x, S.es_y, S.qkv_mid_x, S.qkv_mid_zh, S.xs_y, S.down0_zh,
    S.xs_m, S.es_yc, S.qkv_own_zhx, S.es_my, S.down1_x, S.qkv_own_x, S.out_zh, S.out_x, S.es_mc, S.out_zhx,
    S.up_first, S.xs_yc, S.qkv_mid_zhx, S.up_own_zh, S.xs_my, S.es_myc, S.xs_mc, S.da_own, S.down0_zhx,
    S.up_mid_zh, S.up_mid_x, S.da_oth, S.proj_own, S.proj_own, S.xs_myc, S.up_own_zhx, S.proj_own,
    S.proj_own, S.attn_own, S.proj_oth, S.proj_oth, S.proj_oth, S.proj_oth, S.attn_oth, S.up_mid_zhx, S.gout,
    S.down1_zh, S.gqkv_gn, S.gqkv_gn, S.gqkv_gf, S.gout_f, S.gqkv_gf, S.gqkv_f, S.up_oth, S.up_oth, S.up_oth,
    S.up_oth, S.gout_kf, S.up_own, S.gout_on, S.up_own, S.down1_zhx, S.up_own, S.up_own, S.gdown_gf,
    S.gqkv_kf, S.gqkv_kf, S.gdown_f, S.gqkv_on, S.branch_g, S.branch_g, S.branch_g, S.branch_g, S.branch_c,
    S.dh_oth, S.dh_oth, S.dh_oth, S.dh_oth, S.dh_own, S.gqkv_n, S.dh_own, S.dh_own, S.dh_own, S.branch_kf,
    S.branch_kf, S.branch_y, S.gdown_kf, S.gdown_on, S.gup_gf, S.gup_gf, S.gup_f, S.norm_g, S.norm_g,
    S.norm_g, S.norm_g, S.gqkv_kn, S.gqkv_kn, S.gup_gn, S.norm_c, S.gup_gn, S.gqkv_add, S.gup_n, S.gqkv_x,
    S.branch_kn, S.branch_kn, S.norm_kf, S.norm_kf, S.gup_kf, S.norm_y, S.gup_kf, S.gup_on, S.branch_aa,
    S.branch_m, S.gout_n, S.gdown_gn, S.gup_kn, S.gup_kn, S.small0, S.gout_kn, S.gdown_n, S.norm_kn,
    S.small1, S.small2, S.norm_kn, S.gout_add, S.small3, S.norm_aa, S.norm_m, S.gdown_kn, S.small4, S.gout_x,
    S.gup_add, S.small_end,
]


class Plan:
    def __init__(self):
        self.actions, self.waits = {}, {}

    def send(self, name, needs, starts, *copies):
        self.actions[name] = (None, needs, starts)
        self.waits[name] = copies

    def compute(self, name, needs, run):
        self.actions[name] = (True, needs, run)

    def pending(self, name):
        found = []
        for need in self.actions[name][1]:
            found += self.waits.pop(need, ())
        return found

    def starter(self, name):
        pending, starts = self.pending(name), self.actions[name][2]

        def run():
            for c in pending:
                c()
            for start in starts:
                start()

        return run

    def carry_out(self, order):
        i = 0
        while i < len(order):
            name = order[i]
            i += 1
            compute, _, run = self.actions[name]
            if not compute:
                self.starter(name)()
                continue
            for wait in self.pending(name):
                wait()
            n = 1 + order[i:].count(name)
            hooks = []
            for part in range(1, n):
                while order[i] != name:
                    hooks.append((part, n, self.starter(order[i])))
                    i += 1
                i += 1
            run(hooks) if n > 1 else run(())


N_HBM = 6


def layer_kernel(
    masks, top, length,
    e, up, qkv, down, out, seg, table, x, vec,
    *rest,
):
    n_stage = len(masks)
    (g, slope, g_qkv, g_out, g_down, g_up), rest = rest[:N_HBM], rest[N_HBM:]
    stage_refs = []
    for _ in range(4):
        stage_refs.append((rest[:n_stage], rest[n_stage : 2 * n_stage]))
        rest = rest[2 * n_stage :]
    token_refs, rest = [rest[:6], rest[6:12]], rest[12:]
    (up_new, qkv_new, out_new, small), rest = rest[:4], rest[4:]
    (
        xh, ea, upa, qkva, downa, outa, up16, qkv16, out16, p, da, a, dproj, dh, dk, dv,
        sums, qkv_sum, bias_sum, up_bias, starts, small_in,
        send_sem, recv_sem, local_sem,
    ) = rest
    f = lax.axis_index("fsdp")
    t = lax.axis_index("tp")
    mid = bit_of(f, 2)
    rows, d = x.shape
    feat, sub, orow = up.shape[0], down.shape[0], out.shape[0]
    mine = upa.shape[1]
    chunk = 2 * sub
    hi_n = mine // chunk
    swapped = greet(f, t, masks, top)
    links = Links(send_sem, recv_sem, local_sem)
    plan = Plan()

    mid_peer, y_peer, core_peer = (flip(f, 2), t), (f, flip(t, 2)), (f, flip(t, 1))
    qkv_block = lambda i: block(qkva, i, feat)
    up_block = lambda i: block(upa, i, feat)
    half_sub = sub // 2
    out_block = lambda i: block(outa, out_place(i, top), orow)
    tok = lambda buf, m, j: block(buf, m * 4 + j, rows)

    def sends(name, needs, *copies):
        plan.send(name, needs, [c.start for c in copies], *[c.wait_recv for c in copies])

    own_e = links.local(e, tok(ea, mid, t))
    for prefix, source, buf in (("xs", None, xh), ("es", e, ea)):
        for name, needs, m, j, peer in (
            ("m", (), mid, t, mid_peer),
            ("y", (), mid, t, y_peer),
            ("c", (), mid, t, core_peer),
            ("my", ("m",), 1 - mid, t, y_peer),
            ("mc", ("m",), 1 - mid, t, core_peer),
            ("yc", ("y",), mid, flip(t, 2), core_peer),
            ("myc", ("my",), 1 - mid, flip(t, 2), core_peer),
        ):
            ref = tok(buf, m, j)
            c = links.copy(ref if needs or source is None else source, ref, peer)
            sends(prefix + "_" + name, [prefix + "_" + n for n in needs], c)
    plan.waits["own_e"] = (own_e.wait,)
    own_e.start()

    def spreads(name, group, need):
        sends(name + "_x", need, group.copies[1])
        plan.send(name + "_zh", need, [group.high], *([group.copies[masks[0]].wait_recv] if n_stage == 2 else []))
        if n_stage == 2:
            sends(name + "_zhx", [name + "_zh"], group.copies[masks[0] | 1])
        else:
            plan.send(name + "_zhx", [], [group.rest], *[c.wait_recv for c in group.ends() if c is not group.copies[1]])

    first_up = links.copy(up16, up_block(f), mid_peer)
    first_qkv = links.copy(qkv16, qkv_block(f), mid_peer)
    sends("up_first", [], first_up)
    sends("qkv_first", [], first_qkv)
    spreads("up_own", Group(links, up_block, f, t, masks, f), [])
    spreads("up_mid", Group(links, up_block, f, t, masks, flip(f, 2)), ["up_first"])
    spreads("qkv_own", Group(links, qkv_block, f, t, masks, f), [])
    spreads("qkv_mid", Group(links, qkv_block, f, t, masks, flip(f, 2)), ["qkv_first"])
    for h in range(2):
        at = lambda i, h=h: block(downa, ((i // 4) * 2 + i % 2) * 2 + h, half_sub)
        spreads("down" + str(h), Group(links, at, f, t, masks, f), [])
    out_in = Swap(links, out16, out_block(swapped), out_block(f), f, t, swapped)
    plan.send("out_swap", [], [out_in.start], out_in.wait)
    spreads("out", Group(links, out_block, f, t, masks, f), ["out_swap"])
    other_starts = links.copy(starts.at[pl.ds(0, 8)], starts.at[pl.ds(8, 8)], mid_peer)

    segments = seg[0:1, :]
    count = lambda n: jnp.sum((segments < n).astype(f32), axis=1, keepdims=True)
    lane = lax.broadcasted_iota(jnp.int32, (8, 128), 1)
    starts[0:8, :] = jnp.where(lane == 0, count(1), count(2))
    other_starts.start()
    for ref in (sums, qkv_sum, bias_sum):
        ref[...] = jnp.zeros_like(ref)
    for h in range(hi_n):
        at = pl.ds(pl.multiple_of((h * 2 + mid) * chunk, chunk), chunk)
        up_bias[0:1, h * chunk : (h + 1) * chunk] = sum(
            jnp.where(t == j, vec[9 + j : 10 + j, at], 0.0) for j in range(4)
        )
    head = pl.ds(pl.multiple_of((t * 2 + mid) * HD, HD), HD)
    qkv_bias = lambda: jnp.concatenate([vec[6 + c : 7 + c, head] for c in range(3)], axis=1)

    def cast_qkv(hooks):
        run_cast_qkv(qkv, 1 - mid, qkv16)
        run_cast_qkv(qkv, mid, qkv_block(f))

    def cast_up(hooks):
        run_cast(up, lambda i: i * 2 + 1 - mid, hi_n, chunk, up16)
        run_cast(up, lambda i: i * 2 + mid, hi_n, chunk, up_block(f))

    def norm_own(hooks):
        xh[here(mid * 4 + t, rows), :] = normalise(x[...].astype(f32)).astype(bf16)

    plan.compute("norm_own", [], norm_own)
    plan.compute("cast_qkv", [], cast_qkv)
    plan.compute("cast_up", [], cast_up)
    down_rows = block(downa, (f // 4) * 2 + f % 2, sub)
    plan.compute("cast_down", [], lambda hooks: run_cast(down, lambda i: i, 2, d // 2, down_rows))
    plan.compute("cast_out", [], lambda hooks: run_cast(out, lambda i: i, 1, d, out16))

    per_seq = length // TILE
    names = lambda prefix, *ends: [prefix + "_" + end for end in ends]
    of_up = names("up", "own_x", "own_zhx", "mid_x", "mid_zhx")
    of_qkv = names("qkv", "own_x", "own_zhx", "mid_x", "mid_zhx")
    of_down = ["down0_x", "down0_zhx", "down1_x", "down1_zhx"]
    of_out = ["out_x", "out_zhx"]
    plan.waits["starts"] = (other_starts.wait_recv,)
    for which, seq, arrive in (("own", mid, ("c", "y", "yc")), ("oth", 1 - mid, ("m", "mc", "my", "myc"))):
        own = which == "own"
        rotary = Rotary(table, starts, 0 if own else 1)
        index = lambda i, seq=seq: seq * per_seq + i
        es = names("es", *arrive) + ["own_e"]
        xs = names("xs", *arrive)
        plan.compute(
            "up_" + which,
            of_up + xs,
            lambda hooks, index=index: run_up(vec, up_bias, xh, upa, g, slope, index, per_seq, hooks),
        )
        plan.compute(
            "proj_" + which,
            of_qkv + xs + ["starts"],
            lambda hooks, seq=seq, rotary=rotary: run_project(vec, qkv_bias, xh, qkva, rotary, seq, p, per_seq, hooks),
        )

        def back(hooks, index=index):
            for i in range(per_seq):
                at = here(index(i))
                da[at, :] = dot(ea[at, :], outa[...], NT).astype(bf16)

        plan.compute("da_" + which, of_out + es, back)
        plan.compute(
            "attn_" + which,
            [],
            lambda hooks, seq=seq, rotary=rotary: run_attention(
                length, seq, rotary, p, da, a, dproj, dk, dv, qkv_sum
            ),
        )
        plan.compute(
            "dh_" + which,
            of_down + es,
            lambda hooks, index=index: run_hidden_grad(ea, downa, slope, dh, bias_sum, index, per_seq, hooks),
        )
    all_es = names("es", "c", "y", "yc", "m", "mc", "my", "myc") + ["own_e"]

    same = lambda i: i
    down_place = lambda i: (i // 4) * 2 + i % 2

    def scatter(name, part, place, height, mids, refs):
        s = Scatter(links, part, place, height, mids, *refs, f, t, masks)
        for far, end in ((True, "_f"), (False, "_n")):
            sends(name + end, [], *[s.copies[0, k, j] for k, j in s.each(far)])
        half = s.n_hi // 2
        sends(name + "_on", [], *[s.copies[1, k - half, j] for k, j in s.each(True)])
        plan.compute(name + "_add", [name + "_on"] if n_stage == 2 else [], lambda hooks: s.finish(n_stage == 2))
        return s

    def outer(name, s, left, right, needs, through=None):
        o = Outer(s, left, right, through)
        plan.compute(name + "_gf", needs, lambda hooks: o.give(True, hooks))
        plan.compute(name + "_gn", needs, lambda hooks: o.give(False, hooks))
        plan.compute(name + "_kf", [name + "_f"], lambda hooks: o.keep(True, hooks))
        plan.compute(name + "_kn", [name + "_n"], lambda hooks: o.keep(False, hooks))

    qkv_s = scatter("gqkv", g_qkv, same, feat, (0, 1), stage_refs[0])
    out_s = scatter("gout", g_out, lambda i: out_place(i, top), orow, (None,), stage_refs[1])
    down_s = scatter("gdown", g_down, down_place, sub, (None,), stage_refs[2])
    up_s = scatter("gup", g_up, same, feat, (0, 1), stage_refs[3])
    up_s.to = up_new
    outer("gdown", down_s, g, ea, all_es)
    outer("gqkv", qkv_s, xh, dproj, [], Through(vec, 0, qkva, qkv_sum, sums))
    outer("gup", up_s, xh, dh, [], Through(vec, 1, upa, bias_sum, sums))
    plan.compute("gout", all_es, lambda hooks: run_outer_wide(a, ea, g_out))
    plan.compute("gout_kf", ["gout_f"], lambda hooks: out_s.first_adds(True))
    plan.compute("gout_kn", ["gout_n"], lambda hooks: out_s.first_adds(False))
    out_back = Swap(links, out_s.sums[-1], out_new, out_new, f, t, swapped)
    plan.send("gout_x", [], [out_back.start], out_back.wait)

    def exchange_columns(name, job, dst):
        total = job.sums[-1]
        c = links.copy(block(total, 1 - mid, feat), dst, mid_peer)
        sends(name, [], c)

    exchange_columns("gqkv_x", qkv_s, qkv_new)

    norm_t = Tokens(links, token_refs[0], rows, f, t, run_norm_grad(vec, dh, upa, dproj, qkva))
    branch_t = Tokens(links, token_refs[1], rows, f, t, run_branch(a, outa, g, downa))
    for name, job, needs in (("norm", norm_t, []), ("branch", branch_t, of_down + of_out)):
        plan.compute(name + "_g", needs, lambda hooks, job=job: job.give(hooks))
        sends(name + "_c", [], *job.over_core)
        plan.compute(name + "_kf", [name + "_c"], lambda hooks, job=job: job.keep(True, hooks))
        plan.compute(name + "_kn", [name + "_c"], lambda hooks, job=job: job.keep(False, hooks))
        sends(name + "_y", [], *job.over_y)
        plan.compute(name + "_aa", [name + "_y"], lambda hooks, job=job: job.across())
        sends(name + "_m", [], *job.over_mid)

    small_peers = [core_peer, y_peer, mid_peer] + [(flip(f, m), t) for m in masks]
    small_copies = [links.copy(small, small_in.at[r], peer) for r, peer in enumerate(small_peers)]

    def small_fill():
        small[...] = jnp.zeros_like(small)
        small[0:4, :] = sums[0:4, :]
        small[4:5, :] = jnp.sum(ea[here(mid * 4 + t, rows), :].astype(f32), axis=0, keepdims=True)
        for c in range(3):
            small[5 + c : 6 + c, head] = qkv_sum[0:1, c * HD : (c + 1) * HD]
        for h in range(hi_n):
            at = pl.ds(pl.multiple_of((h * 2 + mid) * chunk, chunk), chunk)
            for j in range(4):
                small[8 + j : 9 + j, at] = jnp.where(t == j, bias_sum[0:1, h * chunk : (h + 1) * chunk], 0.0)
        small_copies[0].start()

    def small_add(r):
        small_copies[r].wait_send()
        small[...] += small_in[r]

    def small_step(r):
        small_add(r - 1)
        small_copies[r].start()

    def small_end(hooks):
        small_add(4)
        for r in range(5, len(small_peers)):
            small_copies[r].start()
            small_copies[r].wait_recv()
            small_add(r)

    plan.send("small0", [], [small_fill], small_copies[0].wait_recv)
    for r in range(1, 5):
        name = "small" + str(r)
        step = functools.partial(small_step, r)
        plan.send(name, ["small" + str(r - 1)], [step], small_copies[r].wait_recv)
    plan.compute("small_end", ["small4"], small_end)

    plan.carry_out([step.name for step in ORDER])
    links.drain()


ANY = pl.BlockSpec(memory_space=pl.ANY)
VMEM = pl.BlockSpec(memory_space=pltpu.VMEM)


def run_layer(masks, top, length, tp, x, e, up, qkv, down, out, seg, table, vec):
    rows, d = x.shape
    tokens = 2 * tp * rows
    mine, wide = up.shape[1] // 2, 3 * HD
    feat, sub, orow = up.shape[0], down.shape[0], out.shape[0]
    n_keys = 1 << len(masks)
    hi_n = n_keys // 2
    shapes = [
        (tokens, mine), (tokens, mine), (d, wide), (HD, d), (mine, d), (d, mine),
    ]
    copies = 2 * 7 + 2 * (1 + 2 * (n_keys - 1)) + 2 * (n_keys - 1) + n_keys + 1
    for height, width, mids in ((feat, wide, 2), (orow, d, 1), (sub, d, 1), (feat, mine, 2)):
        for _ in range(2):
            for level in range(len(masks)):
                shapes.append(((hi_n >> level) * mids * height, width))
        copies += (2 * hi_n - 1) * mids + 1
    for _ in range(2):
        shapes += [(4 * rows, d)] * 3 + [(2 * rows, d)] * 2 + [(rows, d)]
        copies += 7
    shapes += [(feat, mine), (feat, wide), (orow, d)]
    n_small = len(masks) + 3
    copies += n_small
    out_shape = [jax.ShapeDtypeStruct(shape, bf16) for shape in shapes]
    out_shape.append(jax.ShapeDtypeStruct((16, d), f32))
    held = [
        (tokens, d), (tokens, d), (d, mine), (d, wide), (mine, d), (HD, d), (feat, mine), (feat, wide), (orow, d),
        (tokens, wide), (tokens, HD), (tokens, HD), (tokens, wide), (tokens, mine),
    ]
    result = pl.pallas_call(
        functools.partial(layer_kernel, masks, top, length),
        out_shape=out_shape,
        in_specs=[ANY] * 5 + [VMEM] * 4,
        out_specs=[ANY] * len(shapes) + [VMEM],
        scratch_shapes=[pltpu.VMEM(shape, bf16) for shape in held]
        + [
            pltpu.VMEM(shape, f32)
            for shape in (
                (length, HD), (length, HD), (8, d), (8, wide), (8, mine), (8, mine), (16, 128),
                (n_small, 16, d),
            )
        ]
        + [
            pltpu.SemaphoreType.DMA((copies,)),
            pltpu.SemaphoreType.DMA((copies,)),
            pltpu.SemaphoreType.DMA((8,)),
        ],
        compiler_params=pltpu.CompilerParams(
            collective_id=0, has_side_effects=True, vmem_limit_bytes=60 * 2**20
        ),
        name="layer",
    )(e, up, qkv, down, out, seg, table, x, vec)
    stage = len(masks)
    at = N_HBM + 2 * stage * 4
    up_new, qkv_new, out_new, small = result[at + 12 : at + 16]

    def last(i):
        first = N_HBM + 2 * stage * i
        recv, sums = result[first : first + stage], result[first + stage : first + 2 * stage]
        return (sums[0], recv[1]) if stage == 2 else (sums[-1],)

    norm, branch = result[at : at + 6], result[at + 6 : at + 12]
    tokens = [(part[2], part[3], part[5]) for part in (norm, branch)]
    return tokens, (last(0), qkv_new), out_new, (last(3), up_new), last(2), small


class Moves:
    def __init__(self, sem):
        self.sem, self.count, self.out = sem, 0, []

    def copy(self, src, dst):
        c = pltpu.make_async_copy(src, dst, self.sem.at[self.count])
        self.count += 1
        c.start()
        return c

    def load(self, pairs):
        return [self.copy(src, dst) for src, dst in pairs]

    def store(self, pairs):
        self.out += [self.copy(src, dst) for src, dst in pairs]

    def drain(self):
        for c in self.out:
            c.wait()


def adam_loop(bufs, grads, rate, steps, at):
    w, m, v = bufs

    @pl.loop(0, steps)
    def _(i):
        to, of = at(i)
        g = sum(grad[of].astype(f32) for grad in grads)
        m_new, v_new, w_new = adam_step(w[to], m[to], v[to], g, rate, decay_rate)
        w[to] = w_new
        m[to] = m_new
        v[to] = v_new


ROWS = 32


def by_chunks(i):
    at = here(i, ROWS)
    return at, at


def last_blocks(refs, first, second, rows):
    return [block(ref, i, rows) for ref, i in zip(refs, (second,) if len(refs) == 1 else (first, second))]


def columns_of(ref, q, chunk):
    n = ref.shape[1] // (2 * chunk)
    return [ref.at[:, pl.ds(pl.multiple_of((h * 2 + q) * chunk, chunk), chunk)] for h in range(n)]


def side_by_side(buf, chunk):
    return [buf.at[:, h * chunk : (h + 1) * chunk] for h in range(buf.shape[1] // chunk)]


def update_kernel(chunk, rates, n, *refs):
    take = lambda k: [refs.pop(0) for _ in range(k)]
    refs = list(refs)
    qkv, out, up, down = take(3), take(3), take(3), take(3)
    qkv_last, up_last, down_last, (qkv_new, out_new) = take(n), take(n), take(n), take(2)
    qkv_o, out_o, up_o, down_o = take(3), take(3), take(3), take(3)
    qkv_b, out_b, up_b, down_b = take(3), take(3), take(3), take(3)
    qkv_g, up_g, down_g, (qkv_n, out_n) = take(n), take(n), take(n), take(2)
    moves = Moves(refs.pop(0))
    f = lax.axis_index("fsdp")
    mid, half = bit_of(f, 2), bit_of(f, 4)
    feat, sub = up[0].shape[0], down[0].shape[0]
    rate, rate_out = rates
    pair = (half * 2 + mid, mid)
    loads = {}
    loads["qkv"] = moves.load(
        [*zip(qkv, qkv_b), *zip(last_blocks(qkv_last, *pair, feat), qkv_g), (qkv_new, qkv_n)]
    )
    loads["down"] = moves.load([*zip(down, down_b), *zip(last_blocks(down_last, half, 0, sub), down_g)])
    loads["up"] = moves.load(
        [
            move
            for src, dst in zip(up, up_b)
            for move in zip(columns_of(src, mid, chunk), side_by_side(dst, chunk))
        ]
        + [*zip(last_blocks(up_last, *pair, feat), up_g)]
    )
    loads["out"] = moves.load([*zip(out, out_b), (out_new, out_n)])

    def arrive(name):
        for c in loads[name]:
            c.wait()

    arrive("qkv")
    for c in range(3):
        for q, grads in ((mid, qkv_g), (1 - mid, [qkv_n])):

            def at(i, c=c, q=q):
                rows = here(i, ROWS)
                return (c, rows, pl.ds(pl.multiple_of(q * HD, HD), HD)), (rows, slice(c * HD, (c + 1) * HD))

            adam_loop(qkv_b, grads, rate, feat // ROWS, at)
    moves.store(zip((qkv_b[1], qkv_b[2], qkv_b[0]), qkv_o))
    arrive("down")
    adam_loop(down_b, down_g, rate, sub // ROWS, by_chunks)
    moves.store(zip((down_b[1], down_b[2], down_b[0]), down_o))
    arrive("up")
    adam_loop(up_b, up_g, rate, feat // ROWS, by_chunks)
    moves.store(
        [
            move
            for src, dst in zip((up_b[1], up_b[2], up_b[0]), up_o)
            for move in zip(side_by_side(src, chunk), columns_of(dst, mid, chunk))
        ]
    )
    arrive("out")
    rows = min(out[0].shape[0], ROWS)
    adam_loop(out_b, [out_n], rate_out, out[0].shape[0] // rows, lambda i: (here(i, rows), here(i, rows)))
    moves.store(zip((out_b[1], out_b[2], out_b[0]), out_o))
    moves.drain()


def finish_kernel(chunk, rate, x, e, vec, *refs):
    take = lambda k: [refs.pop(0) for _ in range(k)]
    refs = list(refs)
    norm, branch, up, (up_new,), _ = take(3), take(3), take(3), take(1), take(3)
    tokens_o, up_o = take(2), take(3)
    x_b, e_b = take(2)
    parts_b, up_b, (up_g,), out_b = take(6), take(3), take(1), take(2)
    moves = Moves(refs.pop(0))
    f = lax.axis_index("fsdp")
    t = lax.axis_index("tp")
    mid = bit_of(f, 2)
    rows, feat = x.shape[0], up[0].shape[0]
    up_loads = moves.load(
        [
            move
            for src, dst in zip(up, up_b)
            for move in zip(columns_of(src, 1 - mid, chunk), side_by_side(dst, chunk))
        ]
        + [(up_new, up_g)]
    )
    where = lambda part: [block(part[0], mid * 2 + t // 2, rows), block(part[1], mid, rows), part[2]]
    quarter = rows // 4
    piece = lambda ref, i: ref.at[pl.ds(i * quarter, quarter)]
    sources, held = [x, e, *where(norm), *where(branch)], [x_b, e_b, *parts_b]
    token_loads = [moves.load([(piece(s, i), piece(b, i)) for s, b in zip(sources, held)]) for i in range(4)]
    for c in up_loads:
        c.wait()
    adam_loop(up_b, [up_g], rate, feat // ROWS, by_chunks)
    moves.store(
        [
            move
            for src, dst in zip((up_b[1], up_b[2], up_b[0]), up_o)
            for move in zip(side_by_side(src, chunk), columns_of(dst, 1 - mid, chunk))
        ]
    )
    bias = vec[4:5, :] + vec[5:6, :]
    add = lambda part, at: sum(ref[at, :].astype(f32) for ref in part)
    for j in range(4):
        for c in token_loads[j]:
            c.wait()

        @pl.loop(0, quarter // ROWS)
        def _(i, j=j):
            at = here(j * (quarter // ROWS) + i, ROWS)
            stream = x_b[at, :].astype(f32)
            out_b[0][at, :] = stream + add(parts_b[3:], at) + bias
            scaled = add(parts_b[:3], at)
            normal, inverse = normalise(stream, True)
            out_b[1][at, :] = e_b[at, :].astype(f32) + inverse * (
                scaled
                - jnp.mean(scaled, axis=-1, keepdims=True)
                - normal * jnp.mean(scaled * normal, axis=-1, keepdims=True)
            )

        moves.store([(piece(b, j), piece(o, j)) for b, o in zip(out_b, tokens_o)])
    moves.drain()


def run_update(chunk, rates, qkv, out_new, up_last, down_last, weights):
    n = len(up_last)
    flat = [w for group in weights for w in group]
    grads = [*qkv[0], *up_last, *down_last, qkv[1], out_new]
    feat, sub = weights[2][0].shape[0], weights[3][0].shape[0]
    wide, mine, d = qkv[1].shape[1], up_last[0].shape[1], weights[3][0].shape[1]
    half_up = (feat, mine)
    held = [w.shape for w in flat[:6]] + [half_up] * 3 + [w.shape for w in flat[9:]]
    held_grads = [(feat, wide)] * n + [half_up] * n + [(sub, d)] * n + [(feat, wide), out_new.shape]
    pieces = weights[2][0].shape[1] // (2 * chunk)
    n_bytes = 8 * sum(w.size for w in flat)
    return pl.pallas_call(
        functools.partial(update_kernel, chunk, rates, n),
        out_shape=[jax.ShapeDtypeStruct(w.shape, f32) for w in flat],
        in_specs=[ANY] * (len(flat) + len(grads)),
        out_specs=[ANY] * len(flat),
        scratch_shapes=[pltpu.VMEM(shape, f32) for shape in held]
        + [pltpu.VMEM(shape, bf16) for shape in held_grads]
        + [pltpu.SemaphoreType.DMA((2 * 9 + 2 * 3 * pieces + 3 * n + 2,))],
        compiler_params=pltpu.CompilerParams(vmem_limit_bytes=56 * 2**20),
        cost_estimate=pl.CostEstimate(flops=0, bytes_accessed=n_bytes, transcendentals=0),
        name="update",
    )(*flat, *grads)


def run_finish(chunk, rate, x, e, vec, tokens, up, up_new, up_done):
    rows, d = x.shape
    half_up = up_new.shape
    token = jax.ShapeDtypeStruct(x.shape, f32)
    pieces = up[0].shape[1] // (2 * chunk)
    return pl.pallas_call(
        functools.partial(finish_kernel, chunk, rate),
        out_shape=[token, token] + [jax.ShapeDtypeStruct(w.shape, f32) for w in up],
        in_specs=[ANY, ANY, VMEM] + [ANY] * 13,
        out_specs=[ANY] * 5,
        input_output_aliases={13: 2, 14: 3, 15: 4},
        scratch_shapes=[pltpu.VMEM((rows, d), bf16)] * 8
        + [pltpu.VMEM(half_up, f32)] * 3
        + [pltpu.VMEM(half_up, bf16)]
        + [pltpu.VMEM((rows, d), f32)] * 2
        + [pltpu.SemaphoreType.DMA((2 * 3 * pieces + 1 + 4 * (8 + 2),))],
        compiler_params=pltpu.CompilerParams(vmem_limit_bytes=56 * 2**20),
        name="finish",
    )(x, e, vec, *tokens[0], *tokens[1], *up, up_new, *up_done)


def make_local(fsdp, tp):
    masks = [1 << b for b in range(2, fsdp.bit_length() - 1)] + [1]
    top = fsdp // 2

    def local(
        layer_input,
        out_cotangent,
        segments,
        qkv_weight,
        qkv_first,
        qkv_second,
        out_weight,
        out_first,
        out_second,
        up_weight,
        up_first,
        up_second,
        down_weight,
        down_first,
        down_second,
        small_params,
        small_first,
        small_second,
    ):
        d = layer_input.shape[1]
        length = segments.shape[1]
        chunk = 2 * down_weight.shape[1]
        lanes = np.arange(128)
        rate = 10000.0 ** (-(2.0 * (lanes % (ROT // 2))) / ROT)
        angle = np.arange(length)[:, None] * rate[None]
        rates = np.broadcast_to(rate, angle.shape)
        table = jnp.asarray(np.concatenate([np.cos(angle), np.sin(angle), rates], 1), f32)
        vec = small_params.reshape(-1, d)
        token_parts, qkv_parts, out_new, up_parts, down_last, small = run_layer(
            masks, top, length, tp, layer_input, out_cotangent, up_weight[0], qkv_weight[0], down_weight[0],
            out_weight[0], segments, table, vec,
        )
        weights = (
            (qkv_weight[0], qkv_first[0], qkv_second[0]),
            (out_weight[0], out_first[0], out_second[0]),
            (up_weight[0], up_first[0], up_second[0]),
            (down_weight[0], down_first[0], down_second[0]),
        )
        rates = (d ** (-0.5), 4.0 * d ** (-0.5))
        up_last, up_give = up_parts
        up_new = lax.ppermute(up_give, "fsdp", [(i, i ^ 2) for i in range(fsdp)])
        updated = run_update(chunk, rates, qkv_parts, out_new, up_last, down_last, weights)
        finished = run_finish(
            chunk, rates[0], layer_input, out_cotangent, vec, token_parts, weights[2], up_new, updated[6:9]
        )
        results = [*finished[:2], *updated[:6], *finished[2:], *updated[9:]]
        small_total = jnp.concatenate([small[0:5], small[4:5], small[5:12]]).reshape(1, -1)
        small_updated = adam_step(small_params, small_first, small_second, small_total, rate_vector, 0.0)
        return (*results[:2], *[w[None] for w in results[2:]], *small_updated)

    return local


def solution(mesh):
    tokens = P(("fsdp", "tp"), None)
    inner = P(None, ("tp", "fsdp"), None)
    qkv = P(None, None, "fsdp", "tp")
    up = P(None, "fsdp", "tp")
    weights = (qkv,) * 3 + (inner,) * 3 + (up,) * 3 + (inner,) * 3 + (P(),) * 3
    return jax.shard_map(
        make_local(mesh.shape["fsdp"], mesh.shape["tp"]),
        mesh=mesh,
        in_specs=(tokens, tokens, P("fsdp", None)) + weights,
        out_specs=(tokens, tokens) + weights,
        check_vma=False,
    )
```
